128 devices in a mesh: fsdp: 8 (over x_lo, z), ctx: 16 (over x_hi, y, core).
Axes of the slice: x: 4 (x_hi: 2, x_lo: 2; x = x_hi * 2 + x_lo), y: 4, z: 4, core: 2. Of those that a mesh axis runs over, the one named last changes fastest.
Arguments:
- tokens: bfloat16 [8, 2048, 1024], P('fsdp', 'ctx'), may hold values from -6 to 6
- positions: int32 [8, 2048], P('fsdp'), may hold values from 0 to 2047, as said below
- w_qkv: bfloat16 [1024, 4096], P('fsdp'), may hold values from -0.1875 to 0.1875
- w_out: bfloat16 [2048, 1024], P('fsdp'), may hold values from -1 to 1
- w_gate: bfloat16 [1024, 3072], P('fsdp'), may hold values from -0.1875 to 0.1875
- w_up: bfloat16 [1024, 3072], P('fsdp'), may hold values from -0.1875 to 0.1875
- w_down: bfloat16 [3072, 1024], P('fsdp'), may hold values from -0.21875 to 0.21875
- attn_gain: bfloat16 [1024], P('fsdp'), may hold values from 0.5 to 1.5
- ffn_gain: bfloat16 [1024], P('fsdp'), may hold values from 0.5 to 1.5
- q_gain: bfloat16 [128], P('fsdp'), may hold values from 1 to 2
- k_gain: bfloat16 [128], P('fsdp'), may hold values from 1 to 2
- cotangent: bfloat16 [8, 2048, 1024], P('fsdp', 'ctx'), may hold values from -6 to 6
Outputs:
- output: bfloat16 [8, 2048, 1024], P('fsdp', 'ctx')
- tokens_grad: float32 [8, 2048, 1024], P('fsdp', 'ctx')
- w_qkv_grad: float32 [1024, 4096], P('fsdp')
- w_out_grad: float32 [2048, 1024], P('fsdp')
- w_gate_grad: float32 [1024, 3072], P('fsdp')
- w_up_grad: float32 [1024, 3072], P('fsdp')
- w_down_grad: float32 [3072, 1024], P('fsdp')
- attn_gain_grad: float32 [1024], P('fsdp')
- ffn_gain_grad: float32 [1024], P('fsdp')
- q_gain_grad: float32 [128], P('fsdp')
- key_gain_gradient: float32 [128], P('fsdp')
The draws below stay inside these ranges and needn't reach their ends.
Inputs may be any that keep to these rules, and one draw needn't show every extreme that they name: In each sequence the positions are a permutation of 0 to 2047 made of whole runs of 128 consecutive positions, each run starting at a multiple of 128 of the stored order; the order of the runs differs from sequence to sequence.
All inputs are finite; a program needn't handle non-finite values.
Results may differ from the reference program's by a relative error of at most 0.03.
Values may be sent and summed in bfloat16 or wider, within the bound.
No kernel may reach another device: no remote copies, remote signals or barrier semaphores. Data moves between devices by JAX's collectives and lax.ppermute only.
A program may use at most 192 MiB of HBM per device.

```python
import math
import jax
import jax.numpy as jnp
from jax import lax

D = 1024
QUERY_HEADS = 16
KEY_VALUE_HEADS = 8
HEAD_SIZE = 128
FF = 3072
BLOCK = 128
QUERY_FEATURES = 2048
KEY_FEATURES = 1024
LENGTH = 2048
SEQS = 8


def draw_positions(key, part):
    key = jax.random.fold_in(key, 11)
    seq_keys = jax.random.split(key, SEQS)
    orders = jax.vmap(lambda seq_key: jax.random.permutation(seq_key, LENGTH // BLOCK))(seq_keys)
    offsets = jnp.arange(BLOCK, dtype=jnp.int32)
    starts = orders.astype(jnp.int32)[:, :, None] * BLOCK
    return (starts + offsets[None, None, :]).reshape(SEQS, LENGTH).astype(jnp.int32)


def block_levels(rng, dims, cuts, smallest, top_value):
    level, own = 1.0, jax.random.fold_in(rng, 6)
    for axis_at, shards_of in cuts:
        heights = jnp.exp(jax.random.uniform(jax.random.fold_in(own, axis_at), (shards_of,), jnp.float32, smallest / len(cuts), top_value / len(cuts)))
        level = level * jnp.repeat(heights, dims[axis_at] // shards_of).reshape([-1 if axis == axis_at else 1 for axis in range(len(dims))])
    return level


def normal_values(key, shape, spread, bound, pieces=(), kind=jnp.bfloat16):
    level = block_levels(key, shape, pieces, -0.22, 0.18) if pieces else 1.0
    values = jax.random.normal(key, shape, jnp.float32) * spread * level
    return jnp.minimum(jnp.maximum(values, -bound), bound).astype(kind)


def setup_inputs(seed: int = 0) -> dict:
    key_list = jax.random.split(jax.random.key(seed), 13)
    return {
        "tokens": normal_values(key_list[0], (SEQS, LENGTH, D), 1.0, 6.0, ((0, 8), (1, 16))),
        "positions": draw_positions(jax.random.fold_in(key_list[12], 71), 0),
        "w_qkv": normal_values(key_list[2], (D, QUERY_FEATURES + 2 * KEY_FEATURES), D ** -0.5, 0.1875, ((0, 8),)),
        "w_out": normal_values(key_list[3], (QUERY_FEATURES, D), (QUERY_FEATURES // 64) ** -0.5, 1.0, ((0, 8),)),
        "w_gate": normal_values(key_list[4], (D, FF), D ** -0.5, 0.1875, ((0, 8),)),
        "w_up": normal_values(key_list[5], (D, FF), D ** -0.5, 0.1875, ((0, 8),)),
        "w_down": normal_values(key_list[6], (FF, D), (FF // 4) ** -0.5, 0.21875, ((0, 8),)),
        "attn_gain": jnp.clip(1.0 + 0.1 * jax.random.normal(key_list[7], (D,), jnp.float32), 0.5, 1.5).astype(jnp.bfloat16),
        "ffn_gain": jnp.clip(1.0 + 0.1 * jax.random.normal(key_list[8], (D,), jnp.float32), 0.5, 1.5).astype(jnp.bfloat16),
        "q_gain": jnp.clip(jnp.exp(math.log(2.0) - 0.6931472 * jax.random.uniform(key_list[9], (HEAD_SIZE,), jnp.float32) ** block_levels(key_list[9], (HEAD_SIZE,), ((0, 8),), -0.2, 0.2)), 1.0, 2.0).astype(jnp.bfloat16),
        "k_gain": jnp.clip(jnp.exp(math.log(2.0) - 0.6931472 * jax.random.uniform(key_list[10], (HEAD_SIZE,), jnp.float32) ** block_levels(key_list[10], (HEAD_SIZE,), ((0, 8),), -0.2, 0.2)), 1.0, 2.0).astype(jnp.bfloat16),
        "cotangent": normal_values(key_list[11], (SEQS, LENGTH, D), 1.0, 6.0, ((0, 8), (1, 16))),
    }


EPS = 1e-06
THETA = 1000000.0
MASKED_SCORE = -1e+30

@jax.custom_vjp
def lowered_input(v):
    return lax.optimization_barrier(v.astype(jnp.bfloat16)).astype(jnp.float32)

@jax.custom_vjp
def low_back(v):
    return v

def low_keep(v):
    return (lowered_input(v), None)

def low_pass(kept, grad):
    return (grad,)

def back_keep(v):
    return (v, None)

def back_low(kept, grad):
    return (lowered_input(grad),)
lowered_input.defvjp(low_keep, low_pass)
low_back.defvjp(back_keep, back_low)

def matmul(left, right):
    return jnp.dot(left, right, precision=lax.Precision.HIGHEST, preferred_element_type=jnp.float32)

def rms_scale(value_matrix, gain):
    return value_matrix * lax.rsqrt(lax.optimization_barrier(jnp.mean(value_matrix * value_matrix, axis=-1, keepdims=True)) + EPS) * gain

def rotary(value_matrix, angles):
    half = value_matrix.shape[-1] // 2
    cosine = jnp.cos(angles)[:, None, :]
    sine = jnp.sin(angles)[:, None, :]
    first = value_matrix[..., :half]
    second = value_matrix[..., half:]
    return jnp.concatenate([first * cosine - second * sine, second * cosine + first * sine], axis=-1)

def attention(query_matrix, keys, value_rows, pos_rows):
    sequence_length = query_matrix.shape[0]
    query_extent = min(512, sequence_length)
    query_group = QUERY_HEADS // KEY_VALUE_HEADS
    score_scale = HEAD_SIZE ** (-0.5)
    query_block_count = query_matrix.reshape(sequence_length // query_extent, query_extent, KEY_VALUE_HEADS, query_group, HEAD_SIZE)
    pos_blocks = pos_rows.reshape(sequence_length // query_extent, query_extent)

    def one_block(items):
        query_part, query_positions = items
        scores = jnp.einsum('qhgd,khd->hgqk', query_part, keys, precision=lax.Precision.HIGHEST) * score_scale
        scores = low_back(scores)
        allowed = pos_rows[None, :] <= query_positions[:, None]
        scores = jnp.where(allowed[None, None], scores, MASKED_SCORE)
        row_peak = lax.optimization_barrier(jnp.max(scores, axis=-1, keepdims=True))
        expo = jnp.exp(scores - row_peak)
        totals = lax.optimization_barrier(jnp.sum(expo, axis=-1, keepdims=True))
        summed = jnp.einsum('hgqk,khd->qhgd', lowered_input(expo), value_rows, precision=lax.Precision.HIGHEST)
        summed = low_back(summed)
        return (summed / jnp.transpose(totals, (2, 0, 1, 3))).reshape(query_extent, QUERY_HEADS * HEAD_SIZE)
    result = lax.map(jax.checkpoint(one_block), (query_block_count, pos_blocks))
    return result.reshape(sequence_length, QUERY_HEADS * HEAD_SIZE)

def sequence_layer(inputs, pos_rows, w_qkv, w_out, w_gate, w_up, w_down, attn_gain, ffn_gain, q_gain, k_gain):
    sequence_length = inputs.shape[0]
    query_width = QUERY_HEADS * HEAD_SIZE
    key_value_width = KEY_VALUE_HEADS * HEAD_SIZE
    normed = lowered_input(rms_scale(inputs, attn_gain))
    projected_rows = low_back(matmul(normed, w_qkv))
    query_raw = projected_rows[:, :query_width].reshape(sequence_length, QUERY_HEADS, HEAD_SIZE)
    key_unnormed = projected_rows[:, query_width:query_width + key_value_width].reshape(sequence_length, KEY_VALUE_HEADS, HEAD_SIZE)
    value_rows = lowered_input(projected_rows[:, query_width + key_value_width:].reshape(sequence_length, KEY_VALUE_HEADS, HEAD_SIZE))
    inverse = THETA ** (-(jnp.arange(HEAD_SIZE // 2, dtype=jnp.float32) * 2.0 / HEAD_SIZE))
    angles = pos_rows.astype(jnp.float32)[:, None] * inverse[None, :]
    query_matrix = lowered_input(rotary(rms_scale(query_raw, q_gain), angles))
    keys = lowered_input(rotary(rms_scale(key_unnormed, k_gain), angles))
    attended = lowered_input(attention(query_matrix, keys, value_rows, pos_rows))
    middle = inputs + low_back(matmul(attended, w_out))
    ffn_rows = lowered_input(rms_scale(middle, ffn_gain))
    gate_pre = low_back(matmul(ffn_rows, w_gate))
    up_pre = low_back(matmul(ffn_rows, w_up))
    activated = lowered_input(jax.nn.silu(gate_pre) * up_pre)
    return middle + low_back(matmul(activated, w_down))

def reference(tokens, positions, w_qkv, w_out, w_gate, w_up, w_down, attn_gain, ffn_gain, q_gain, k_gain, cotangent):
    inputs = tokens.astype(jnp.float32)
    weights = (w_qkv.astype(jnp.float32), w_out.astype(jnp.float32), w_gate.astype(jnp.float32), w_up.astype(jnp.float32), w_down.astype(jnp.float32), attn_gain.astype(jnp.float32), ffn_gain.astype(jnp.float32), q_gain.astype(jnp.float32), k_gain.astype(jnp.float32))

    def forward(all_inputs, *params):

        def one_sequence(carry, items):
            seq_inputs, seq_pos = items
            return (carry, jax.checkpoint(sequence_layer)(seq_inputs, seq_pos, *params))
        _, results = lax.scan(one_sequence, jnp.zeros((), jnp.float32), (all_inputs, positions))
        return results
    results, pullback = jax.vjp(forward, inputs, *weights)
    grads = pullback(cotangent.astype(jnp.float32))
    return (results.astype(jnp.bfloat16), grads[0], grads[1], grads[2], grads[3], grads[4], grads[5], grads[6], grads[7], grads[8], grads[9])
```

```python
import jax
import jax.numpy as jnp
from jax import lax
from jax.experimental import pallas as pl
from jax.experimental.pallas import tpu as pltpu
from jax.sharding import Mesh
from jax.sharding import PartitionSpec as P

HEAD = 128
EPS = 1e-06
THETA = 1000000.0
SCALE = HEAD**-0.5
LOG2E = 1.4426950408889634
RUN = 128
CHUNK = 256
FSDP = ("xlo", "z")
CTX = ("xhi", "y", "core")
TP = ("y", "core")
SIZES = {"xlo": 2, "z": 4, "xhi": 2, "y": 4, "core": 2}
BF = jnp.bfloat16
F32 = jnp.float32
SLOT, SEEN, FOF, TOF, CORE = 0, 16, 32, 40, 48


def shift(x, axis, step):
    n = SIZES[axis]
    return lax.ppermute(x, axis, [(i, (i + step) % n) for i in range(n)])


def gather_tokens(x):
    own = jnp.concatenate([x] + [shift(x, "y", k) for k in (1, 2, 3)], axis=0)
    return own, shift(own, "core", 1)


def scatter_tokens(own, other):
    blocks = (own.astype(F32) + shift(other, "core", 1).astype(F32)).astype(BF).reshape(4, RUN, -1)
    return [blocks[0]] + [shift(blocks[k], "y", 4 - k) for k in (1, 2, 3)]


def exchange(own, other):
    both = jnp.stack([own, shift(other, "core", 1)], axis=1)
    return [both[0]] + [shift(both[k], "y", 4 - k) for k in (1, 2, 3)]


def spread_z(pair):
    return [pair] + [shift(pair, "z", k) for k in (1, 2, 3)]


def after(x, *others):
    return lax.optimization_barrier((x,) + others)[0]


def dot(a, b):
    return jnp.dot(a, b, preferred_element_type=F32)


def dot_nt(a, b):
    return lax.dot_general(a, b, (((1,), (1,)), ((), ())), preferred_element_type=F32)


def dot_tn(a, b):
    return lax.dot_general(a, b, (((0,), (0,)), ((), ())), preferred_element_type=F32)


def inv_rms(x):
    return lax.rsqrt(jnp.mean(x * x, axis=-1, keepdims=True) + EPS)


def norm_pull(x, gain, grad):
    inv = inv_rms(x)
    hat = x * inv
    scaled = grad * gain
    return inv * (scaled - hat * jnp.mean(scaled * hat, axis=-1, keepdims=True)), grad * hat


def ds(at, size):
    return pl.ds(pl.multiple_of(at, size), size)


def rows_of(i, size):
    return slice(i * size, (i + 1) * size)


def key_value_kernel(info, own, sib, w0, w1, w2, w3, cos, sin, h_ref, w_ref, gain_ref, raw_ref, kv_ref):
    gain_ref[...] = jnp.zeros_like(gain_ref)
    for k, part in enumerate((w0, w1, w2, w3)):
        for j in range(2):
            f = info[FOF + 4 * j + k]
            w_ref[ds(f * RUN, RUN), :] = part[j, :RUN, :]
            row = part[j, RUN:, :].astype(F32)[:8]
            gain_ref[:, ds(f * RUN, RUN)] = row[:, :128]
            gain_ref[:, ds(1024 + f * RUN, RUN)] = row[:, 128:256]
            gain_ref[:, 2048:2176] += pltpu.roll(row[:, 256:384], f * 16, 1)
            gain_ref[:, 2176:2304] += pltpu.roll(row[:, 384:512], f * 16, 1)
    attn_gain, k_gain = gain_ref[0:1, :1024], gain_ref[0:1, 2176:2304]
    for i in range(4):
        part = (own, sib)[i // 2]
        here = rows_of(i, 256)
        x = part[rows_of(i % 2, 256), :].astype(F32)
        h = (x * inv_rms(x) * attn_gain).astype(BF)
        h_ref[here, :] = h
        raw = dot(h, w_ref[:, 256:])
        raw_ref[here, :] = raw[:, :HEAD]
        key = raw[:, :HEAD]
        key = key * inv_rms(key) * k_gain
        key = key * cos[here, :] + pltpu.roll(key, HEAD // 2, 1) * sin[here, :]
        kv_ref[here, :HEAD] = key.astype(BF)
        kv_ref[here, HEAD:] = raw[:, HEAD:].astype(BF)


def query_kernel(h_ref, w_ref, gain_ref, cos, sin, raw_ref, q_ref):
    gain = gain_ref[0:1, 2048:2176]
    for i in range(4):
        here = rows_of(i, 256)
        raw = dot(h_ref[here, :], w_ref[:, :256])
        raw_ref[here, :] = raw
        for a in range(2):
            u = raw[:, rows_of(a, HEAD)]
            u = u * inv_rms(u) * gain
            u = u * cos[here, :] + pltpu.roll(u, HEAD // 2, 1) * sin[here, :]
            q_ref[here, rows_of(a, HEAD)] = u.astype(BF)


def stacked(rows):
    return jnp.concatenate([rows[:, :HEAD], rows[:, HEAD:]], axis=0)


def sort_runs(info, base, pos_ref, kv, ks, kp):
    for b in range(8):
        at = ds(info[SLOT + base + b] * RUN, RUN)
        ks[at, :] = kv[rows_of(b, RUN), :HEAD]
        kp[at, :] = jnp.broadcast_to(pos_ref[base + b], (RUN, RUN)).T


def keep_seen(p, at, i, pos_ref, kp):
    row = jnp.concatenate([pos_ref[i], pos_ref[i]], axis=1)
    return jnp.where(kp[at, :1] <= row, p, 0.0)


def loop_seen(info, base, i, step):
    seen = info[SEEN + base + i]
    full = seen // (CHUNK // RUN)
    pl.loop(0, full)(lambda c: step(c, False))
    pl.when(seen % (CHUNK // RUN) > 0)(lambda: step(full, True))


def forward_kernel(base, info, pos_ref, q_ref, kv, *refs):
    before, (o_ref, *rest, ks, vt, kp, acc) = (refs[:1], refs[1:]) if base else ((), refs)
    sort_runs(info, base, pos_ref, kv, ks, kp)
    for b in range(8):
        vt[:HEAD, ds(info[SLOT + base + b] * RUN, RUN)] = kv[rows_of(b, RUN), HEAD:].T
    vt[HEAD:, :] = jnp.ones((HEAD, vt.shape[1]), BF)
    for i in range(8):
        q = stacked(q_ref[rows_of(i, RUN), :])
        if base:
            acc[: HEAD + 8, :] = before[0][i]
        else:
            acc[...] = jnp.zeros_like(acc)

        def step(c, masked):
            at = ds(c * CHUNK, CHUNK)
            e = jnp.exp2(dot_nt(ks[at, :], q) * (SCALE * LOG2E))
            if masked or not base:
                e = keep_seen(e, at, i, pos_ref, kp)
            acc[...] += dot(vt[:, at], e.astype(BF))

        loop_seen(info, base, i, step)
        if not base:
            o_ref[i] = acc[: HEAD + 8, :]
            continue
        lse_ref, low_ref = rest
        total = acc[HEAD : HEAD + 1, :]
        out = (acc[:HEAD, :] / total).T
        out = jnp.concatenate([out[:RUN], out[RUN:]], axis=1)
        o_ref[rows_of(i, RUN), :] = out
        low_ref[i // 4, i % 4] = out.astype(BF)
        lse_ref[i] = jnp.log2(total)


def out_kernel(info, x_ref, o0, o1, o2, o3, w_ref, gain_ref, x2_ref, h2_ref, oall_ref):
    for k, part in enumerate((o0, o1, o2, o3)):
        for j in range(2):
            oall_ref[:, ds(info[TOF + 4 * j + (4 - k) % 4] * 256, 256)] = part[j]
    x2 = x_ref[...].astype(F32) + dot(oall_ref[...], w_ref[...])
    x2_ref[...] = x2
    h2_ref[...] = (x2 * inv_rms(x2) * gain_ref[0:1, 1024:2048]).astype(BF)


def ffn_kernel(h2_ref, dy_ref, wgu, wd, act_ref, dgu_ref, part_ref):
    for i in range(2):
        here = rows_of(i, 256)
        gu = dot(h2_ref[here, :], wgu[...])
        gate, up = gu[:, :384], gu[:, 384:]
        sg = 1.0 / (1.0 + jnp.exp(-gate))
        silu = gate * sg
        act_ref[here, :] = (silu * up).astype(BF)
        d_act = dot_nt(dy_ref[here, :], wd[...])
        d_gate = (d_act * up * (sg * (1.0 + gate * (1.0 - sg)))).astype(BF)
        d_gu = jnp.concatenate([d_gate, (d_act * silu).astype(BF)], axis=1)
        dgu_ref[here, :] = d_gu
        part_ref[here, :] = dot_nt(d_gu, wgu[...]).astype(BF)


def ffn_grad_kernel(h2_own, h2_sib, dy_own, dy_sib, act_own, act_sib, dgu_own, dgu_sib, wd, g_ref, y_own, y_sib):
    y_own[...] = dot(act_own[...], wd[...]).astype(BF)
    y_sib[...] = dot(act_sib[...], wd[...]).astype(BF)
    for a in range(4):
        cols = rows_of(a, 256)
        g = (dot_tn(h2_own[:, cols], dgu_own[...]) + dot_tn(h2_sib[:, cols], dgu_sib[...])).astype(BF)
        g_ref[2 * a, :RUN, :] = g[:RUN]
        g_ref[2 * a + 1, :RUN, :] = g[RUN:]
    g = (dot_tn(act_own[...], dy_own[...]) + dot_tn(act_sib[...], dy_sib[...])).astype(BF)
    for f in range(8):
        rows = g[f * 48 : (f + 1) * 48]
        g_ref[f, 128:176, :] = rows[:, :768]
        for n in range(3):
            g_ref[f, 176:192, rows_of(n, 256)] = rows[16 * n : 16 * n + 16, 768:]


def middle_kernel(info, p0, p1, p2, p3, x2_ref, dy_ref, gain_ref, w_ref, dx2_ref, low_ref, gsum_ref, do_own, do_other, do):
    grad = sum(p[...].astype(F32) for p in (p0, p1, p2, p3))
    pulled, by_gain = norm_pull(x2_ref[...], gain_ref[0:1, 1024:2048], grad)
    gsum_ref[...] = jnp.sum(by_gain, axis=0, keepdims=True)
    dx2 = dy_ref[...].astype(F32) + pulled
    dx2_ref[...] = dx2
    low = dx2.astype(BF)
    low_ref[...] = low
    do[...] = dot_nt(low, w_ref[...]).astype(BF)
    for k in range(4):
        do_own[k] = do[:, ds(info[TOF + k] * 256, 256)]
        do_other[k] = do[:, ds(info[TOF + 4 + k] * 256, 256)]


def out_grad_kernel(info, o_ref, d_ref, own_ref, other_ref, g_all):
    for a in range(8):
        rows = rows_of(a, 256)
        g_all[...] = dot_tn(o_ref[:, rows], d_ref[...]).astype(BF)
        for k in range(4):
            own_ref[k, rows, :] = g_all[:, ds(info[TOF + k] * RUN, RUN)]
            other_ref[k, rows, :] = g_all[:, ds(info[TOF + 4 + k] * RUN, RUN)]


def backward_kernel(base, info, pos_ref, q_ref, kv, o_ref, lse_ref, d0, d1, d2, d3, *refs):
    before, (dq_ref, dkv_ref, ks, vs, kp, dk, dv, dq) = ((), refs) if base else (refs[:1], refs[1:])
    sort_runs(info, base, pos_ref, kv, ks, kp)
    for b in range(8):
        vs[ds(info[SLOT + base + b] * RUN, RUN), :] = kv[rows_of(b, RUN), HEAD:]
    dk[...] = jnp.zeros_like(dk)
    dv[...] = jnp.zeros_like(dv)
    for i in range(8):
        q = stacked(q_ref[rows_of(i, RUN), :])
        do = stacked((d0, d3, d2, d1)[i % 4][i // 4])
        delta = jnp.sum((do.astype(F32) * stacked(o_ref[rows_of(i, RUN), :])).T, axis=0, keepdims=True)
        lse = lse_ref[i]
        dq[...] = jnp.zeros_like(dq) if base else before[0][i]

        def step(c, masked):
            at = ds(c * CHUNK, CHUNK)
            keys = ks[at, :]
            p = jnp.exp2(dot_nt(keys, q) * (SCALE * LOG2E) - lse)
            if masked or not base:
                p = keep_seen(p, at, i, pos_ref, kp)
            d_s = (p * (dot_nt(vs[at, :], do) - delta)).astype(BF)
            dv[at, :] += dot(p.astype(BF), do)
            dk[at, :] += dot(d_s, q)
            dq[...] += dot_tn(d_s, keys)

        loop_seen(info, base, i, step)
        if base:
            dq_ref[i] = dq[...]
        else:
            dq_ref[rows_of(i, RUN), :HEAD] = dq[:RUN] * SCALE
            dq_ref[rows_of(i, RUN), HEAD:] = dq[RUN:] * SCALE
    for b in range(8):
        at = ds(info[SLOT + base + b] * RUN, RUN)
        dkv_ref[rows_of(b, RUN), :HEAD] = (dk[at, :] * SCALE).astype(dkv_ref.dtype)
        dkv_ref[rows_of(b, RUN), HEAD:] = dv[at, :].astype(dkv_ref.dtype)


def head_back(raw, gain, grad, cos, sin):
    grad = grad * cos + pltpu.roll(grad * sin, HEAD // 2, 1)
    pulled, by_gain = norm_pull(raw, gain, grad)
    return pulled.astype(BF), jnp.sum(by_gain, axis=0, keepdims=True)


def query_back_kernel(info, h_ref, gain_ref, cos, sin, raw, dq_ref, low_ref, g_ref, sum_ref):
    sum_ref[...] = jnp.zeros_like(sum_ref)
    for i in range(4):
        here = rows_of(i, 256)
        for a in range(2):
            cols = rows_of(a, HEAD)
            low, by_gain = head_back(raw[here, cols], gain_ref[0:1, 2048:2176], dq_ref[here, cols], cos[here, :], sin[here, :])
            low_ref[here, cols] = low
            sum_ref[...] += by_gain
    for k in range(4):
        for j in range(2):
            f = info[FOF + 4 * j + (4 - k) % 4]
            g_ref[k, j] = dot_tn(h_ref[:, ds(f * RUN, RUN)], low_ref[...])


def key_value_back_kernel(
    info, h_ref, w_ref, gain_ref, cos, sin, raw, dkv_ref, recv, gq_ref, qsum, ffn_ref, low_ref, g0, g1, g2, g3
):
    sums = jnp.zeros((1, HEAD), F32)
    for i in range(4):
        here = rows_of(i, 256)
        dkv = dkv_ref[here, :] + recv[here, :].astype(F32)
        low, by_gain = head_back(raw[here, :], gain_ref[0:1, 2176:2304], dkv[:, :HEAD], cos[here, :], sin[here, :])
        low_ref[here, :HEAD] = low
        low_ref[here, HEAD:] = dkv[:, HEAD:].astype(BF)
        sums += by_gain
    lane = lax.broadcasted_iota(jnp.int32, (8, HEAD), 1)
    heads = [jnp.broadcast_to(s, (8, HEAD)) for s in (qsum[...], sums)]
    for k, g_ref in enumerate((g0, g1, g2, g3)):
        for j in range(2):
            f = info[FOF + 4 * j + (4 - k) % 4]
            here = ds(f * RUN, RUN)
            gkv = dot_tn(h_ref[:, here], low_ref[...])
            gq = gq_ref[k, j]
            g_ref[j, :RUN, :256] = gq.astype(BF)
            g_ref[j, :RUN, 256:] = gkv.astype(BF)
            by_attn = jnp.sum(gq * w_ref[here, :256].astype(F32) + gkv * w_ref[here, 256:].astype(F32), axis=1, keepdims=True)
            by_attn = jnp.broadcast_to(by_attn, (RUN, RUN)).T[:8] / gain_ref[:, here]
            rows = [by_attn, jnp.broadcast_to(ffn_ref[0:1, here], (8, RUN))]
            rows += [jnp.where(lane < 16, pltpu.roll(r, HEAD - 16 * f, 1), 0.0) for r in heads]
            rows = jnp.concatenate(rows, axis=1)
            g_ref[j, RUN:, :] = jnp.concatenate([rows, rows], axis=0).astype(BF)


def normed_back_kernel(dq_ref, dkv_ref, w_ref, own_ref, sib_ref):
    for i in range(4):
        here = rows_of(i, 256)
        part = dot_nt(dq_ref[here, :], w_ref[:, :256]) + dot_nt(dkv_ref[here, :], w_ref[:, 256:])
        (own_ref, sib_ref)[i // 2][rows_of(i % 2, 256), :] = part.astype(BF)


def last_kernel(p0, p1, p2, p3, x_ref, dx2_ref, gain_ref, out_ref):
    grad = sum(p[...].astype(F32) for p in (p0, p1, p2, p3))
    out_ref[...] = dx2_ref[...] + norm_pull(x_ref[...].astype(F32), gain_ref[0:1, :1024], grad)[0]


def unpack_kernel(info, own, sib, g_ref, gain_ref):
    gain_ref[...] = jnp.zeros_like(gain_ref)
    for j, part in enumerate((own, sib)):
        for k in range(4):
            t = info[TOF + 4 * j + k]
            g_ref[:, ds(t * 256, 256)] = part[k, :RUN, :256].astype(F32)
            g_ref[:, ds(2048 + t * RUN, RUN)] = part[k, :RUN, 256:384].astype(F32)
            g_ref[:, ds(3072 + t * RUN, RUN)] = part[k, :RUN, 384:].astype(F32)
            gain_ref[...] += part[k, RUN:, :].astype(F32)[:8]


def assemble_kernel(info, o0, o1, o2, o3, sib, w_ref):
    core = info[CORE]
    for k, part in enumerate((o0, o1, o2, o3)):
        for j in range(2):
            f = info[FOF + 4 * j + k]
            w_ref[ds((2 * f + core) * HEAD, HEAD), :] = part[j]
            w_ref[ds((2 * f + 1 - core) * HEAD, HEAD), :] = sib[k, j]


def call(kernel, outs, scratch, micros, *args, info=None):
    smem = [] if info is None else [info]
    return pl.pallas_call(
        kernel,
        out_shape=[jax.ShapeDtypeStruct(*o) for o in outs],
        in_specs=[pl.BlockSpec(memory_space=pltpu.SMEM)] * len(smem)
        + [pl.BlockSpec(memory_space=pltpu.VMEM)] * len(args),
        out_specs=[pl.BlockSpec(memory_space=pltpu.VMEM)] * len(outs),
        scratch_shapes=[pltpu.VMEM(*s) for s in scratch],
        compiler_params=pltpu.CompilerParams(vmem_limit_bytes=48 * 2**20),
        cost_estimate=pl.CostEstimate(flops=int(micros * 1e9), bytes_accessed=2**20, transcendentals=0),
    )(*smem, *args)


def shards(
    tokens, positions, w_qkv, w_out, w_gate, w_up, w_down, attn_gain, ffn_gain, q_gain, k_gain, cotangent
):
    xhi, y, core = (lax.axis_index(a) for a in CTX)
    xlo, z = (lax.axis_index(a) for a in FSDP)
    t = y * 2 + core
    x_own, dy = tokens[0], cotangent[0]

    xs = gather_tokens(x_own)
    eight = jnp.arange(8, dtype=jnp.int32)
    block = lax.rem(y - eight % 4 + 4, 4) * 2 + (core ^ (eight // 4))
    f_of = (xlo ^ (eight // 4)) * 4 + lax.rem(z - eight % 4 + 4, 4)
    blocks = jnp.concatenate([xhi * 8 + block, (1 - xhi) * 8 + block])
    pos = positions[0].reshape(16, RUN)[blocks]
    rank = pos[:, 0] // RUN
    seen = rank[:, None, None] >= rank.reshape(1, 2, 8)
    seen = jnp.sum(seen, axis=2, dtype=jnp.int32)
    slot = jnp.concatenate([seen[:8, 0], seen[8:, 1]]) - 1
    info = jnp.concatenate([slot, seen[:8, 0], seen[:8, 1], f_of, block, core[None]]).astype(jnp.int32)
    pos_rows = pos.astype(F32).reshape(16, 1, RUN)
    inverse = THETA ** (-(jnp.arange(HEAD // 2, dtype=F32) * 2.0 / HEAD))
    angles = pos[:8].reshape(1024).astype(F32)[:, None] * inverse[None, :]
    cosine, sine = jnp.cos(angles), jnp.sin(angles)
    cosine = jnp.concatenate([cosine, cosine], axis=1)
    sine = jnp.concatenate([-sine, sine], axis=1)

    def columns(w, at, width):
        return lax.dynamic_slice_in_dim(w, at, width, 1)

    none = jnp.zeros((112,), BF)
    gains = jnp.concatenate([attn_gain, ffn_gain, q_gain, none, k_gain, none])
    slice_qkv = jnp.concatenate(
        [
            jnp.concatenate(
                [columns(w_qkv, t * 256, 256), columns(w_qkv, 2048 + t * 128, 128), columns(w_qkv, 3072 + t * 128, 128)],
                axis=1,
            ),
            jnp.broadcast_to(gains[None], (16, 512)),
        ],
        axis=0,
    )
    pair_qkv = jnp.stack([slice_qkv, shift(slice_qkv, "xlo", 1)])
    parts_qkv = spread_z(pair_qkv)
    slice_out = after(lax.dynamic_slice_in_dim(w_out, core * HEAD, HEAD, 0), pair_qkv)
    pair_out = jnp.stack([slice_out, shift(slice_out, "xlo", 1)])
    pair_out = after(pair_out, *parts_qkv)
    parts_out = spread_z(pair_out)
    sib_out = shift(jnp.stack(parts_out), "core", 1)
    (w_out_all,) = call(assemble_kernel, [((2048, 1024), BF)], [], 2, *parts_out, sib_out, info=info)

    def strided(w):
        return lax.dynamic_slice_in_dim(w.reshape(128, 8, 384), t * 48, 48, 2).reshape(128, 384)

    down = lax.dynamic_slice_in_dim(w_down, t * 48, 48, 0)
    slice_ffn = jnp.concatenate(
        [
            jnp.concatenate([strided(w_gate), strided(w_up)], axis=1),
            down[:, :768],
            jnp.concatenate([down[16 * n : 16 * n + 16, 768:] for n in range(3)], axis=1),
        ],
        axis=0,
    )
    wide = lax.all_gather(after(slice_ffn, *parts_qkv), FSDP, axis=0)
    wgu = wide[:, :128].reshape(1024, 768)
    tail = jnp.concatenate([wide[:, 176:, rows_of(n, 256)] for n in range(3)], axis=1)
    wd = jnp.concatenate([wide[:, 128:176], tail], axis=2).reshape(384, 1024)

    h, wqkv, gain, kraw, kv = call(
        key_value_kernel,
        [((1024, 1024), BF), ((1024, 512), BF), ((8, 2304), F32), ((1024, HEAD), F32), ((1024, 256), BF)],
        [],
        5,
        *xs, *parts_qkv, cosine, sine,
        info=info,
    )
    kv_other = shift(kv, "xhi", 1)
    dys = gather_tokens(after(dy, kv))
    qraw, q = call(query_kernel, [((1024, 256), F32), ((1024, 256), BF)], [], 3, h, wqkv, gain, cosine, sine)

    def attend(base, other, outs, micros, *more):
        return call(
            lambda *refs: forward_kernel(base, *refs),
            outs,
            [((1024, HEAD), BF), ((256, 1024), BF), ((1024, RUN), F32), ((256, 256), F32)],
            micros,
            pos_rows, q, other, *more,
            info=info,
        )

    (partial,) = attend(0, kv, [((8, HEAD + 8, 256), F32)], 7)
    kv_other = after(kv_other, partial, dys[0])
    o32, lse, o_low = attend(
        8, kv_other, [((1024, 256), F32), ((8, 1, 256), F32), ((2, 4, RUN, 256), BF)], 7, partial
    )
    x2, h2_own, o_all = call(
        out_kernel,
        [((RUN, 1024), F32), ((RUN, 1024), BF), ((RUN, 2048), BF)],
        [],
        4,
        x_own, *exchange(o_low[0], o_low[1]), w_out_all, gain,
        info=info,
    )

    h2 = gather_tokens(h2_own)
    ffn = [
        call(
            ffn_kernel,
            [((512, 384), BF), ((512, 768), BF), ((512, 1024), BF)],
            [],
            6,
            h2[j], dys[j], wgu, wd,
        )
        for j in (1, 0)
    ]
    (act_sib, dgu_sib, part_sib), (act_own, dgu_own, part_own) = ffn
    d_h2 = scatter_tokens(part_own, part_sib)
    d_x2, d_branch, ffn_sum, do_own, do_other = call(
        middle_kernel,
        [((RUN, 1024), F32), ((RUN, 1024), BF), ((1, 1024), F32), ((4, RUN, 256), BF), ((4, RUN, 256), BF)],
        [((RUN, 2048), BF)],
        5,
        *d_h2, x2, dy, gain, w_out_all,
        info=info,
    )
    d_o = exchange(do_own, do_other)
    g_ffn, y_own, y_sib = call(
        ffn_grad_kernel,
        [((8, 192, 768), BF), ((512, 1024), BF), ((512, 1024), BF)],
        [],
        8,
        *h2, *dys, act_own, act_sib, dgu_own, dgu_sib, wd,
    )
    g_out_own, g_out_other = call(
        out_grad_kernel, [((4, 2048, RUN), BF)] * 2, [((256, 1024), BF)], 4, o_all, d_branch, info=info
    )

    def add_halves(g):
        return (g.astype(F32) + shift(g, "xhi", 1).astype(F32)).astype(BF)

    rows_ffn = lax.psum_scatter(g_ffn, FSDP, scatter_dimension=0, tiled=False)
    blocks_out = (g_out_own.astype(F32) + shift(g_out_other, "core", 1).astype(F32)).astype(BF)
    y_blocks = (y_own.astype(F32) + shift(y_sib, "core", 1).astype(F32)).astype(BF).reshape(4, RUN, -1)
    q_later = after(q, *d_o, blocks_out, y_blocks)
    parts_out = [blocks_out[0]] + [shift(blocks_out[k], "y", 4 - k) for k in (1, 2, 3)]
    y_parts = [y_blocks[0]] + [shift(y_blocks[k], "y", 4 - k) for k in (1, 2, 3)]

    def attend_back(base, other, outs, *more):
        return call(
            lambda *refs: backward_kernel(base, *refs),
            outs,
            [((1024, HEAD), BF), ((1024, HEAD), BF), ((1024, RUN), F32), ((1024, HEAD), F32), ((1024, HEAD), F32), ((256, HEAD), F32)],
            8,
            pos_rows, q_later, other, o32, lse, *d_o, *more,
            info=info,
        )

    d_q, d_other = attend_back(8, kv_other, [((8, 256, HEAD), F32), ((1024, 256), BF)])
    recv = shift(d_other, "xhi", 1)
    d_q, d_kv = attend_back(0, kv, [((1024, 256), F32), ((1024, 256), F32)], d_q)
    dq_low, g_q, q_sum = call(
        query_back_kernel,
        [((1024, 256), BF), ((4, 2, RUN, 256), F32), ((1, HEAD), F32)],
        [],
        5,
        h, gain, cosine, sine, qraw, d_q,
        info=info,
    )
    output = (x2 + sum(p.astype(F32) for p in y_parts)).astype(BF)
    out_rows = sum(p.astype(F32) for p in parts_out).astype(BF).reshape(8, 256, RUN)
    recv = after(recv, output, out_rows)
    dkv_low, *g_qkv = call(
        key_value_back_kernel,
        [((1024, 256), BF)] + [((2, 144, 512), BF)] * 4,
        [],
        5,
        h, wqkv, gain, cosine, sine, kraw, d_kv, recv, g_q, q_sum, ffn_sum,
        info=info,
    )
    out_rows = lax.psum_scatter(after(out_rows, rows_ffn), FSDP, scatter_dimension=0, tiled=False)
    part_own, part_sib = call(
        normed_back_kernel, [((512, 1024), BF), ((512, 1024), BF)], [], 5, dq_low, dkv_low, wqkv
    )
    sum_ffn = lax.all_gather(add_halves(rows_ffn), TP, axis=0)
    sum_gate, sum_up = (
        jnp.transpose(sum_ffn[:, :128, part].astype(F32).reshape(8, 128, 8, 48), (1, 2, 0, 3)).reshape(128, 3072)
        for part in (slice(0, 384), slice(384, 768))
    )
    tail = jnp.concatenate([sum_ffn[:, 176:, rows_of(n, 256)] for n in range(3)], axis=1)
    sum_down = jnp.concatenate([sum_ffn[:, 128:176], tail], axis=2).reshape(384, 1024).astype(F32)
    sum_out = lax.all_gather(add_halves(out_rows), TP, axis=0)
    sum_out = jnp.transpose(sum_out, (1, 0, 2)).reshape(256, 1024).astype(F32)

    pair = g_qkv[0].astype(F32) + sum(shift(g_qkv[k], "z", k).astype(F32) for k in (1, 2, 3))
    pair = pair.astype(BF)
    d_h = scatter_tokens(part_own, part_sib)
    pair = after(pair, *d_h)
    cross = lax.ppermute(pair[1], ("xlo", "xhi"), [(i, i ^ 3) for i in range(4)])
    total = pair[0].astype(F32) + shift(pair[1], "xlo", 1).astype(F32)
    total = (total + shift(pair[0], "xhi", 1).astype(F32) + cross.astype(F32)).astype(BF)
    own = jnp.stack([total] + [shift(total, "y", k) for k in (1, 2, 3)])
    sum_qkv, sum_gains = call(
        unpack_kernel, [((128, 4096), F32), ((8, 512), F32)], [], 3, own, shift(own, "core", 1), info=info
    )
    (input_grad,) = call(last_kernel, [((RUN, 1024), F32)], [], 2, *d_h, x_own, d_x2, gain)
    return (
        output[None],
        input_grad[None],
        sum_qkv,
        sum_out,
        sum_gate,
        sum_up,
        sum_down,
        sum_gains[0, :128],
        sum_gains[0, 128:256],
        sum_gains[0, 256:272],
        sum_gains[0, 384:400],
    )


def solution(mesh):
    split = Mesh(mesh.devices.reshape(tuple(SIZES.values())), FSDP + CTX)
    rows, both = P(FSDP, None), P(FSDP, CTX, None)
    return jax.shard_map(
        shards,
        mesh=split,
        in_specs=(both,) + (rows,) * 6 + (P(FSDP),) * 4 + (both,),
        out_specs=(both, both) + (rows,) * 5 + (P(FSDP),) * 4,
        check_vma=False,
    )
```

```python
import functools

import jax
import jax.numpy as jnp
from jax import lax
from jax.experimental import pallas as pl
from jax.experimental.pallas import tpu as pltpu
from jax.sharding import Mesh
from jax.sharding import PartitionSpec as P

HEAD = 128
EPS = 1e-06
MASKED = -1e30
THETA = 1000000.0
SCALE = HEAD**-0.5
LOG2E = 1.4426950408889634
RUN = 128
FSDP = ("xlo", "z")
CTX = ("xhi", "y", "core")
TP = ("y", "core")
SIZES = {"xlo": 2, "z": 4, "xhi": 2, "y": 4, "core": 2}
BF = jnp.bfloat16
F32 = jnp.float32
SORTED, FOF, TOF, CORE = 0, 8, 16, 24


def shift(x, axis, step):
    n = SIZES[axis]
    return lax.ppermute(x, axis, [(i, (i + step) % n) for i in range(n)])


def gather_tokens(x):
    own = jnp.concatenate([x] + [shift(x, "y", k) for k in (1, 2, 3)], axis=0)
    return own, shift(own, "core", 1)


def scatter_tokens(own, other):
    blocks = (own.astype(F32) + shift(other, "core", 1).astype(F32)).astype(BF).reshape(4, own.shape[0] // 4, -1)
    return [blocks[0]] + [shift(blocks[k], "y", 4 - k) for k in (1, 2, 3)]


def exchange(own, other):
    both = jnp.stack([own, shift(other, "core", 1)], axis=1)
    return [both[0]] + [shift(both[k], "y", 4 - k) for k in (1, 2, 3)]


def spread_z(pair):
    return [pair] + [shift(pair, "z", k) for k in (1, 2, 3)]


def dot(a, b):
    return jnp.dot(a, b, preferred_element_type=F32)


def dot_nt(a, b):
    return lax.dot_general(a, b, (((1,), (1,)), ((), ())), preferred_element_type=F32)


def dot_tn(a, b):
    return lax.dot_general(a, b, (((0,), (0,)), ((), ())), preferred_element_type=F32)


def inv_rms(x):
    return lax.rsqrt(jnp.mean(x * x, axis=-1, keepdims=True) + EPS)


def norm_pull(x, gain, grad):
    inv = inv_rms(x)
    hat = x * inv
    scaled = grad * gain
    return inv * (scaled - hat * jnp.mean(scaled * hat, axis=-1, keepdims=True)), grad * hat


def ds(at, size):
    return pl.ds(pl.multiple_of(at, size), size)


def rows_of(i, size):
    return slice(i * size, (i + 1) * size)


def pack_kernel(at, q_ref, k_ref, v_ref, attn, ffn, qg, kg, out):
    out[:RUN, :256] = q_ref[...]
    out[:RUN, 256:384] = k_ref[...]
    out[:RUN, 384:] = v_ref[...]
    none = jnp.zeros((16, 112), BF)
    rows = [jnp.broadcast_to(g[...], (16, g.shape[1])) for g in (attn, ffn, qg, kg)]
    out[RUN:, :128] = rows[0]
    out[RUN:, 128:256] = rows[1]
    out[RUN:, 256:384] = jnp.concatenate([rows[2], none], axis=1)
    out[RUN:, 384:] = jnp.concatenate([rows[3], none], axis=1)


def key_value_kernel(info, own, sib, w0, w1, w2, w3, cos, sin, dy, h_ref, w_ref, gain_ref, raw_ref, kv_ref, dy_ref):
    dy_ref[...] = dy[...]
    gain_ref[...] = jnp.zeros_like(gain_ref)
    for k, part in enumerate((w0, w1, w2, w3)):
        for j in range(2):
            f = info[FOF + 4 * j + k]
            w_ref[ds(f * RUN, RUN), :] = part[j, :RUN, :]
            row = part[j, RUN:, :].astype(F32)[:8]
            gain_ref[:, ds(f * RUN, RUN)] = row[:, :128]
            gain_ref[:, ds(1024 + f * RUN, RUN)] = row[:, 128:256]
            gain_ref[:, 2048:2176] += pltpu.roll(row[:, 256:384], f * 16, 1)
            gain_ref[:, 2176:2304] += pltpu.roll(row[:, 384:512], f * 16, 1)
    attn_gain, k_gain = gain_ref[0:1, :1024], gain_ref[0:1, 2176:2304]
    for i in range(4):
        part = (own, sib)[i // 2]
        here = rows_of(i, 256)
        x = part[rows_of(i % 2, 256), :].astype(F32)
        h = (x * inv_rms(x) * attn_gain).astype(BF)
        h_ref[here, :] = h
        raw = dot(h, w_ref[:, 256:])
        raw_ref[here, :] = raw[:, :HEAD]
        key = raw[:, :HEAD]
        key = key * inv_rms(key) * k_gain
        key = key * cos[here, :] + pltpu.roll(key, HEAD // 2, 1) * sin[here, :]
        kv_ref[here, :HEAD] = key.astype(BF)
        kv_ref[here, HEAD:] = raw[:, HEAD:].astype(BF)


def query_kernel(h_ref, w_ref, gain_ref, cos, sin, raw_ref, q_ref):
    gain = gain_ref[0:1, 2048:2176]
    for i in range(4):
        here = rows_of(i, 256)
        raw = dot(h_ref[here, :], w_ref[:, :256])
        raw_ref[here, :] = raw
        for a in range(2):
            u = raw[:, rows_of(a, HEAD)]
            u = u * inv_rms(u) * gain
            u = u * cos[here, :] + pltpu.roll(u, HEAD // 2, 1) * sin[here, :]
            q_ref[here, rows_of(a, HEAD)] = u.astype(BF)


def stacked(rows):
    return jnp.concatenate([rows[:, :HEAD], rows[:, HEAD:]], axis=0)


def own_mask(pos_ref, b):
    row = pos_ref[b]
    keys = jnp.broadcast_to(row, (RUN, RUN)).T
    return jnp.concatenate([keys, keys], axis=1) <= jnp.concatenate([row, row], axis=1)


def expo(keys, q):
    return jnp.exp2(dot_nt(keys, q) * (SCALE * LOG2E))


def forward_own_kernel(info, pos_ref, q_ref, kv, part_ref, ks, vt):
    vt[HEAD:, :] = jnp.ones((HEAD, vt.shape[1]), BF)
    for s in range(8):
        src = ds(info[SORTED + s] * RUN, RUN)
        ks[rows_of(s, RUN), :] = kv[src, :HEAD]
        vt[:HEAD, rows_of(s, RUN)] = kv[src, HEAD:].T
    for s in range(8):
        b = info[SORTED + s]
        q = stacked(q_ref[ds(b * RUN, RUN), :])
        e = jnp.where(own_mask(pos_ref, b), expo(ks[rows_of(s, RUN), :], q), 0.0)
        acc = dot(vt[:, rows_of(s, RUN)], e.astype(BF))
        if s:
            acc += dot(vt[:, : s * RUN], expo(ks[: s * RUN, :], q).astype(BF))
        part_ref[b] = acc[: HEAD + 8]


def forward_other_kernel(bias, q_ref, kv, part_ref, o_ref, lse_ref, low_ref, vt):
    vt[HEAD:, :] = jnp.ones((HEAD, vt.shape[1]), BF)
    vt[:HEAD, :] = kv[:, HEAD:].T
    for i in range(8):
        q = stacked(q_ref[rows_of(i, RUN), :])
        scores = dot_nt(kv[:, :HEAD], q) * (SCALE * LOG2E)
        e = jnp.concatenate([jnp.exp2(scores[rows_of(b, RUN)] + bias[i, b]).astype(BF) for b in range(8)], axis=0)
        acc = dot(vt[...], e)
        total = acc[HEAD : HEAD + 1, :] + part_ref[i, HEAD : HEAD + 1, :]
        out = ((acc[:HEAD, :] + part_ref[i, :HEAD, :]) / total).T
        out = jnp.concatenate([out[:RUN], out[RUN:]], axis=1)
        o_ref[rows_of(i, RUN), :] = out
        low_ref[i // 4, i % 4] = out.astype(BF)
        lse_ref[i] = jnp.log2(total)


def out_kernel(info, x_ref, o0, o1, o2, o3, w_own, w_sib, gain_ref, x2_ref, h2_ref, oall_ref):
    core = info[CORE]
    for k, part in enumerate((o0, o1, o2, o3)):
        for j in range(2):
            at = info[TOF + 4 * j + (4 - k) % 4] * HEAD
            oall_ref[:, ds(at, HEAD)] = part[j, :, ds(core * HEAD, HEAD)]
            oall_ref[:, ds(1024 + at, HEAD)] = part[j, :, ds((1 - core) * HEAD, HEAD)]
    x2 = x_ref[...].astype(F32) + dot(oall_ref[:, :1024], w_own[...]) + dot(oall_ref[:, 1024:], w_sib[...])
    x2_ref[...] = x2
    h2_ref[...] = (x2 * inv_rms(x2) * gain_ref[0:1, 1024:2048]).astype(BF)


def pack_ffn_kernel(rank, gate, up, down, out):
    at = rank[0] * 48
    q = jnp.minimum(at // RUN, 1)
    for a, w in ((0, gate), (384, up)):
        pieces = []
        for f in range(8):
            window = w[:, pl.ds(pl.multiple_of(f * 384 + q * RUN, RUN), 256)].astype(F32)
            pieces.append(pltpu.roll(window, (256 - (at - q * RUN)) % 256, 1)[:, :48])
        out[:RUN, a : a + 384] = jnp.concatenate(pieces, axis=1).astype(BF)
    rows = down[pl.ds(pl.multiple_of(at, 16), 48), :]
    out[128:176, :] = rows[:, :768]
    for n in range(3):
        out[176:192, rows_of(n, 256)] = rows[16 * n : 16 * n + 16, 768:]


def copy_kernel(a, out):
    out[...] = a[...]


def pair_kernel(rank, a, b, out, rank_out):
    out[0] = a[...]
    out[1] = b[...]
    rank_out[...] = jnp.full(rank_out.shape, rank[0], jnp.int32)


def assemble_out_kernel(info, p0, p1, p2, p3, w_ref):
    for k, part in enumerate((p0, p1, p2, p3)):
        for j in range(2):
            w_ref[ds(info[FOF + 4 * j + k] * HEAD, HEAD), :] = part[j]


def assemble_kernel(info, p0, p1, p2, p3, wgu, wd):
    for k, part in enumerate((p0, p1, p2, p3)):
        for j in range(2):
            f = info[FOF + 4 * j + k]
            wgu[ds(f * RUN, RUN), :] = part[j, :RUN, :]
            wd[pl.ds(pl.multiple_of(f * 48, 16), 48), :768] = part[j, 128:176, :]
            for n in range(3):
                wd[ds(f * 48 + 16 * n, 16), 768:] = part[j, 176:192, rows_of(n, 256)]


def blocks_of(info, dy_ref, first, count):
    return jnp.concatenate([dy_ref[ds(info[TOF + first + n] * RUN, RUN), :] for n in range(count)], axis=0)


def ffn_kernel(base, info, h2_ref, dy_ref, wgu, wd, act_ref, dgu_ref, part_ref):
    for i in range(2):
        here = rows_of(i, 256)
        gu = dot(h2_ref[here, :], wgu[...])
        gate, up = gu[:, :384], gu[:, 384:]
        sg = 1.0 / (1.0 + jnp.exp(-gate))
        silu = gate * sg
        act_ref[here, :] = (silu * up).astype(BF)
        d_act = dot_nt(blocks_of(info, dy_ref, base + 2 * i, 2), wd[...])
        d_gate = (d_act * up * (sg * (1.0 + gate * (1.0 - sg)))).astype(BF)
        d_gu = jnp.concatenate([d_gate, (d_act * silu).astype(BF)], axis=1)
        dgu_ref[here, :] = d_gu
        part_ref[here, :] = dot_nt(d_gu, wgu[...]).astype(BF)


def ffn_grad_kernel(info, h2_own, h2_sib, dy_ref, act_own, act_sib, dgu_own, dgu_sib, wd, g_ref, y_own, y_sib):
    y_own[...] = dot(act_own[...], wd[...]).astype(BF)
    y_sib[...] = dot(act_sib[...], wd[...]).astype(BF)
    for a in range(4):
        cols = rows_of(a, 256)
        g = (dot_tn(h2_own[:, cols], dgu_own[...]) + dot_tn(h2_sib[:, cols], dgu_sib[...])).astype(BF)
        g_ref[2 * a, :RUN, :] = g[:RUN]
        g_ref[2 * a + 1, :RUN, :] = g[RUN:]
    g = dot_tn(act_own[...], blocks_of(info, dy_ref, 0, 4)) + dot_tn(act_sib[...], blocks_of(info, dy_ref, 4, 4))
    g = g.astype(BF)
    for f in range(8):
        rows = g[f * 48 : (f + 1) * 48]
        g_ref[f, 128:176, :] = rows[:, :768]
        for n in range(3):
            g_ref[f, 176:192, rows_of(n, 256)] = rows[16 * n : 16 * n + 16, 768:]


def middle_kernel(
    info, p0, p1, p2, p3, x2_ref, dy_ref, gain_ref, w_own, w_sib, dx2_ref, low_ref, gsum_ref, do_own, do_other, do
):
    grad = sum(p[...].astype(F32) for p in (p0, p1, p2, p3))
    pulled, by_gain = norm_pull(x2_ref[...], gain_ref[0:1, 1024:2048], grad)
    gsum_ref[...] = jnp.sum(by_gain, axis=0, keepdims=True)
    dx2 = dy_ref[...].astype(F32) + pulled
    dx2_ref[...] = dx2
    low = dx2.astype(BF)
    low_ref[...] = low
    do[:, :1024] = dot_nt(low, w_own[...]).astype(BF)
    do[:, 1024:] = dot_nt(low, w_sib[...]).astype(BF)
    core = info[CORE]
    for j, out in enumerate((do_own, do_other)):
        for k in range(4):
            at = info[TOF + 4 * j + k] * HEAD
            out[k, :, ds(core * HEAD, HEAD)] = do[:, ds(at, HEAD)]
            out[k, :, ds((1 - core) * HEAD, HEAD)] = do[:, ds(1024 + at, HEAD)]


def out_grad_kernel(info, o_ref, d_ref, own_ref, other_ref, g_all):
    core = info[CORE]
    for a in range(8):
        g_all[...] = dot_tn(o_ref[:, rows_of(a, 256)], d_ref[...]).astype(BF)
        for n in range(2):
            f, half = (2 * a + n) % 8, core if a < 4 else 1 - core
            rows = ds((2 * f + half) * HEAD, HEAD)
            for k in range(4):
                own_ref[k, rows, :] = g_all[rows_of(n, HEAD), ds(info[TOF + k] * RUN, RUN)]
                other_ref[k, rows, :] = g_all[rows_of(n, HEAD), ds(info[TOF + 4 + k] * RUN, RUN)]


def backward_run(b, ref_b, q_ref, o_ref, lse_ref, do):
    rows = ds(b * RUN, RUN)
    q = stacked(q_ref[rows, :])
    do = stacked(do)
    delta = jnp.sum((do.astype(F32) * stacked(o_ref[rows, :])).T, axis=0, keepdims=True)
    return q, do, delta, lse_ref[ref_b]


def backward_other_kernel(bias, q_ref, kv, o_ref, lse_ref, d0, d1, d2, d3, dq_ref, dkv_ref, dk, dv):
    for i in range(8):
        q, do, delta, lse = backward_run(i, i, q_ref, o_ref, lse_ref, (d0, d3, d2, d1)[i % 4][i // 4])
        scores = dot_nt(kv[:, :HEAD], q) * (SCALE * LOG2E)
        p = jnp.concatenate([jnp.exp2(scores[rows_of(b, RUN)] - (lse - bias[i, b])) for b in range(8)], axis=0)
        d_s = (p * (dot_nt(kv[:, HEAD:], do) - delta)).astype(BF)
        by_v, by_k = dot(p.astype(BF), do), dot(d_s, q)
        dv[...] = by_v if i == 0 else dv[...] + by_v
        dk[...] = by_k if i == 0 else dk[...] + by_k
        dq_ref[i] = dot_tn(d_s, kv[:, :HEAD])
    dkv_ref[:, :HEAD] = (dk[...] * SCALE).astype(BF)
    dkv_ref[:, HEAD:] = dv[...].astype(BF)


def backward_own_kernel(
    info, pos_ref, q_ref, kv, o_ref, lse_ref, d0, d1, d2, d3, before, dq_ref, dkv_ref, ks, vs, dk, dv, dos
):
    for s in range(8):
        src = ds(info[SORTED + s] * RUN, RUN)
        ks[rows_of(s, RUN), :] = kv[src, :HEAD]
        vs[rows_of(s, RUN), :] = kv[src, HEAD:]
        dos[s] = (d0, d3, d2, d1)[s % 4][s // 4]
    dk[...] = jnp.zeros_like(dk)
    dv[...] = jnp.zeros_like(dv)
    for s in range(8):
        b = info[SORTED + s]
        q, do, delta, lse = backward_run(b, b, q_ref, o_ref, lse_ref, dos[b])
        keys = ks[: (s + 1) * RUN, :]
        p = jnp.exp2(dot_nt(keys, q) * (SCALE * LOG2E) - lse)
        diagonal = jnp.where(own_mask(pos_ref, b), p[s * RUN :], 0.0)
        p = jnp.concatenate([p[: s * RUN], diagonal], axis=0) if s else diagonal
        d_s = (p * (dot_nt(vs[: (s + 1) * RUN, :], do) - delta)).astype(BF)
        dv[: (s + 1) * RUN, :] += dot(p.astype(BF), do)
        dk[: (s + 1) * RUN, :] += dot(d_s, q)
        dq = (dot_tn(d_s, keys) + before[b]) * SCALE
        dq_ref[ds(b * RUN, RUN), :HEAD] = dq[:RUN]
        dq_ref[ds(b * RUN, RUN), HEAD:] = dq[RUN:]
    for s in range(8):
        src = ds(info[SORTED + s] * RUN, RUN)
        dkv_ref[src, :HEAD] = dk[rows_of(s, RUN), :] * SCALE
        dkv_ref[src, HEAD:] = dv[rows_of(s, RUN), :]


def head_back(raw, gain, grad, cos, sin):
    grad = grad * cos + pltpu.roll(grad * sin, HEAD // 2, 1)
    pulled, by_gain = norm_pull(raw, gain, grad)
    return pulled.astype(BF), jnp.sum(by_gain, axis=0, keepdims=True)


def query_back_kernel(info, h_ref, gain_ref, cos, sin, raw, dq_ref, low_ref, g_ref, sum_ref):
    sum_ref[...] = jnp.zeros_like(sum_ref)
    for i in range(4):
        here = rows_of(i, 256)
        for a in range(2):
            cols = rows_of(a, HEAD)
            low, by_gain = head_back(raw[here, cols], gain_ref[0:1, 2048:2176], dq_ref[here, cols], cos[here, :], sin[here, :])
            low_ref[here, cols] = low
            sum_ref[...] += by_gain
    for k in range(4):
        for j in range(2):
            f = info[FOF + 4 * j + (4 - k) % 4]
            g_ref[k, j] = dot_tn(h_ref[:, ds(f * RUN, RUN)], low_ref[...])


def key_value_back_kernel(
    info, h_ref, w_ref, gain_ref, cos, sin, raw, dkv_ref, recv, gq_ref, qsum, ffn_ref,
    out0, out1, out2, out3, dq_ref, y_own, y_sib, g0, g1, g2, g3, own_ref, sib_ref, low_ref,
):
    sums = jnp.zeros((1, HEAD), F32)
    for i in range(4):
        here = rows_of(i, 256)
        dkv = dkv_ref[here, :] + recv[here, :].astype(F32)
        low, by_gain = head_back(raw[here, :], gain_ref[0:1, 2176:2304], dkv[:, :HEAD], cos[here, :], sin[here, :])
        low_ref[here, :HEAD] = low
        low_ref[here, HEAD:] = dkv[:, HEAD:].astype(BF)
        sums += by_gain
    lane = lax.broadcasted_iota(jnp.int32, (8, HEAD), 1)
    heads = [jnp.broadcast_to(s, (8, HEAD)) for s in (qsum[...], sums)]
    for k, g_ref in enumerate((g0, g1, g2, g3)):
        for j in range(2):
            f = info[FOF + 4 * j + (4 - k) % 4]
            here = ds(f * RUN, RUN)
            gkv = dot_tn(h_ref[:, here], low_ref[...])
            gq = gq_ref[k, j]
            g_ref[j, :RUN, :256] = gq.astype(BF)
            g_ref[j, :RUN, 256:] = gkv.astype(BF)
            by_attn = jnp.sum(gq * w_ref[here, :256].astype(F32) + gkv * w_ref[here, 256:].astype(F32), axis=1, keepdims=True)
            by_attn = jnp.broadcast_to(by_attn, (RUN, RUN)).T[:8] / gain_ref[:, here]
            rows = [by_attn, jnp.broadcast_to(ffn_ref[0:1, here], (8, RUN))]
            rows += [jnp.where(lane < 16, pltpu.roll(r, HEAD - 16 * f, 1), 0.0) for r in heads]
            rows = jnp.concatenate(rows, axis=1)
            g_ref[j, RUN : RUN + 16, :] = jnp.concatenate([rows, rows], axis=0).astype(BF)
            for n in range(4):
                src = ds(f * 256 + n * 64, 64)
                rows = sum(o[src, :].astype(F32) for o in (out0, out1, out2, out3))
                g_ref[j, RUN + 16 :, rows_of(n, RUN)] = rows.astype(BF)
    for i in range(4):
        here = rows_of(i, 256)
        part = dot_nt(dq_ref[here, :], w_ref[:, :256]) + dot_nt(low_ref[here, :], w_ref[:, 256:])
        part = part.astype(BF)
        out, y_ref = ((own_ref, y_own), (sib_ref, y_sib))[i // 2]
        for n in range(2):
            k = 2 * (i % 2) + n
            out[rows_of(2 * k, RUN), :] = part[rows_of(n, RUN)]
            out[rows_of(2 * k + 1, RUN), :] = y_ref[rows_of(k, RUN), :]


def last_kernel(p0, p1, p2, p3, x_ref, x2_ref, dx2_ref, gain_ref, out_ref, grad_ref):
    sums = sum(p[...].astype(F32) for p in (p0, p1, p2, p3))
    out_ref[...] = (x2_ref[...] + sums[RUN:]).astype(BF)
    grad_ref[...] = dx2_ref[...] + norm_pull(x_ref[...].astype(F32), gain_ref[0:1, :1024], sums[:RUN])[0]


def unpack_kernel(info, own, sib, g_ref, out_ref, gain_ref):
    gain_ref[...] = jnp.zeros_like(gain_ref)
    for j, part in enumerate((own, sib)):
        for k in range(4):
            t = info[TOF + 4 * j + k]
            g_ref[:, ds(t * 256, 256)] = part[k, :RUN, :256].astype(F32)
            g_ref[:, ds(2048 + t * RUN, RUN)] = part[k, :RUN, 256:384].astype(F32)
            g_ref[:, ds(3072 + t * RUN, RUN)] = part[k, :RUN, 384:].astype(F32)
            gain_ref[...] += part[k, RUN : RUN + 16, :].astype(F32)[:8]
            for n in range(4):
                out_ref[rows_of(n, 64), ds(t * RUN, RUN)] = part[k, RUN + 16 :, rows_of(n, RUN)].astype(F32)


def z_sum_kernel(g0, g1, g2, g3, mine, theirs):
    for j, out in enumerate((mine, theirs)):
        out[...] = sum(p[j].astype(F32) for p in (g0, g1, g2, g3)).astype(BF)


def add_kernel(a, b, out):
    for i in range(8):
        here = rows_of(i, 128)
        out[here, :] = (a[here, :].astype(F32) + b[here, :].astype(F32)).astype(BF)


def sum_kernel(a, b, c, d, out):
    out[...] = (a[...].astype(F32) + b[...].astype(F32) + c[...].astype(F32) + d[...].astype(F32)).astype(BF)


def unpack_ffn_kernel(wide, gate, up, down):
    for a, out in ((0, gate), (384, up)):
        for f in range(8):
            cols = slice(a + f * 48, a + f * 48 + 48)
            here = slice(f * 384, (f + 1) * 384)
            out[:96, here] = jnp.concatenate([wide[t, :, cols].astype(F32) for t in range(8)], axis=1)
            out[96:, here] = jnp.concatenate([wide[8 + t, :32, cols].astype(F32) for t in range(8)], axis=1)
    for t in range(8):
        down[t * 48 : (t + 1) * 48, :768] = wide[8 + t, 32:80, :].astype(F32)
        for n in range(3):
            at = t * 48 + 16 * n
            down[at : at + 16, 768:] = wide[8 + t, 80:96, rows_of(n, 256)].astype(F32)


def call(kernel, outs, scratch, micros, *args, info=None, deps=()):
    smem = [] if info is None else [info]
    first, late = len(smem) + len(args), len(smem) + len(args) + len(deps)
    return pl.pallas_call(
        lambda *refs: kernel(*refs[:first], *refs[late:]),
        name=getattr(kernel, "func", kernel).__name__,
        out_shape=[jax.ShapeDtypeStruct(*o) for o in outs],
        in_specs=[pl.BlockSpec(memory_space=pltpu.SMEM)] * len(smem)
        + [pl.BlockSpec(memory_space=pltpu.VMEM)] * len(args)
        + [pl.BlockSpec(memory_space=pl.ANY)] * len(deps),
        out_specs=[pl.BlockSpec(memory_space=pltpu.VMEM)] * len(outs),
        scratch_shapes=[pltpu.VMEM(*s) for s in scratch],
        compiler_params=pltpu.CompilerParams(vmem_limit_bytes=16 * 2**20),
        cost_estimate=pl.CostEstimate(flops=int(micros * 1e7), bytes_accessed=2**10, transcendentals=0),
    )(*smem, *args, *deps)


def shards(
    tokens, positions, w_qkv, w_out, w_gate, w_up, w_down, attn_gain, ffn_gain, q_gain, k_gain, cotangent
):
    xhi, y, core = (lax.axis_index(a) for a in CTX)
    xlo, z = (lax.axis_index(a) for a in FSDP)
    t = y * 2 + core
    x_own, dy = tokens[0], cotangent[0]

    wqs = [pl.BlockSpec((RUN, n), lambda i, at, first=first: (0, first + at[0])) for n, first in ((256, 0), (128, 16), (128, 24))]
    small = [g[None] for g in (attn_gain, ffn_gain, q_gain, k_gain)]
    slice_qkv = pl.pallas_call(
        pack_kernel,
        out_shape=jax.ShapeDtypeStruct((RUN + 16, 512), BF),
        grid_spec=pltpu.PrefetchScalarGridSpec(
            num_scalar_prefetch=1,
            grid=(1,),
            in_specs=wqs + [pl.BlockSpec(g.shape, lambda i, at: (0, 0)) for g in small],
            out_specs=pl.BlockSpec((RUN + 16, 512), lambda i, at: (0, 0)),
        ),
    )(t[None].astype(jnp.int32), w_qkv, w_qkv, w_qkv, *small)
    xs = gather_tokens(x_own)
    here = t[None].astype(jnp.int32)
    later = ((8, RUN), jnp.int32)
    pair_qkv, later_t = call(
        pair_kernel, [((2, RUN + 16, 512), BF), later], [], 1, slice_qkv, shift(slice_qkv, "xlo", 1), info=here
    )
    parts_qkv = spread_z(pair_qkv)
    later_t = later_t[0, 0]
    eight = jnp.arange(8, dtype=jnp.int32)
    block = lax.rem(y - eight % 4 + 4, 4) * 2 + (core ^ (eight // 4))
    f_of = (xlo ^ (eight // 4)) * 4 + lax.rem(z - eight % 4 + 4, 4)
    blocks = jnp.concatenate([xhi * 8 + block, (1 - xhi) * 8 + block])
    pos = (positions[0] + later_t // 8).reshape(16, RUN)[blocks]
    rank = pos[:, 0] // RUN
    place = jnp.sum(rank[:8, None] > rank[None, :8], axis=1)
    in_order = jnp.argmax(place[None, :] == eight[:, None], axis=1)
    info = jnp.concatenate([in_order, f_of, block, core[None]]).astype(jnp.int32)
    bias = jnp.where(rank[:8, None] > rank[None, 8:], 0.0, MASKED)
    pos_rows = pos.astype(F32).reshape(16, 1, RUN)
    inverse = THETA ** (-(jnp.arange(HEAD // 2, dtype=F32) * 2.0 / HEAD))
    angles = pos[:8].reshape(1024).astype(F32)[:, None] * inverse[None, :]
    cosine, sine = jnp.cos(angles), jnp.sin(angles)
    cosine = jnp.concatenate([cosine, cosine], axis=1)
    sine = jnp.concatenate([-sine, sine], axis=1)

    half_out = lax.dynamic_slice_in_dim(w_out, core * HEAD, HEAD, 0)
    pair_out, _ = call(
        pair_kernel,
        [((2, RUN, 1024), BF), later],
        [],
        1,
        half_out, shift(half_out, "xlo", 1),
        info=here,
        deps=parts_qkv[1:],
    )
    parts_out = spread_z(pair_out)
    (slice_ffn,) = call(
        pack_ffn_kernel, [((192, 768), BF)], [], 3, w_gate, w_up, w_down, info=here, deps=[pair_qkv]
    )
    received = shift(slice_ffn, "xlo", 1)

    h, wqkv, gain, kraw, kv, dy_later = call(
        key_value_kernel,
        [((1024, 1024), BF), ((1024, 512), BF), ((8, 2304), F32), ((1024, HEAD), F32), ((1024, 256), BF), ((RUN, 1024), BF)],
        [],
        5,
        *xs, *parts_qkv, cosine, sine, dy,
        info=info,
        deps=[slice_ffn, pair_out],
    )
    kv_other = shift(kv, "xhi", 1)
    qraw, q = call(query_kernel, [((1024, 256), F32), ((1024, 256), BF)], [], 3, h, wqkv, gain, cosine, sine)
    (partial,) = call(
        forward_own_kernel,
        [((8, HEAD + 8, 256), F32)],
        [((1024, HEAD), BF), ((256, 1024), BF)],
        5,
        pos_rows, q, kv,
        info=info,
    )
    ffn_pairs = lambda *deps: call(
        pair_kernel, [((2, 192, 768), BF), later], [], 1, slice_ffn, received, info=here, deps=deps
    )[0]
    pair_ffn = ffn_pairs(parts_out[1], parts_out[3], kv_other)
    parts_ffn = [pair_ffn, shift(pair_ffn, "z", 1), None, shift(pair_ffn, "z", 3)]
    dy_all = lax.all_gather(dy_later, TP, axis=0, tiled=True)
    o32, lse, o_low = call(
        forward_other_kernel,
        [((1024, 256), F32), ((8, 1, 256), F32), ((2, 4, RUN, 256), BF)],
        [((256, 1024), BF)],
        6,
        q, kv_other, partial,
        info=bias,
        deps=[parts_out[1], parts_out[3]],
    )
    (wout_own,) = call(assemble_out_kernel, [((1024, 1024), BF)], [], 1, *parts_out, info=info, deps=[o_low])
    wout_sib = shift(wout_own, "core", 1)
    x2, h2_own, o_all = call(
        out_kernel,
        [((RUN, 1024), F32), ((RUN, 1024), BF), ((RUN, 2048), BF)],
        [],
        4,
        x_own, *exchange(o_low[0], o_low[1]), wout_own, wout_sib, gain,
        info=info,
        deps=[parts_ffn[1], parts_ffn[3]],
    )
    parts_ffn[2] = shift(ffn_pairs(h2_own), "z", 2)
    wgu, wd = call(assemble_kernel, [((1024, 768), BF), ((384, 1024), BF)], [], 2, *parts_ffn, info=info)

    h2 = gather_tokens(h2_own)
    ffn = [
        call(
            functools.partial(ffn_kernel, 4 * j),
            [((512, 384), BF), ((512, 768), BF), ((512, 1024), BF)],
            [],
            6,
            h2[j], dy_all, wgu, wd,
            info=info,
        )
        for j in (1, 0)
    ]
    (act_sib, dgu_sib, part_sib), (act_own, dgu_own, part_own) = ffn
    d_h2 = scatter_tokens(part_own, part_sib)
    g_ffn, y_own, y_sib = call(
        ffn_grad_kernel,
        [((8, 192, 768), BF), ((512, 1024), BF), ((512, 1024), BF)],
        [],
        8,
        *h2, dy_all, act_own, act_sib, dgu_own, dgu_sib, wd,
        info=info,
    )
    d_x2, d_branch, ffn_sum, do_own, do_other = call(
        middle_kernel,
        [((RUN, 1024), F32), ((RUN, 1024), BF), ((1, 1024), F32), ((4, RUN, 256), BF), ((4, RUN, 256), BF)],
        [((RUN, 2048), BF)],
        5,
        *d_h2, x2, dy, gain, wout_own, wout_sib,
        info=info,
        deps=[g_ffn],
    )
    d_o = exchange(do_own, do_other)
    g_out_own, g_out_other = call(
        out_grad_kernel, [((4, 2048, RUN), BF)] * 2, [((256, 1024), BF)], 4, o_all, d_branch, info=info
    )

    rows_ffn = lax.psum_scatter(g_ffn.reshape(16, 96, 768), FSDP + ("xhi",), scatter_dimension=0, tiled=False)
    blocks_out = (g_out_own.astype(F32) + shift(g_out_other, "core", 1).astype(F32)).astype(BF)
    out_parts = [blocks_out[0]] + [shift(blocks_out[k], "y", 4 - k) for k in (1, 2, 3)]

    d_q, d_other = call(
        backward_other_kernel,
        [((8, 256, HEAD), F32), ((1024, 256), BF)],
        [((1024, HEAD), F32), ((1024, HEAD), F32)],
        8,
        q, kv_other, o32, lse, *d_o,
        info=bias,
        deps=[blocks_out],
    )
    recv = shift(d_other, "xhi", 1)
    d_q, d_kv = call(
        backward_own_kernel,
        [((1024, 256), F32), ((1024, 256), F32)],
        [((1024, HEAD), BF), ((1024, HEAD), BF), ((1024, HEAD), F32), ((1024, HEAD), F32), ((8, RUN, 256), BF)],
        8,
        pos_rows, q, kv, o32, lse, *d_o, d_q,
        info=info,
    )
    dq_low, g_q, q_sum = call(
        query_back_kernel,
        [((1024, 256), BF), ((4, 2, RUN, 256), F32), ((1, HEAD), F32)],
        [],
        5,
        h, gain, cosine, sine, qraw, d_q,
        info=info,
    )
    *g_qkv, part_own, part_sib = call(
        key_value_back_kernel,
        [((2, 208, 512), BF)] * 4 + [((1024, 1024), BF)] * 2,
        [((1024, 256), BF)],
        5,
        h, wqkv, gain, cosine, sine, kraw, d_kv, recv, g_q, q_sum, ffn_sum, *out_parts, dq_low, y_own, y_sib,
        info=info,
    )
    g_qkv = [g_qkv[0]] + [shift(g_qkv[k], "z", k) for k in (1, 2, 3)]
    (d_h,) = call(add_kernel, [((1024, 1024), BF)], [], 1, part_own, shift(part_sib, "core", 1))
    sum_ffn = lax.all_gather(rows_ffn, CTX, axis=0)
    sum_gate, sum_up, sum_down = call(
        unpack_ffn_kernel, [((128, 3072), F32), ((128, 3072), F32), ((384, 1024), F32)], [], 4, sum_ffn
    )
    mine, theirs = call(z_sum_kernel, [((208, 512), BF)] * 2, [], 1, *g_qkv, deps=[d_h])
    d_h = d_h.reshape(4, 256, 1024)
    d_h = [d_h[0]] + [shift(d_h[k], "y", 4 - k) for k in (1, 2, 3)]
    cross = lax.ppermute(theirs, ("xlo", "xhi"), [(i, i ^ 3) for i in range(4)])
    (total,) = call(
        sum_kernel, [((208, 512), BF)], [], 1, mine, shift(theirs, "xlo", 1), shift(mine, "xhi", 1), cross, deps=[sum_gate] + d_h[1:]
    )
    own = jnp.stack([total] + [shift(total, "y", k) for k in (1, 2, 3)])
    sum_qkv, sum_out, sum_gains = call(
        unpack_kernel,
        [((128, 4096), F32), ((256, 1024), F32), ((8, 512), F32)],
        [],
        3,
        own, shift(own, "core", 1),
        info=info,
    )
    output, input_grad = call(
        last_kernel, [((RUN, 1024), BF), ((RUN, 1024), F32)], [], 2, *d_h, x_own, x2, d_x2, gain
    )
    return (
        output[None],
        input_grad[None],
        sum_qkv,
        sum_out,
        sum_gate,
        sum_up,
        sum_down,
        sum_gains[0, :128],
        sum_gains[0, 128:256],
        sum_gains[0, 256:272],
        sum_gains[0, 384:400],
    )


def solution(mesh):
    split = Mesh(mesh.devices.reshape(tuple(SIZES.values())), FSDP + CTX)
    rows, both = P(FSDP, None), P(FSDP, CTX, None)
    return jax.shard_map(
        shards,
        mesh=split,
        in_specs=(both,) + (rows,) * 6 + (P(FSDP),) * 4 + (both,),
        out_specs=(both, both) + (rows,) * 5 + (P(FSDP),) * 4,
        check_vma=False,
    )
```

```python
import functools

import jax
import jax.numpy as jnp
from jax import lax
from jax.experimental import pallas as pl
from jax.experimental.pallas import tpu as pltpu
from jax.sharding import Mesh
from jax.sharding import PartitionSpec as P

HEAD = 128
EPS = 1e-06
MASKED = -1e30
THETA = 1000000.0
SCALE = HEAD**-0.5
LOG2E = 1.4426950408889634
RUN = 128
FSDP = ("xlo", "z")
CTX = ("xhi", "y", "core")
TP = ("y", "core")
SIZES = {"xlo": 2, "z": 4, "xhi": 2, "y": 4, "core": 2}
BF = jnp.bfloat16
F32 = jnp.float32
SORTED, FOF, TOF, CORE = 0, 8, 16, 24


def shift(x, axis, step):
    n = SIZES[axis]
    return lax.ppermute(x, axis, [(i, (i + step) % n) for i in range(n)])


def gather_tokens(x):
    own = jnp.concatenate([x] + [shift(x, "y", k) for k in (1, 2, 3)], axis=0)
    return own, shift(own, "core", 1)


def scatter_tokens(own, other):
    blocks = (own.astype(F32) + shift(other, "core", 1).astype(F32)).astype(BF).reshape(4, own.shape[0] // 4, -1)
    return [blocks[0]] + [shift(blocks[k], "y", 4 - k) for k in (1, 2, 3)]


def exchange(own, other):
    both = jnp.stack([own, shift(other, "core", 1)], axis=1)
    return [both[0]] + [shift(both[k], "y", 4 - k) for k in (1, 2, 3)]


def spread_z(pair):
    return [pair] + [shift(pair, "z", k) for k in (1, 2, 3)]


def dot(a, b):
    return jnp.dot(a, b, preferred_element_type=F32)


def dot_nt(a, b):
    return lax.dot_general(a, b, (((1,), (1,)), ((), ())), preferred_element_type=F32)


def dot_tn(a, b):
    return lax.dot_general(a, b, (((0,), (0,)), ((), ())), preferred_element_type=F32)


def inv_rms(x):
    return lax.rsqrt(jnp.mean(x * x, axis=-1, keepdims=True) + EPS)


def norm_pull(x, gain, grad):
    inv = inv_rms(x)
    hat = x * inv
    scaled = grad * gain
    return inv * (scaled - hat * jnp.mean(scaled * hat, axis=-1, keepdims=True)), grad * hat


def ds(at, size):
    return pl.ds(pl.multiple_of(at, size), size)


def rows_of(i, size):
    return slice(i * size, (i + 1) * size)


def pack_kernel(at, q_ref, k_ref, v_ref, attn, ffn, qg, kg, out):
    out[:RUN, :256] = q_ref[...]
    out[:RUN, 256:384] = k_ref[...]
    out[:RUN, 384:] = v_ref[...]
    none = jnp.zeros((16, 112), BF)
    rows = [jnp.broadcast_to(g[...], (16, g.shape[1])) for g in (attn, ffn, qg, kg)]
    out[RUN:, :128] = rows[0]
    out[RUN:, 128:256] = rows[1]
    out[RUN:, 256:384] = jnp.concatenate([rows[2], none], axis=1)
    out[RUN:, 384:] = jnp.concatenate([rows[3], none], axis=1)


def key_value_kernel(info, own, sib, w0, w1, w2, w3, cos, sin, dy, h_ref, w_ref, gain_ref, raw_ref, kv_ref, dy_ref):
    dy_ref[...] = dy[...]
    gain_ref[...] = jnp.zeros_like(gain_ref)
    for k, part in enumerate((w0, w1, w2, w3)):
        for j in range(2):
            f = info[FOF + 4 * j + k]
            w_ref[ds(f * RUN, RUN), :] = part[j, :RUN, :]
            row = part[j, RUN:, :].astype(F32)[:8]
            gain_ref[:, ds(f * RUN, RUN)] = row[:, :128]
            gain_ref[:, ds(1024 + f * RUN, RUN)] = row[:, 128:256]
            gain_ref[:, 2048:2176] += pltpu.roll(row[:, 256:384], f * 16, 1)
            gain_ref[:, 2176:2304] += pltpu.roll(row[:, 384:512], f * 16, 1)
    attn_gain, k_gain = gain_ref[0:1, :1024], gain_ref[0:1, 2176:2304]
    for i in range(4):
        part = (own, sib)[i // 2]
        here = rows_of(i, 256)
        x = part[rows_of(i % 2, 256), :].astype(F32)
        h = (x * inv_rms(x) * attn_gain).astype(BF)
        h_ref[here, :] = h
        raw = dot(h, w_ref[:, 256:])
        raw_ref[here, :] = raw[:, :HEAD]
        key = raw[:, :HEAD]
        key = key * inv_rms(key) * k_gain
        key = key * cos[here, :] + pltpu.roll(key, HEAD // 2, 1) * sin[here, :]
        kv_ref[here, :HEAD] = key.astype(BF)
        kv_ref[here, HEAD:] = raw[:, HEAD:].astype(BF)


def query_kernel(h_ref, w_ref, gain_ref, cos, sin, raw_ref, q_ref):
    gain = gain_ref[0:1, 2048:2176]
    for i in range(4):
        here = rows_of(i, 256)
        raw = dot(h_ref[here, :], w_ref[:, :256])
        raw_ref[here, :] = raw
        for a in range(2):
            u = raw[:, rows_of(a, HEAD)]
            u = u * inv_rms(u) * gain
            u = u * cos[here, :] + pltpu.roll(u, HEAD // 2, 1) * sin[here, :]
            q_ref[here, rows_of(a, HEAD)] = u.astype(BF)


def stacked(rows):
    return jnp.concatenate([rows[:, :HEAD], rows[:, HEAD:]], axis=0)


def own_mask(pos_ref, b):
    row = pos_ref[b]
    keys = jnp.broadcast_to(row, (RUN, RUN)).T
    return jnp.concatenate([keys, keys], axis=1) <= jnp.concatenate([row, row], axis=1)


def expo(keys, q):
    return jnp.exp2(dot_nt(keys, q) * (SCALE * LOG2E))


def forward_own_kernel(info, pos_ref, q_ref, kv, part_ref, ks, vt):
    vt[HEAD:, :] = jnp.ones((HEAD, vt.shape[1]), BF)
    for s in range(8):
        src = ds(info[SORTED + s] * RUN, RUN)
        ks[rows_of(s, RUN), :] = kv[src, :HEAD]
        vt[:HEAD, rows_of(s, RUN)] = kv[src, HEAD:].T
    for s in range(8):
        b = info[SORTED + s]
        q = stacked(q_ref[ds(b * RUN, RUN), :])
        e = jnp.where(own_mask(pos_ref, b), expo(ks[rows_of(s, RUN), :], q), 0.0)
        acc = dot(vt[:, rows_of(s, RUN)], e.astype(BF))
        if s:
            acc += dot(vt[:, : s * RUN], expo(ks[: s * RUN, :], q).astype(BF))
        part_ref[b] = acc[: HEAD + 8]


def forward_other_kernel(bias, q_ref, kv, part_ref, o_ref, lse_ref, low_ref, vt):
    vt[HEAD:, :] = jnp.ones((HEAD, vt.shape[1]), BF)
    vt[:HEAD, :] = kv[:, HEAD:].T
    for i in range(8):
        q = stacked(q_ref[rows_of(i, RUN), :])
        scores = dot_nt(kv[:, :HEAD], q) * (SCALE * LOG2E)
        e = jnp.concatenate([jnp.exp2(scores[rows_of(b, RUN)] + bias[i, b]).astype(BF) for b in range(8)], axis=0)
        acc = dot(vt[...], e)
        total = acc[HEAD : HEAD + 1, :] + part_ref[i, HEAD : HEAD + 1, :]
        out = ((acc[:HEAD, :] + part_ref[i, :HEAD, :]) / total).T
        out = jnp.concatenate([out[:RUN], out[RUN:]], axis=1)
        o_ref[rows_of(i, RUN), :] = out
        low_ref[i // 4, i % 4] = out.astype(BF)
        lse_ref[i] = jnp.log2(total)


def out_kernel(info, x_ref, o0, o1, o2, o3, w_own, w_sib, gain_ref, x2_ref, h2_ref, oall_ref):
    core = info[CORE]
    for k, part in enumerate((o0, o1, o2, o3)):
        for j in range(2):
            at = info[TOF + 4 * j + (4 - k) % 4] * HEAD
            oall_ref[:, ds(at, HEAD)] = part[j, :, ds(core * HEAD, HEAD)]
            oall_ref[:, ds(1024 + at, HEAD)] = part[j, :, ds((1 - core) * HEAD, HEAD)]
    x2 = x_ref[...].astype(F32) + dot(oall_ref[:, :1024], w_own[...]) + dot(oall_ref[:, 1024:], w_sib[...])
    x2_ref[...] = x2
    h2_ref[...] = (x2 * inv_rms(x2) * gain_ref[0:1, 1024:2048]).astype(BF)


def pack_ffn_kernel(rank, gate, up, down, out):
    at = rank[0] * 48
    q = jnp.minimum(at // RUN, 1)
    for a, w in ((0, gate), (384, up)):
        pieces = []
        for f in range(8):
            window = w[:, pl.ds(pl.multiple_of(f * 384 + q * RUN, RUN), 256)].astype(F32)
            pieces.append(pltpu.roll(window, (256 - (at - q * RUN)) % 256, 1)[:, :48])
        out[:RUN, a : a + 384] = jnp.concatenate(pieces, axis=1).astype(BF)
    rows = down[pl.ds(pl.multiple_of(at, 16), 48), :]
    out[128:176, :] = rows[:, :768]
    for n in range(3):
        out[176:192, rows_of(n, 256)] = rows[16 * n : 16 * n + 16, 768:]


def copy_kernel(a, out):
    out[...] = a[...]


def join_kernel(a, b, c, d, out):
    for i, part in enumerate((a, b, c, d)):
        out[rows_of(i, RUN), :] = part[...]


def pair_kernel(rank, a, b, out, rank_out):
    out[0] = a[...]
    out[1] = b[...]
    rank_out[...] = jnp.full(rank_out.shape, rank[0], jnp.int32)


def assemble_out_kernel(info, p0, p1, p2, p3, w_ref):
    for k, part in enumerate((p0, p1, p2, p3)):
        for j in range(2):
            w_ref[ds(info[FOF + 4 * j + k] * HEAD, HEAD), :] = part[j]


def assemble_kernel(info, p0, p1, p2, p3, wgu, wd):
    for k, part in enumerate((p0, p1, p2, p3)):
        for j in range(2):
            f = info[FOF + 4 * j + k]
            wgu[ds(f * RUN, RUN), :] = part[j, :RUN, :]
            wd[pl.ds(pl.multiple_of(f * 48, 16), 48), :768] = part[j, 128:176, :]
            for n in range(3):
                wd[ds(f * 48 + 16 * n, 16), 768:] = part[j, 176:192, rows_of(n, 256)]


def blocks_of(info, dy_ref, first, count):
    return jnp.concatenate([dy_ref[ds(info[TOF + first + n] * RUN, RUN), :] for n in range(count)], axis=0)


def ffn_kernel(base, info, h2_ref, dy_ref, wgu, wd, act_ref, dgu_ref, part_ref):
    for i in range(2):
        here = rows_of(i, 256)
        gu = dot(h2_ref[here, :], wgu[...])
        gate, up = gu[:, :384], gu[:, 384:]
        sg = 1.0 / (1.0 + jnp.exp(-gate))
        silu = gate * sg
        act_ref[here, :] = (silu * up).astype(BF)
        d_act = dot_nt(blocks_of(info, dy_ref, base + 2 * i, 2), wd[...])
        d_gate = (d_act * up * (sg * (1.0 + gate * (1.0 - sg)))).astype(BF)
        d_gu = jnp.concatenate([d_gate, (d_act * silu).astype(BF)], axis=1)
        dgu_ref[here, :] = d_gu
        part_ref[here, :] = dot_nt(d_gu, wgu[...]).astype(BF)


def ffn_grad_kernel(info, h2_own, h2_sib, dy_ref, act_own, act_sib, dgu_own, dgu_sib, wd, g_ref, y_own, y_sib):
    y_own[...] = dot(act_own[...], wd[...]).astype(BF)
    y_sib[...] = dot(act_sib[...], wd[...]).astype(BF)
    for a in range(4):
        cols = rows_of(a, 256)
        g = (dot_tn(h2_own[:, cols], dgu_own[...]) + dot_tn(h2_sib[:, cols], dgu_sib[...])).astype(BF)
        g_ref[2 * a, :RUN, :] = g[:RUN]
        g_ref[2 * a + 1, :RUN, :] = g[RUN:]
    g = dot_tn(act_own[...], blocks_of(info, dy_ref, 0, 4)) + dot_tn(act_sib[...], blocks_of(info, dy_ref, 4, 4))
    g = g.astype(BF)
    for f in range(8):
        rows = g[f * 48 : (f + 1) * 48]
        g_ref[f, 128:176, :] = rows[:, :768]
        for n in range(3):
            g_ref[f, 176:192, rows_of(n, 256)] = rows[16 * n : 16 * n + 16, 768:]


def middle_kernel(
    info, p0, p1, p2, p3, x2_ref, dy_ref, gain_ref, w_own, w_sib, dx2_ref, low_ref, gsum_ref, do_own, do_other, do
):
    grad = sum(p[...].astype(F32) for p in (p0, p1, p2, p3))
    pulled, by_gain = norm_pull(x2_ref[...], gain_ref[0:1, 1024:2048], grad)
    gsum_ref[...] = jnp.sum(by_gain, axis=0, keepdims=True)
    dx2 = dy_ref[...].astype(F32) + pulled
    dx2_ref[...] = dx2
    low = dx2.astype(BF)
    low_ref[...] = low
    do[:, :1024] = dot_nt(low, w_own[...]).astype(BF)
    do[:, 1024:] = dot_nt(low, w_sib[...]).astype(BF)
    core = info[CORE]
    for j, out in enumerate((do_own, do_other)):
        for k in range(4):
            at = info[TOF + 4 * j + k] * HEAD
            out[k, :, ds(core * HEAD, HEAD)] = do[:, ds(at, HEAD)]
            out[k, :, ds((1 - core) * HEAD, HEAD)] = do[:, ds(1024 + at, HEAD)]


def out_grad_kernel(info, o_ref, d_ref, own_ref, other_ref, g_all):
    core = info[CORE]
    for a in range(8):
        g_all[...] = dot_tn(o_ref[:, rows_of(a, 256)], d_ref[...]).astype(BF)
        for n in range(2):
            f, half = (2 * a + n) % 8, core if a < 4 else 1 - core
            rows = ds((2 * f + half) * HEAD, HEAD)
            for k in range(4):
                own_ref[k, rows, :] = g_all[rows_of(n, HEAD), ds(info[TOF + k] * RUN, RUN)]
                other_ref[k, rows, :] = g_all[rows_of(n, HEAD), ds(info[TOF + 4 + k] * RUN, RUN)]


def backward_run(b, ref_b, q_ref, o_ref, lse_ref, do):
    rows = ds(b * RUN, RUN)
    q = stacked(q_ref[rows, :])
    do = stacked(do)
    delta = jnp.sum((do.astype(F32) * stacked(o_ref[rows, :])).T, axis=0, keepdims=True)
    return q, do, delta, lse_ref[ref_b]


def backward_other_kernel(bias, q_ref, kv, o_ref, lse_ref, d0, d1, d2, d3, dq_ref, dkv_ref, dk, dv):
    for i in range(8):
        q, do, delta, lse = backward_run(i, i, q_ref, o_ref, lse_ref, (d0, d3, d2, d1)[i % 4][i // 4])
        scores = dot_nt(kv[:, :HEAD], q) * (SCALE * LOG2E)
        p = jnp.concatenate([jnp.exp2(scores[rows_of(b, RUN)] - (lse - bias[i, b])) for b in range(8)], axis=0)
        d_s = (p * (dot_nt(kv[:, HEAD:], do) - delta)).astype(BF)
        by_v, by_k = dot(p.astype(BF), do), dot(d_s, q)
        dv[...] = by_v if i == 0 else dv[...] + by_v
        dk[...] = by_k if i == 0 else dk[...] + by_k
        dq_ref[i] = dot_tn(d_s, kv[:, :HEAD])
    dkv_ref[:, :HEAD] = (dk[...] * SCALE).astype(BF)
    dkv_ref[:, HEAD:] = dv[...].astype(BF)


def backward_own_kernel(
    info, pos_ref, q_ref, kv, o_ref, lse_ref, d0, d1, d2, d3, before, dq_ref, dkv_ref, ks, vs, dk, dv, dos
):
    for s in range(8):
        src = ds(info[SORTED + s] * RUN, RUN)
        ks[rows_of(s, RUN), :] = kv[src, :HEAD]
        vs[rows_of(s, RUN), :] = kv[src, HEAD:]
        dos[s] = (d0, d3, d2, d1)[s % 4][s // 4]
    dk[...] = jnp.zeros_like(dk)
    dv[...] = jnp.zeros_like(dv)
    for s in range(8):
        b = info[SORTED + s]
        q, do, delta, lse = backward_run(b, b, q_ref, o_ref, lse_ref, dos[b])
        keys = ks[: (s + 1) * RUN, :]
        p = jnp.exp2(dot_nt(keys, q) * (SCALE * LOG2E) - lse)
        diagonal = jnp.where(own_mask(pos_ref, b), p[s * RUN :], 0.0)
        p = jnp.concatenate([p[: s * RUN], diagonal], axis=0) if s else diagonal
        d_s = (p * (dot_nt(vs[: (s + 1) * RUN, :], do) - delta)).astype(BF)
        dv[: (s + 1) * RUN, :] += dot(p.astype(BF), do)
        dk[: (s + 1) * RUN, :] += dot(d_s, q)
        dq = (dot_tn(d_s, keys) + before[b]) * SCALE
        dq_ref[ds(b * RUN, RUN), :HEAD] = dq[:RUN]
        dq_ref[ds(b * RUN, RUN), HEAD:] = dq[RUN:]
    for s in range(8):
        src = ds(info[SORTED + s] * RUN, RUN)
        dkv_ref[src, :HEAD] = dk[rows_of(s, RUN), :] * SCALE
        dkv_ref[src, HEAD:] = dv[rows_of(s, RUN), :]


def head_back(raw, gain, grad, cos, sin):
    grad = grad * cos + pltpu.roll(grad * sin, HEAD // 2, 1)
    pulled, by_gain = norm_pull(raw, gain, grad)
    return pulled.astype(BF), jnp.sum(by_gain, axis=0, keepdims=True)


def query_back_kernel(info, h_ref, gain_ref, cos, sin, raw, dq_ref, low_ref, g_ref, sum_ref):
    sum_ref[...] = jnp.zeros_like(sum_ref)
    for i in range(4):
        here = rows_of(i, 256)
        for a in range(2):
            cols = rows_of(a, HEAD)
            low, by_gain = head_back(raw[here, cols], gain_ref[0:1, 2048:2176], dq_ref[here, cols], cos[here, :], sin[here, :])
            low_ref[here, cols] = low
            sum_ref[...] += by_gain
    for k in range(4):
        for j in range(2):
            f = info[FOF + 4 * j + (4 - k) % 4]
            g_ref[k, j] = dot_tn(h_ref[:, ds(f * RUN, RUN)], low_ref[...])


def key_value_back_kernel(
    info, h_ref, w_ref, gain_ref, cos, sin, raw, dkv_ref, recv, gq_ref, qsum, ffn_ref,
    out0, out1, out2, out3, dq_ref, y_own, y_sib, g0, g1, g2, g3, own_ref, sib_ref, low_ref,
):
    sums = jnp.zeros((1, HEAD), F32)
    for i in range(4):
        here = rows_of(i, 256)
        dkv = dkv_ref[here, :] + recv[here, :].astype(F32)
        low, by_gain = head_back(raw[here, :], gain_ref[0:1, 2176:2304], dkv[:, :HEAD], cos[here, :], sin[here, :])
        low_ref[here, :HEAD] = low
        low_ref[here, HEAD:] = dkv[:, HEAD:].astype(BF)
        sums += by_gain
    lane = lax.broadcasted_iota(jnp.int32, (8, HEAD), 1)
    heads = [jnp.broadcast_to(s, (8, HEAD)) for s in (qsum[...], sums)]
    for k, g_ref in enumerate((g0, g1, g2, g3)):
        for j in range(2):
            f = info[FOF + 4 * j + (4 - k) % 4]
            here = ds(f * RUN, RUN)
            gkv = dot_tn(h_ref[:, here], low_ref[...])
            gq = gq_ref[k, j]
            g_ref[j, :RUN, :256] = gq.astype(BF)
            g_ref[j, :RUN, 256:] = gkv.astype(BF)
            by_attn = jnp.sum(gq * w_ref[here, :256].astype(F32) + gkv * w_ref[here, 256:].astype(F32), axis=1, keepdims=True)
            by_attn = jnp.broadcast_to(by_attn, (RUN, RUN)).T[:8] / gain_ref[:, here]
            rows = [by_attn, jnp.broadcast_to(ffn_ref[0:1, here], (8, RUN))]
            rows += [jnp.where(lane < 16, pltpu.roll(r, HEAD - 16 * f, 1), 0.0) for r in heads]
            rows = jnp.concatenate(rows, axis=1)
            g_ref[j, RUN : RUN + 16, :] = jnp.concatenate([rows, rows], axis=0).astype(BF)
            for n in range(4):
                src = ds(f * 256 + n * 64, 64)
                rows = sum(o[src, :].astype(F32) for o in (out0, out1, out2, out3))
                g_ref[j, RUN + 16 :, rows_of(n, RUN)] = rows.astype(BF)
    for i in range(4):
        here = rows_of(i, 256)
        part = dot_nt(dq_ref[here, :], w_ref[:, :256]) + dot_nt(low_ref[here, :], w_ref[:, 256:])
        part = part.astype(BF)
        out, y_ref = ((own_ref, y_own), (sib_ref, y_sib))[i // 2]
        for n in range(2):
            k = 2 * (i % 2) + n
            out[rows_of(2 * k, RUN), :] = part[rows_of(n, RUN)]
            out[rows_of(2 * k + 1, RUN), :] = y_ref[rows_of(k, RUN), :]


def last_kernel(p0, p1, p2, p3, x_ref, x2_ref, dx2_ref, gain_ref, out_ref, grad_ref):
    sums = sum(p[...].astype(F32) for p in (p0, p1, p2, p3))
    out_ref[...] = (x2_ref[...] + sums[RUN:]).astype(BF)
    grad_ref[...] = dx2_ref[...] + norm_pull(x_ref[...].astype(F32), gain_ref[0:1, :1024], sums[:RUN])[0]


def unpack_kernel(info, own, sib, g_ref, out_ref, gain_ref):
    gain_ref[...] = jnp.zeros_like(gain_ref)
    for j, part in enumerate((own, sib)):
        for k in range(4):
            t = info[TOF + 4 * j + k]
            g_ref[:, ds(t * 256, 256)] = part[k, :RUN, :256].astype(F32)
            g_ref[:, ds(2048 + t * RUN, RUN)] = part[k, :RUN, 256:384].astype(F32)
            g_ref[:, ds(3072 + t * RUN, RUN)] = part[k, :RUN, 384:].astype(F32)
            gain_ref[...] += part[k, RUN : RUN + 16, :].astype(F32)[:8]
            for n in range(4):
                out_ref[rows_of(n, 64), ds(t * RUN, RUN)] = part[k, RUN + 16 :, rows_of(n, RUN)].astype(F32)


def z_sum_kernel(g0, g1, g2, g3, mine, theirs):
    for j, out in enumerate((mine, theirs)):
        out[...] = sum(p[j].astype(F32) for p in (g0, g1, g2, g3)).astype(BF)


def add_kernel(a, b, out):
    for i in range(8):
        here = rows_of(i, a.shape[0] // 8)
        out[here, :] = (a[here, :].astype(F32) + b[here, :].astype(F32)).astype(BF)


def sum_kernel(a, b, c, d, out):
    out[...] = (a[...].astype(F32) + b[...].astype(F32) + c[...].astype(F32) + d[...].astype(F32)).astype(BF)


def unpack_ffn_kernel(wide, gate, up, down):
    for a, out in ((0, gate), (384, up)):
        for f in range(8):
            pieces = [wide[t, :RUN, a + f * 48 : a + f * 48 + 48].astype(F32) for t in range(8)]
            out[:, f * 384 : (f + 1) * 384] = jnp.concatenate(pieces, axis=1)
    for t in range(8):
        down[t * 48 : (t + 1) * 48, :768] = wide[t, 128:176, :].astype(F32)
        for n in range(3):
            at = t * 48 + 16 * n
            down[at : at + 16, 768:] = wide[t, 176:192, rows_of(n, 256)].astype(F32)


def call(kernel, outs, scratch, micros, *args, info=None, deps=()):
    smem = [] if info is None else [info]
    first, late = len(smem) + len(args), len(smem) + len(args) + len(deps)
    return pl.pallas_call(
        lambda *refs: kernel(*refs[:first], *refs[late:]),
        name=getattr(kernel, "func", kernel).__name__,
        out_shape=[jax.ShapeDtypeStruct(*o) for o in outs],
        in_specs=[pl.BlockSpec(memory_space=pltpu.SMEM)] * len(smem)
        + [pl.BlockSpec(memory_space=pltpu.VMEM)] * len(args)
        + [pl.BlockSpec(memory_space=pl.ANY)] * len(deps),
        out_specs=[pl.BlockSpec(memory_space=pltpu.VMEM)] * len(outs),
        scratch_shapes=[pltpu.VMEM(*s) for s in scratch],
        compiler_params=pltpu.CompilerParams(vmem_limit_bytes=16 * 2**20),
        cost_estimate=pl.CostEstimate(flops=int(micros * 3e8), bytes_accessed=2**12, transcendentals=0),
    )(*smem, *args, *deps)


def shards(
    tokens, positions, w_qkv, w_out, w_gate, w_up, w_down, attn_gain, ffn_gain, q_gain, k_gain, cotangent
):
    xhi, y, core = (lax.axis_index(a) for a in CTX)
    xlo, z = (lax.axis_index(a) for a in FSDP)
    t = y * 2 + core
    x_own, dy = tokens[0], cotangent[0]

    wqs = [pl.BlockSpec((RUN, n), lambda i, at, first=first: (0, first + at[0])) for n, first in ((256, 0), (128, 16), (128, 24))]
    small = [g[None] for g in (attn_gain, ffn_gain, q_gain, k_gain)]
    slice_qkv = pl.pallas_call(
        pack_kernel,
        out_shape=jax.ShapeDtypeStruct((RUN + 16, 512), BF),
        grid_spec=pltpu.PrefetchScalarGridSpec(
            num_scalar_prefetch=1,
            grid=(1,),
            in_specs=wqs + [pl.BlockSpec(g.shape, lambda i, at: (0, 0)) for g in small],
            out_specs=pl.BlockSpec((RUN + 16, 512), lambda i, at: (0, 0)),
        ),
    )(t[None].astype(jnp.int32), w_qkv, w_qkv, w_qkv, *small)
    xs = gather_tokens(x_own)
    here = t[None].astype(jnp.int32)
    later = ((8, RUN), jnp.int32)
    pair_qkv, later_t = call(
        pair_kernel, [((2, RUN + 16, 512), BF), later], [], 1, slice_qkv, shift(slice_qkv, "xlo", 1), info=here
    )
    parts_qkv = spread_z(pair_qkv)
    later_t = later_t[0, 0]
    eight = jnp.arange(8, dtype=jnp.int32)
    block = lax.rem(y - eight % 4 + 4, 4) * 2 + (core ^ (eight // 4))
    f_of = (xlo ^ (eight // 4)) * 4 + lax.rem(z - eight % 4 + 4, 4)
    blocks = jnp.concatenate([xhi * 8 + block, (1 - xhi) * 8 + block])
    pos = (positions[0] + later_t // 8).reshape(16, RUN)[blocks]
    rank = pos[:, 0] // RUN
    place = jnp.sum(rank[:8, None] > rank[None, :8], axis=1)
    in_order = jnp.argmax(place[None, :] == eight[:, None], axis=1)
    info = jnp.concatenate([in_order, f_of, block, core[None]]).astype(jnp.int32)
    bias = jnp.where(rank[:8, None] > rank[None, 8:], 0.0, MASKED)
    pos_rows = pos.astype(F32).reshape(16, 1, RUN)
    inverse = THETA ** (-(jnp.arange(HEAD // 2, dtype=F32) * 2.0 / HEAD))
    angles = pos[:8].reshape(1024).astype(F32)[:, None] * inverse[None, :]
    cosine, sine = jnp.cos(angles), jnp.sin(angles)
    cosine = jnp.concatenate([cosine, cosine], axis=1)
    sine = jnp.concatenate([-sine, sine], axis=1)

    (slice_ffn,) = call(
        pack_ffn_kernel, [((192, 768), BF)], [], 3, w_gate, w_up, w_down, info=here, deps=[pair_qkv]
    )
    received = shift(slice_ffn, "xlo", 1)
    half_out = lax.dynamic_slice_in_dim(w_out, core * HEAD, HEAD, 0)
    pair_out, _ = call(
        pair_kernel,
        [((2, RUN, 1024), BF), later],
        [],
        1,
        half_out, shift(half_out, "xlo", 1),
        info=here,
        deps=[received] + parts_qkv[1:],
    )
    parts_out = spread_z(pair_out)

    h, wqkv, gain, kraw, kv, dy_later = call(
        key_value_kernel,
        [((1024, 1024), BF), ((1024, 512), BF), ((8, 2304), F32), ((1024, HEAD), F32), ((1024, 256), BF), ((RUN, 1024), BF)],
        [],
        5,
        *xs, *parts_qkv, cosine, sine, dy,
        info=info,
        deps=[pair_out],
    )
    kv_other = shift(kv, "xhi", 1)
    qraw, q = call(query_kernel, [((1024, 256), F32), ((1024, 256), BF)], [], 3, h, wqkv, gain, cosine, sine)
    (partial,) = call(
        forward_own_kernel,
        [((8, HEAD + 8, 256), F32)],
        [((1024, HEAD), BF), ((256, 1024), BF)],
        5,
        pos_rows, q, kv,
        info=info,
    )
    dy_all = lax.all_gather(dy_later, TP, axis=0, tiled=True)
    o32, lse, o_low = call(
        forward_other_kernel,
        [((1024, 256), F32), ((8, 1, 256), F32), ((2, 4, RUN, 256), BF)],
        [((256, 1024), BF)],
        6,
        q, kv_other, partial,
        info=bias,
        deps=[parts_out[1], parts_out[3]],
    )
    parts_o = exchange(o_low[0], o_low[1])
    (wout_own,) = call(assemble_out_kernel, [((1024, 1024), BF)], [], 1, *parts_out, info=info, deps=[o_low])
    wout_sib = shift(wout_own, "core", 1)
    pair_ffn, _ = call(
        pair_kernel,
        [((2, 192, 768), BF), later],
        [],
        1,
        slice_ffn, received,
        info=here,
        deps=parts_o[1:],
    )
    parts_ffn = spread_z(pair_ffn)
    x2, h2_own, o_all = call(
        out_kernel,
        [((RUN, 1024), F32), ((RUN, 1024), BF), ((RUN, 2048), BF)],
        [],
        4,
        x_own, *parts_o, wout_own, wout_sib, gain,
        info=info,
    )
    wgu, wd = call(assemble_kernel, [((1024, 768), BF), ((384, 1024), BF)], [], 2, *parts_ffn, info=info)

    h2_parts = [h2_own] + [shift(h2_own, "y", k) for k in (1, 2, 3)]
    (h2_join,) = call(join_kernel, [((512, 1024), BF)], [], 1, *h2_parts, deps=[wgu])
    h2 = h2_join, shift(h2_join, "core", 1)
    ffn = [
        call(
            functools.partial(ffn_kernel, 4 * j),
            [((512, 384), BF), ((512, 768), BF), ((512, 1024), BF)],
            [],
            6,
            h2[j], dy_all, wgu, wd,
            info=info,
        )
        for j in (1, 0)
    ]
    (act_sib, dgu_sib, part_sib), (act_own, dgu_own, part_own) = ffn
    d_h2 = scatter_tokens(part_own, part_sib)
    g_ffn, y_own, y_sib = call(
        ffn_grad_kernel,
        [((8, 192, 768), BF), ((512, 1024), BF), ((512, 1024), BF)],
        [],
        8,
        *h2, dy_all, act_own, act_sib, dgu_own, dgu_sib, wd,
        info=info,
    )
    d_x2, d_branch, ffn_sum, do_own, do_other = call(
        middle_kernel,
        [((RUN, 1024), F32), ((RUN, 1024), BF), ((1, 1024), F32), ((4, RUN, 256), BF), ((4, RUN, 256), BF)],
        [((RUN, 2048), BF)],
        0,
        *d_h2, x2, dy, gain, wout_own, wout_sib,
        info=info,
        deps=[g_ffn],
    )
    d_o = exchange(do_own, do_other)
    g_out_own, g_out_other = call(
        out_grad_kernel, [((4, 2048, RUN), BF)] * 2, [((256, 1024), BF)], 0, o_all, d_branch, info=info
    )

    rows_ffn = lax.psum_scatter(g_ffn, FSDP, scatter_dimension=0, tiled=False)
    (blocks_out,) = call(
        add_kernel,
        [((4 * 2048, RUN), BF)],
        [],
        0,
        g_out_own.reshape(-1, RUN), shift(g_out_other, "core", 1).reshape(-1, RUN),
    )
    blocks_out = blocks_out.reshape(4, 2048, RUN)
    out_parts = [blocks_out[0]] + [shift(blocks_out[k], "y", 4 - k) for k in (1, 2, 3)]

    d_q, d_other = call(
        backward_other_kernel,
        [((8, 256, HEAD), F32), ((1024, 256), BF)],
        [((1024, HEAD), F32), ((1024, HEAD), F32)],
        0,
        q, kv_other, o32, lse, *d_o,
        info=bias,
        deps=[blocks_out],
    )
    recv = shift(d_other, "xhi", 1)
    d_q, d_kv = call(
        backward_own_kernel,
        [((1024, 256), F32), ((1024, 256), F32)],
        [((1024, HEAD), BF), ((1024, HEAD), BF), ((1024, HEAD), F32), ((1024, HEAD), F32), ((8, RUN, 256), BF)],
        8,
        pos_rows, q, kv, o32, lse, *d_o, d_q,
        info=info,
    )
    dq_low, g_q, q_sum = call(
        query_back_kernel,
        [((1024, 256), BF), ((4, 2, RUN, 256), F32), ((1, HEAD), F32)],
        [],
        5,
        h, gain, cosine, sine, qraw, d_q,
        info=info,
    )
    (rows_later,) = call(copy_kernel, [((192, 768), BF)], [], 1, rows_ffn, deps=[dq_low, recv] + out_parts[1:])
    half_ffn = (rows_later.astype(F32) + shift(rows_later, "xhi", 1).astype(F32)).astype(BF)
    *g_qkv, part_own, part_sib = call(
        key_value_back_kernel,
        [((2, 208, 512), BF)] * 4 + [((1024, 1024), BF)] * 2,
        [((1024, 256), BF)],
        8,
        h, wqkv, gain, cosine, sine, kraw, d_kv, recv, g_q, q_sum, ffn_sum, *out_parts, dq_low, y_own, y_sib,
        info=info,
    )
    g_qkv = [g_qkv[0]] + [shift(g_qkv[k], "z", k) for k in (1, 2, 3)]
    (d_h,) = call(add_kernel, [((1024, 1024), BF)], [], 1, part_own, shift(part_sib, "core", 1))
    sum_ffn = lax.all_gather(half_ffn, TP, axis=0)
    sum_gate, sum_up, sum_down = call(
        unpack_ffn_kernel, [((128, 3072), F32), ((128, 3072), F32), ((384, 1024), F32)], [], 4, sum_ffn
    )
    mine, theirs = call(z_sum_kernel, [((208, 512), BF)] * 2, [], 1, *g_qkv, deps=[d_h])
    d_h = d_h.reshape(4, 256, 1024)
    d_h = [d_h[0]] + [shift(d_h[k], "y", 4 - k) for k in (1, 2, 3)]
    cross = lax.ppermute(theirs, ("xlo", "xhi"), [(i, i ^ 3) for i in range(4)])
    (total,) = call(
        sum_kernel, [((208, 512), BF)], [], 1, mine, shift(theirs, "xlo", 1), shift(mine, "xhi", 1), cross, deps=[sum_gate] + d_h[1:]
    )
    own = jnp.stack([total] + [shift(total, "y", k) for k in (1, 2, 3)])
    sum_qkv, sum_out, sum_gains = call(
        unpack_kernel,
        [((128, 4096), F32), ((256, 1024), F32), ((8, 512), F32)],
        [],
        3,
        own, shift(own, "core", 1),
        info=info,
    )
    output, input_grad = call(
        last_kernel, [((RUN, 1024), BF), ((RUN, 1024), F32)], [], 2, *d_h, x_own, x2, d_x2, gain
    )
    return (
        output[None],
        input_grad[None],
        sum_qkv,
        sum_out,
        sum_gate,
        sum_up,
        sum_down,
        sum_gains[0, :128],
        sum_gains[0, 128:256],
        sum_gains[0, 256:272],
        sum_gains[0, 384:400],
    )


def solution(mesh):
    split = Mesh(mesh.devices.reshape(tuple(SIZES.values())), FSDP + CTX)
    rows, both = P(FSDP, None), P(FSDP, CTX, None)
    return jax.shard_map(
        shards,
        mesh=split,
        in_specs=(both,) + (rows,) * 6 + (P(FSDP),) * 4 + (both,),
        out_specs=(both, both) + (rows,) * 5 + (P(FSDP),) * 4,
        check_vma=False,
    )
```

```python
import functools

import jax
import jax.numpy as jnp
from jax import lax
from jax.experimental import pallas as pl
from jax.experimental.pallas import tpu as pltpu
from jax.sharding import Mesh
from jax.sharding import PartitionSpec as P

HEAD = 128
EPS = 1e-06
MASKED = -1e30
THETA = 1000000.0
SCALE = HEAD**-0.5
LOG2E = 1.4426950408889634
RUN = 128
FSDP = ("xlo", "z")
CTX = ("xhi", "y", "core")
TP = ("y", "core")
SIZES = {"xlo": 2, "z": 4, "xhi": 2, "y": 4, "core": 2}
BF = jnp.bfloat16
F32 = jnp.float32
TOKEN = ((8, 128), jnp.float32)
SORTED, FOF, TOF, CORE = 0, 8, 16, 24


def shift(x, axis, step):
    n = SIZES[axis]
    return lax.ppermute(x, axis, [(i, (i + step) % n) for i in range(n)])


def gather_tokens(x):
    own = jnp.concatenate([x] + [shift(x, "y", k) for k in (1, 2, 3)], axis=0)
    return own, shift(own, "core", 1)


def scatter_tokens(own, other):
    blocks = (own.astype(F32) + shift(other, "core", 1).astype(F32)).astype(BF).reshape(4, own.shape[0] // 4, -1)
    return [blocks[0]] + [shift(blocks[k], "y", 4 - k) for k in (1, 2, 3)]


def exchange(own, other):
    both = jnp.stack([own, shift(other, "core", 1)], axis=1)
    return [both[0]] + [shift(both[k], "y", 4 - k) for k in (1, 2, 3)]


def spread_z(pair):
    return [pair] + [shift(pair, "z", k) for k in (1, 2, 3)]


def dot(a, b):
    return jnp.dot(a, b, preferred_element_type=F32)


def dot_nt(a, b):
    return lax.dot_general(a, b, (((1,), (1,)), ((), ())), preferred_element_type=F32)


def dot_tn(a, b):
    return lax.dot_general(a, b, (((0,), (0,)), ((), ())), preferred_element_type=F32)


def inv_rms(x):
    return lax.rsqrt(jnp.mean(x * x, axis=-1, keepdims=True) + EPS)


def norm_pull(x, gain, grad):
    inv = inv_rms(x)
    hat = x * inv
    scaled = grad * gain
    return inv * (scaled - hat * jnp.mean(scaled * hat, axis=-1, keepdims=True)), grad * hat


def ds(at, size):
    return pl.ds(pl.multiple_of(at, size), size)


def rows_of(i, size):
    return slice(i * size, (i + 1) * size)


def pack_kernel(at, q_ref, k_ref, v_ref, attn, ffn, qg, kg, out):
    out[:RUN, :256] = q_ref[...]
    out[:RUN, 256:384] = k_ref[...]
    out[:RUN, 384:] = v_ref[...]
    none = jnp.zeros((16, 112), BF)
    rows = [jnp.broadcast_to(g[...], (16, g.shape[1])) for g in (attn, ffn, qg, kg)]
    out[RUN:, :128] = rows[0]
    out[RUN:, 128:256] = rows[1]
    out[RUN:, 256:384] = jnp.concatenate([rows[2], none], axis=1)
    out[RUN:, 384:] = jnp.concatenate([rows[3], none], axis=1)


def key_value_kernel(info, own, sib, w0, w1, w2, w3, cos, sin, dy, h_ref, w_ref, gain_ref, raw_ref, kv_ref, dy_ref):
    dy_ref[...] = dy[...]
    gain_ref[...] = jnp.zeros_like(gain_ref)
    for k, part in enumerate((w0, w1, w2, w3)):
        for j in range(2):
            f = info[FOF + 4 * j + k]
            w_ref[ds(f * RUN, RUN), :] = part[j, :RUN, :]
            row = part[j, RUN:, :].astype(F32)[:8]
            gain_ref[:, ds(f * RUN, RUN)] = row[:, :128]
            gain_ref[:, ds(1024 + f * RUN, RUN)] = row[:, 128:256]
            gain_ref[:, 2048:2176] += pltpu.roll(row[:, 256:384], f * 16, 1)
            gain_ref[:, 2176:2304] += pltpu.roll(row[:, 384:512], f * 16, 1)
    attn_gain, k_gain = gain_ref[0:1, :1024], gain_ref[0:1, 2176:2304]
    for i in range(4):
        part = (own, sib)[i // 2]
        here = rows_of(i, 256)
        x = part[rows_of(i % 2, 256), :].astype(F32)
        h = (x * inv_rms(x) * attn_gain).astype(BF)
        h_ref[here, :] = h
        raw = dot(h, w_ref[:, 256:])
        raw_ref[here, :] = raw[:, :HEAD]
        key = raw[:, :HEAD]
        key = key * inv_rms(key) * k_gain
        key = key * cos[here, :] + pltpu.roll(key, HEAD // 2, 1) * sin[here, :]
        kv_ref[here, :HEAD] = key.astype(BF)
        kv_ref[here, HEAD:] = raw[:, HEAD:].astype(BF)


def query_kernel(h_ref, w_ref, gain_ref, cos, sin, raw_ref, q_ref):
    gain = gain_ref[0:1, 2048:2176]
    for i in range(4):
        here = rows_of(i, 256)
        raw = dot(h_ref[here, :], w_ref[:, :256])
        raw_ref[here, :] = raw
        for a in range(2):
            u = raw[:, rows_of(a, HEAD)]
            u = u * inv_rms(u) * gain
            u = u * cos[here, :] + pltpu.roll(u, HEAD // 2, 1) * sin[here, :]
            q_ref[here, rows_of(a, HEAD)] = u.astype(BF)


def stacked(rows):
    return jnp.concatenate([rows[:, :HEAD], rows[:, HEAD:]], axis=0)


def own_mask(pos_ref, b):
    row = pos_ref[b]
    keys = jnp.broadcast_to(row, (RUN, RUN)).T
    return jnp.concatenate([keys, keys], axis=1) <= jnp.concatenate([row, row], axis=1)


def expo(keys, q):
    return jnp.exp2(dot_nt(keys, q) * (SCALE * LOG2E))


def forward_own_kernel(info, pos_ref, q_ref, kv, part_ref, ks, vt):
    vt[HEAD:, :] = jnp.ones((HEAD, vt.shape[1]), BF)
    for s in range(8):
        src = ds(info[SORTED + s] * RUN, RUN)
        ks[rows_of(s, RUN), :] = kv[src, :HEAD]
        vt[:HEAD, rows_of(s, RUN)] = kv[src, HEAD:].T
    for s in range(8):
        b = info[SORTED + s]
        q = stacked(q_ref[ds(b * RUN, RUN), :])
        e = jnp.where(own_mask(pos_ref, b), expo(ks[rows_of(s, RUN), :], q), 0.0)
        acc = dot(vt[:, rows_of(s, RUN)], e.astype(BF))
        if s:
            acc += dot(vt[:, : s * RUN], expo(ks[: s * RUN, :], q).astype(BF))
        part_ref[b] = acc[: HEAD + 8]


def forward_other_kernel(bias, q_ref, kv, part_ref, o_ref, lse_ref, low_ref, vt):
    vt[HEAD:, :] = jnp.ones((HEAD, vt.shape[1]), BF)
    vt[:HEAD, :] = kv[:, HEAD:].T
    for i in range(8):
        q = stacked(q_ref[rows_of(i, RUN), :])
        scores = dot_nt(kv[:, :HEAD], q) * (SCALE * LOG2E)
        e = jnp.concatenate([jnp.exp2(scores[rows_of(b, RUN)] + bias[i, b]).astype(BF) for b in range(8)], axis=0)
        acc = dot(vt[...], e)
        total = acc[HEAD : HEAD + 1, :] + part_ref[i, HEAD : HEAD + 1, :]
        out = ((acc[:HEAD, :] + part_ref[i, :HEAD, :]) / total).T
        out = jnp.concatenate([out[:RUN], out[RUN:]], axis=1)
        o_ref[rows_of(i, RUN), :] = out
        low_ref[i // 4, i % 4] = out.astype(BF)
        lse_ref[i] = jnp.log2(total)


def out_kernel(info, x_ref, o0, o1, o2, o3, w_own, w_sib, gain_ref, x2_ref, h2_ref, oall_ref):
    core = info[CORE]
    for k, part in enumerate((o0, o1, o2, o3)):
        for j in range(2):
            at = info[TOF + 4 * j + (4 - k) % 4] * HEAD
            oall_ref[:, ds(at, HEAD)] = part[j, :, ds(core * HEAD, HEAD)]
            oall_ref[:, ds(1024 + at, HEAD)] = part[j, :, ds((1 - core) * HEAD, HEAD)]
    x2 = x_ref[...].astype(F32) + dot(oall_ref[:, :1024], w_own[...]) + dot(oall_ref[:, 1024:], w_sib[...])
    x2_ref[...] = x2
    h2_ref[...] = (x2 * inv_rms(x2) * gain_ref[0:1, 1024:2048]).astype(BF)


def pack_ffn_kernel(rank, gate, up, down, out):
    at = rank[0] * 48
    q = jnp.minimum(at // RUN, 1)
    for a, w in ((0, gate), (384, up)):
        pieces = []
        for f in range(8):
            window = w[:, pl.ds(pl.multiple_of(f * 384 + q * RUN, RUN), 256)].astype(F32)
            pieces.append(pltpu.roll(window, (256 - (at - q * RUN)) % 256, 1)[:, :48])
        out[:RUN, a : a + 384] = jnp.concatenate(pieces, axis=1).astype(BF)
    rows = down[pl.ds(pl.multiple_of(at, 16), 48), :]
    out[128:176, :] = rows[:, :768]
    for n in range(3):
        out[176:192, rows_of(n, 256)] = rows[16 * n : 16 * n + 16, 768:]


def join_kernel(a, b, c, d, out):
    for i, part in enumerate((a, b, c, d)):
        out[rows_of(i, RUN), :] = part[...]


def pair_kernel(rank, a, b, out, rank_out):
    out[0] = a[...]
    out[1] = b[...]
    rank_out[...] = jnp.full(rank_out.shape, rank[0], jnp.int32)


def assemble_out_kernel(info, p0, p1, p2, p3, w_ref):
    for k, part in enumerate((p0, p1, p2, p3)):
        for j in range(2):
            w_ref[ds(info[FOF + 4 * j + k] * HEAD, HEAD), :] = part[j]


def assemble_kernel(info, p0, p1, p2, p3, wgu, wd):
    for k, part in enumerate((p0, p1, p2, p3)):
        for j in range(2):
            f = info[FOF + 4 * j + k]
            wgu[ds(f * RUN, RUN), :] = part[j, :RUN, :]
            wd[pl.ds(pl.multiple_of(f * 48, 16), 48), :768] = part[j, 128:176, :]
            for n in range(3):
                wd[ds(f * 48 + 16 * n, 16), 768:] = part[j, 176:192, rows_of(n, 256)]


def blocks_of(info, dy_ref, first, count):
    return jnp.concatenate([dy_ref[ds(info[TOF + first + n] * RUN, RUN), :] for n in range(count)], axis=0)


def ffn_kernel(base, info, h2_ref, dy_ref, wgu, wd, act_ref, dgu_ref, part_ref):
    for i in range(2):
        here = rows_of(i, 256)
        gu = dot(h2_ref[here, :], wgu[...])
        gate, up = gu[:, :384], gu[:, 384:]
        sg = 1.0 / (1.0 + jnp.exp(-gate))
        silu = gate * sg
        act_ref[here, :] = (silu * up).astype(BF)
        d_act = dot_nt(blocks_of(info, dy_ref, base + 2 * i, 2), wd[...])
        d_gate = (d_act * up * (sg * (1.0 + gate * (1.0 - sg)))).astype(BF)
        d_gu = jnp.concatenate([d_gate, (d_act * silu).astype(BF)], axis=1)
        dgu_ref[here, :] = d_gu
        part_ref[here, :] = dot_nt(d_gu, wgu[...]).astype(BF)


def ffn_grad_kernel(info, h2_own, h2_sib, dy_ref, act_own, act_sib, dgu_own, dgu_sib, wd, g_ref, y_own, y_sib):
    y_own[...] = dot(act_own[...], wd[...]).astype(BF)
    y_sib[...] = dot(act_sib[...], wd[...]).astype(BF)
    for a in range(4):
        cols = rows_of(a, 256)
        g = (dot_tn(h2_own[:, cols], dgu_own[...]) + dot_tn(h2_sib[:, cols], dgu_sib[...])).astype(BF)
        g_ref[2 * a, :RUN, :] = g[:RUN]
        g_ref[2 * a + 1, :RUN, :] = g[RUN:]
    g = dot_tn(act_own[...], blocks_of(info, dy_ref, 0, 4)) + dot_tn(act_sib[...], blocks_of(info, dy_ref, 4, 4))
    g = g.astype(BF)
    for f in range(8):
        rows = g[f * 48 : (f + 1) * 48]
        g_ref[f, 128:176, :] = rows[:, :768]
        for n in range(3):
            g_ref[f, 176:192, rows_of(n, 256)] = rows[16 * n : 16 * n + 16, 768:]


def middle_kernel(
    info, p0, p1, p2, p3, x2_ref, dy_ref, gain_ref, w_own, w_sib, dx2_ref, low_ref, gsum_ref, do_own, do_other, do
):
    grad = sum(p[...].astype(F32) for p in (p0, p1, p2, p3))
    pulled, by_gain = norm_pull(x2_ref[...], gain_ref[0:1, 1024:2048], grad)
    gsum_ref[...] = jnp.sum(by_gain, axis=0, keepdims=True)
    dx2 = dy_ref[...].astype(F32) + pulled
    dx2_ref[...] = dx2
    low = dx2.astype(BF)
    low_ref[...] = low
    do[:, :1024] = dot_nt(low, w_own[...]).astype(BF)
    do[:, 1024:] = dot_nt(low, w_sib[...]).astype(BF)
    core = info[CORE]
    for j, out in enumerate((do_own, do_other)):
        for k in range(4):
            at = info[TOF + 4 * j + k] * HEAD
            out[k, :, ds(core * HEAD, HEAD)] = do[:, ds(at, HEAD)]
            out[k, :, ds((1 - core) * HEAD, HEAD)] = do[:, ds(1024 + at, HEAD)]


def out_grad_kernel(info, o_ref, d_ref, own_ref, other_ref, g_all):
    core = info[CORE]
    for a in range(8):
        g_all[...] = dot_tn(o_ref[:, rows_of(a, 256)], d_ref[...]).astype(BF)
        for n in range(2):
            f, half = (2 * a + n) % 8, core if a < 4 else 1 - core
            rows = ds((2 * f + half) * HEAD, HEAD)
            for k in range(4):
                own_ref[k, rows, :] = g_all[rows_of(n, HEAD), ds(info[TOF + k] * RUN, RUN)]
                other_ref[k, rows, :] = g_all[rows_of(n, HEAD), ds(info[TOF + 4 + k] * RUN, RUN)]


def backward_run(b, ref_b, q_ref, o_ref, lse_ref, do):
    rows = ds(b * RUN, RUN)
    q = stacked(q_ref[rows, :])
    do = stacked(do)
    delta = jnp.sum((do.astype(F32) * stacked(o_ref[rows, :])).T, axis=0, keepdims=True)
    return q, do, delta, lse_ref[ref_b]


def backward_other_kernel(bias, q_ref, kv, o_ref, lse_ref, d0, d1, d2, d3, dq_ref, dkv_ref, dk, dv):
    for i in range(8):
        q, do, delta, lse = backward_run(i, i, q_ref, o_ref, lse_ref, (d0, d3, d2, d1)[i % 4][i // 4])
        scores = dot_nt(kv[:, :HEAD], q) * (SCALE * LOG2E)
        p = jnp.concatenate([jnp.exp2(scores[rows_of(b, RUN)] - (lse - bias[i, b])) for b in range(8)], axis=0)
        d_s = (p * (dot_nt(kv[:, HEAD:], do) - delta)).astype(BF)
        by_v, by_k = dot(p.astype(BF), do), dot(d_s, q)
        dv[...] = by_v if i == 0 else dv[...] + by_v
        dk[...] = by_k if i == 0 else dk[...] + by_k
        dq_ref[i] = dot_tn(d_s, kv[:, :HEAD])
    dkv_ref[:, :HEAD] = (dk[...] * SCALE).astype(BF)
    dkv_ref[:, HEAD:] = dv[...].astype(BF)


def backward_own_kernel(
    info, pos_ref, q_ref, kv, o_ref, lse_ref, d0, d1, d2, d3, before, dq_ref, dkv_ref, ks, vs, dk, dv, dos
):
    for s in range(8):
        src = ds(info[SORTED + s] * RUN, RUN)
        ks[rows_of(s, RUN), :] = kv[src, :HEAD]
        vs[rows_of(s, RUN), :] = kv[src, HEAD:]
        dos[s] = (d0, d3, d2, d1)[s % 4][s // 4]
    dk[...] = jnp.zeros_like(dk)
    dv[...] = jnp.zeros_like(dv)
    for s in range(8):
        b = info[SORTED + s]
        q, do, delta, lse = backward_run(b, b, q_ref, o_ref, lse_ref, dos[b])
        keys = ks[: (s + 1) * RUN, :]
        p = jnp.exp2(dot_nt(keys, q) * (SCALE * LOG2E) - lse)
        diagonal = jnp.where(own_mask(pos_ref, b), p[s * RUN :], 0.0)
        p = jnp.concatenate([p[: s * RUN], diagonal], axis=0) if s else diagonal
        d_s = (p * (dot_nt(vs[: (s + 1) * RUN, :], do) - delta)).astype(BF)
        dv[: (s + 1) * RUN, :] += dot(p.astype(BF), do)
        dk[: (s + 1) * RUN, :] += dot(d_s, q)
        dq = (dot_tn(d_s, keys) + before[b]) * SCALE
        dq_ref[ds(b * RUN, RUN), :HEAD] = dq[:RUN]
        dq_ref[ds(b * RUN, RUN), HEAD:] = dq[RUN:]
    for s in range(8):
        src = ds(info[SORTED + s] * RUN, RUN)
        dkv_ref[src, :HEAD] = dk[rows_of(s, RUN), :] * SCALE
        dkv_ref[src, HEAD:] = dv[rows_of(s, RUN), :]


def head_back(raw, gain, grad, cos, sin):
    grad = grad * cos + pltpu.roll(grad * sin, HEAD // 2, 1)
    pulled, by_gain = norm_pull(raw, gain, grad)
    return pulled.astype(BF), jnp.sum(by_gain, axis=0, keepdims=True)


def query_back_kernel(info, h_ref, gain_ref, cos, sin, raw, dq_ref, low_ref, g_ref, sum_ref):
    sum_ref[...] = jnp.zeros_like(sum_ref)
    for i in range(4):
        here = rows_of(i, 256)
        for a in range(2):
            cols = rows_of(a, HEAD)
            low, by_gain = head_back(raw[here, cols], gain_ref[0:1, 2048:2176], dq_ref[here, cols], cos[here, :], sin[here, :])
            low_ref[here, cols] = low
            sum_ref[...] += by_gain
    for k in range(4):
        for j in range(2):
            f = info[FOF + 4 * j + (4 - k) % 4]
            g_ref[k, j] = dot_tn(h_ref[:, ds(f * RUN, RUN)], low_ref[...])


def key_value_back_kernel(
    info, h_ref, w_ref, gain_ref, cos, sin, raw, dkv_ref, recv, gq_ref, qsum, ffn_ref,
    out0, out1, out2, out3, dq_ref, y_own, y_sib, g0, g1, g2, g3, own_ref, sib_ref, low_ref,
):
    sums = jnp.zeros((1, HEAD), F32)
    for i in range(4):
        here = rows_of(i, 256)
        dkv = dkv_ref[here, :] + recv[here, :].astype(F32)
        low, by_gain = head_back(raw[here, :], gain_ref[0:1, 2176:2304], dkv[:, :HEAD], cos[here, :], sin[here, :])
        low_ref[here, :HEAD] = low
        low_ref[here, HEAD:] = dkv[:, HEAD:].astype(BF)
        sums += by_gain
    lane = lax.broadcasted_iota(jnp.int32, (8, HEAD), 1)
    heads = [jnp.broadcast_to(s, (8, HEAD)) for s in (qsum[...], sums)]
    for k, g_ref in enumerate((g0, g1, g2, g3)):
        for j in range(2):
            f = info[FOF + 4 * j + (4 - k) % 4]
            here = ds(f * RUN, RUN)
            gkv = dot_tn(h_ref[:, here], low_ref[...])
            gq = gq_ref[k, j]
            g_ref[j, :RUN, :256] = gq.astype(BF)
            g_ref[j, :RUN, 256:] = gkv.astype(BF)
            by_attn = jnp.sum(gq * w_ref[here, :256].astype(F32) + gkv * w_ref[here, 256:].astype(F32), axis=1, keepdims=True)
            by_attn = jnp.broadcast_to(by_attn, (RUN, RUN)).T[:8] / gain_ref[:, here]
            rows = [by_attn, jnp.broadcast_to(ffn_ref[0:1, here], (8, RUN))]
            rows += [jnp.where(lane < 16, pltpu.roll(r, HEAD - 16 * f, 1), 0.0) for r in heads]
            rows = jnp.concatenate(rows, axis=1)
            g_ref[j, RUN : RUN + 16, :] = jnp.concatenate([rows, rows], axis=0).astype(BF)
            for n in range(4):
                src = ds(f * 256 + n * 64, 64)
                rows = sum(o[src, :].astype(F32) for o in (out0, out1, out2, out3))
                g_ref[j, RUN + 16 :, rows_of(n, RUN)] = rows.astype(BF)
    for i in range(4):
        here = rows_of(i, 256)
        part = dot_nt(dq_ref[here, :], w_ref[:, :256]) + dot_nt(low_ref[here, :], w_ref[:, 256:])
        part = part.astype(BF)
        out, y_ref = ((own_ref, y_own), (sib_ref, y_sib))[i // 2]
        for n in range(2):
            k = 2 * (i % 2) + n
            out[rows_of(2 * k, RUN), :] = part[rows_of(n, RUN)]
            out[rows_of(2 * k + 1, RUN), :] = y_ref[rows_of(k, RUN), :]


def last_kernel(p0, p1, p2, p3, x_ref, x2_ref, dx2_ref, gain_ref, out_ref, grad_ref):
    sums = sum(p[...].astype(F32) for p in (p0, p1, p2, p3))
    out_ref[...] = (x2_ref[...] + sums[RUN:]).astype(BF)
    grad_ref[...] = dx2_ref[...] + norm_pull(x_ref[...].astype(F32), gain_ref[0:1, :1024], sums[:RUN])[0]


def unpack_kernel(info, own, sib, g_ref, out_ref, gain_ref):
    gain_ref[...] = jnp.zeros_like(gain_ref)
    for j, part in enumerate((own, sib)):
        for k in range(4):
            t = info[TOF + 4 * j + k]
            g_ref[:, ds(t * 256, 256)] = part[k, :RUN, :256].astype(F32)
            g_ref[:, ds(2048 + t * RUN, RUN)] = part[k, :RUN, 256:384].astype(F32)
            g_ref[:, ds(3072 + t * RUN, RUN)] = part[k, :RUN, 384:].astype(F32)
            gain_ref[...] += part[k, RUN : RUN + 16, :].astype(F32)[:8]
            for n in range(4):
                out_ref[rows_of(n, 64), ds(t * RUN, RUN)] = part[k, RUN + 16 :, rows_of(n, RUN)].astype(F32)


def z_sum_kernel(g0, g1, g2, g3, rows, mine, theirs):
    for j, out in enumerate((mine, theirs)):
        out[:208, :] = sum(p[j].astype(F32) for p in (g0, g1, g2, g3)).astype(BF)
    mine[208:400, :] = rows[:, :512]
    mine[400:, :256] = rows[:96, 512:]
    mine[400:, 256:] = rows[96:, 512:]


def add_kernel(a, b, out):
    for i in range(8):
        here = rows_of(i, a.shape[0] // 8)
        out[here, :] = (a[here, :].astype(F32) + b[here, :].astype(F32)).astype(BF)


def sum_kernel(mine, xlo, xhi, cross, out, rows):
    both = mine[...].astype(F32) + xhi[...].astype(F32)
    out[...] = (both[:208] + xlo[...].astype(F32) + cross[...].astype(F32)).astype(BF)
    both = both.astype(BF)
    rows[:, :512] = both[208:400]
    rows[:96, 512:] = both[400:, :256]
    rows[96:, 512:] = both[400:, 256:]


def unpack_ffn_kernel(wide, gate, up, down):
    for a, out in ((0, gate), (384, up)):
        for f in range(8):
            pieces = [wide[t, :RUN, a + f * 48 : a + f * 48 + 48].astype(F32) for t in range(8)]
            out[:, f * 384 : (f + 1) * 384] = jnp.concatenate(pieces, axis=1)
    for t in range(8):
        down[t * 48 : (t + 1) * 48, :768] = wide[t, 128:176, :].astype(F32)
        for n in range(3):
            at = t * 48 + 16 * n
            down[at : at + 16, 768:] = wide[t, 176:192, rows_of(n, 256)].astype(F32)


def call(kernel, outs, scratch, micros, *args, info=None, deps=(), token=False):
    smem = [] if info is None else [info]
    first, late = len(smem) + len(args), len(smem) + len(args) + len(deps)
    outs = outs + [TOKEN] * token
    end = late + len(outs) - token

    def body(*refs):
        kernel(*refs[:first], *refs[late:end], *refs[end + token :])
        if token:
            refs[end][...] = jnp.zeros(TOKEN[0], F32)

    vmem = pl.BlockSpec(memory_space=pltpu.VMEM)
    return pl.pallas_call(
        body,
        name=getattr(kernel, "func", kernel).__name__,
        out_shape=[jax.ShapeDtypeStruct(*o) for o in outs],
        in_specs=[pl.BlockSpec(memory_space=pltpu.SMEM)] * len(smem)
        + [vmem] * (len(args) + len(deps)),
        out_specs=[vmem] * len(outs),
        scratch_shapes=[pltpu.VMEM(*s) for s in scratch],
        compiler_params=pltpu.CompilerParams(vmem_limit_bytes=16 * 2**20),
        cost_estimate=pl.CostEstimate(flops=int(micros * 3e8), bytes_accessed=2**12, transcendentals=0),
    )(*smem, *args, *deps)


def shards(
    tokens, positions, w_qkv, w_out, w_gate, w_up, w_down, attn_gain, ffn_gain, q_gain, k_gain, cotangent
):
    xhi, y, core = (lax.axis_index(a) for a in CTX)
    xlo, z = (lax.axis_index(a) for a in FSDP)
    t = y * 2 + core
    x_own, dy = tokens[0], cotangent[0]

    wqs = [pl.BlockSpec((RUN, n), lambda i, at, first=first: (0, first + at[0])) for n, first in ((256, 0), (128, 16), (128, 24))]
    small = [g[None] for g in (attn_gain, ffn_gain, q_gain, k_gain)]
    slice_qkv = pl.pallas_call(
        pack_kernel,
        out_shape=jax.ShapeDtypeStruct((RUN + 16, 512), BF),
        grid_spec=pltpu.PrefetchScalarGridSpec(
            num_scalar_prefetch=1,
            grid=(1,),
            in_specs=wqs + [pl.BlockSpec(g.shape, lambda i, at: (0, 0)) for g in small],
            out_specs=pl.BlockSpec((RUN + 16, 512), lambda i, at: (0, 0)),
        ),
    )(t[None].astype(jnp.int32), w_qkv, w_qkv, w_qkv, *small)
    xs = gather_tokens(x_own)
    here = t[None].astype(jnp.int32)
    later = ((8, RUN), jnp.int32)
    pair_qkv, later_t = call(
        pair_kernel, [((2, RUN + 16, 512), BF), later], [], 1, slice_qkv, shift(slice_qkv, "xlo", 1), info=here
    )
    parts_qkv = spread_z(pair_qkv)
    later_t = later_t[0, 0]
    eight = jnp.arange(8, dtype=jnp.int32)
    block = lax.rem(y - eight % 4 + 4, 4) * 2 + (core ^ (eight // 4))
    f_of = (xlo ^ (eight // 4)) * 4 + lax.rem(z - eight % 4 + 4, 4)
    blocks = jnp.concatenate([xhi * 8 + block, (1 - xhi) * 8 + block])
    pos = (positions[0] + later_t // 8).reshape(16, RUN)[blocks]
    rank = pos[:, 0] // RUN
    place = jnp.sum(rank[:8, None] > rank[None, :8], axis=1)
    in_order = jnp.argmax(place[None, :] == eight[:, None], axis=1)
    info = jnp.concatenate([in_order, f_of, block, core[None]]).astype(jnp.int32)
    bias = jnp.where(rank[:8, None] > rank[None, 8:], 0.0, MASKED)
    pos_rows = pos.astype(F32).reshape(16, 1, RUN)
    inverse = THETA ** (-(jnp.arange(HEAD // 2, dtype=F32) * 2.0 / HEAD))
    angles = pos[:8].reshape(1024).astype(F32)[:, None] * inverse[None, :]
    cosine, sine = jnp.cos(angles), jnp.sin(angles)
    cosine = jnp.concatenate([cosine, cosine], axis=1)
    sine = jnp.concatenate([-sine, sine], axis=1)

    (slice_ffn,) = call(
        pack_ffn_kernel, [((192, 768), BF)], [], 3, w_gate, w_up, w_down, info=here, deps=[pair_qkv]
    )
    received = shift(slice_ffn, "xlo", 1)
    half_out = lax.dynamic_slice_in_dim(w_out, core * HEAD, HEAD, 0)
    pair_out, _, out_token = call(
        pair_kernel,
        [((2, RUN, 1024), BF), later],
        [],
        1,
        half_out, shift(half_out, "xlo", 1),
        info=here,
        deps=[received] + parts_qkv[1:],
        token=True,
    )
    parts_out = spread_z(pair_out)

    h, wqkv, gain, kraw, kv, dy_later = call(
        key_value_kernel,
        [((1024, 1024), BF), ((1024, 512), BF), ((8, 2304), F32), ((1024, HEAD), F32), ((1024, 256), BF), ((RUN, 1024), BF)],
        [],
        5,
        *xs, *parts_qkv, cosine, sine, dy,
        info=info,
        deps=[out_token],
    )
    kv_other = shift(kv, "xhi", 1)
    qraw, q = call(query_kernel, [((1024, 256), F32), ((1024, 256), BF)], [], 3, h, wqkv, gain, cosine, sine)
    (partial,) = call(
        forward_own_kernel,
        [((8, HEAD + 8, 256), F32)],
        [((1024, HEAD), BF), ((256, 1024), BF)],
        5,
        pos_rows, q, kv,
        info=info,
    )
    dy_all = lax.all_gather(dy_later, TP, axis=0, tiled=True)
    o32, lse, o_low, o_token = call(
        forward_other_kernel,
        [((1024, 256), F32), ((8, 1, 256), F32), ((2, 4, RUN, 256), BF)],
        [((256, 1024), BF)],
        6,
        q, kv_other, partial,
        info=bias,
        deps=[parts_out[1], parts_out[3]],
        token=True,
    )
    parts_o = exchange(o_low[0], o_low[1])
    (wout_own,) = call(assemble_out_kernel, [((1024, 1024), BF)], [], 1, *parts_out, info=info, deps=[o_token])
    wout_sib = shift(wout_own, "core", 1)
    ffn_pairs = lambda follow: call(
        pair_kernel, [((2, 192, 768), BF), later], [], 1, slice_ffn, received, info=here, deps=[follow]
    )[0]
    pair_ffn = ffn_pairs(o_token)
    parts_ffn = [pair_ffn, shift(pair_ffn, "z", 1), None, shift(pair_ffn, "z", 3)]
    x2, h2_own, o_all, x_token = call(
        out_kernel,
        [((RUN, 1024), F32), ((RUN, 1024), BF), ((RUN, 2048), BF)],
        [],
        4,
        x_own, *parts_o, wout_own, wout_sib, gain,
        info=info,
        deps=[parts_ffn[1], parts_ffn[3]],
        token=True,
    )
    parts_ffn[2] = shift(ffn_pairs(x_token), "z", 2)
    wgu, wd, w_token = call(assemble_kernel, [((1024, 768), BF), ((384, 1024), BF)], [], 2, *parts_ffn, info=info, token=True)

    h2_parts = [h2_own] + [shift(h2_own, "y", k) for k in (1, 2, 3)]
    (h2_join,) = call(join_kernel, [((512, 1024), BF)], [], 1, *h2_parts, deps=[w_token])
    h2 = h2_join, shift(h2_join, "core", 1)
    ffn = [
        call(
            functools.partial(ffn_kernel, 4 * j),
            [((512, 384), BF), ((512, 768), BF), ((512, 1024), BF)],
            [],
            6,
            h2[j], dy_all, wgu, wd,
            info=info,
        )
        for j in (1, 0)
    ]
    (act_sib, dgu_sib, part_sib), (act_own, dgu_own, part_own) = ffn
    d_h2 = scatter_tokens(part_own, part_sib)
    g_ffn, y_own, y_sib, g_token = call(
        ffn_grad_kernel,
        [((8, 192, 768), BF), ((512, 1024), BF), ((512, 1024), BF)],
        [],
        8,
        *h2, dy_all, act_own, act_sib, dgu_own, dgu_sib, wd,
        info=info,
        token=True,
    )
    d_x2, d_branch, ffn_sum, do_own, do_other = call(
        middle_kernel,
        [((RUN, 1024), F32), ((RUN, 1024), BF), ((1, 1024), F32), ((4, RUN, 256), BF), ((4, RUN, 256), BF)],
        [((RUN, 2048), BF)],
        0,
        *d_h2, x2, dy, gain, wout_own, wout_sib,
        info=info,
        deps=[g_token],
    )
    d_o = exchange(do_own, do_other)
    g_out_own, g_out_other = call(
        out_grad_kernel, [((4, 2048, RUN), BF)] * 2, [((256, 1024), BF)], 0, o_all, d_branch, info=info
    )

    rows_ffn = lax.psum_scatter(g_ffn, FSDP, scatter_dimension=0, tiled=False)
    blocks_out, b_token = call(
        add_kernel,
        [((4 * 2048, RUN), BF)],
        [],
        0,
        g_out_own.reshape(-1, RUN), shift(g_out_other, "core", 1).reshape(-1, RUN),
        token=True,
    )
    blocks_out = blocks_out.reshape(4, 2048, RUN)
    out_parts = [blocks_out[0]] + [shift(blocks_out[k], "y", 4 - k) for k in (1, 2, 3)]

    d_q, d_other = call(
        backward_other_kernel,
        [((8, 256, HEAD), F32), ((1024, 256), BF)],
        [((1024, HEAD), F32), ((1024, HEAD), F32)],
        0,
        q, kv_other, o32, lse, *d_o,
        info=bias,
        deps=[b_token],
    )
    recv = shift(d_other, "xhi", 1)
    d_q, d_kv = call(
        backward_own_kernel,
        [((1024, 256), F32), ((1024, 256), F32)],
        [((1024, HEAD), BF), ((1024, HEAD), BF), ((1024, HEAD), F32), ((1024, HEAD), F32), ((8, RUN, 256), BF)],
        8,
        pos_rows, q, kv, o32, lse, *d_o, d_q,
        info=info,
    )
    dq_low, g_q, q_sum = call(
        query_back_kernel,
        [((1024, 256), BF), ((4, 2, RUN, 256), F32), ((1, HEAD), F32)],
        [],
        5,
        h, gain, cosine, sine, qraw, d_q,
        info=info,
    )
    *g_qkv, part_own, part_sib = call(
        key_value_back_kernel,
        [((2, 208, 512), BF)] * 4 + [((1024, 1024), BF)] * 2,
        [((1024, 256), BF)],
        8,
        h, wqkv, gain, cosine, sine, kraw, d_kv, recv, g_q, q_sum, ffn_sum, *out_parts, dq_low, y_own, y_sib,
        info=info,
        deps=[rows_ffn],
    )
    g_qkv = [g_qkv[0]] + [shift(g_qkv[k], "z", k) for k in (1, 2, 3)]
    d_h, d_token = call(
        add_kernel, [((1024, 1024), BF)], [], 1, part_own, shift(part_sib, "core", 1), token=True
    )
    mine, theirs = call(z_sum_kernel, [((496, 512), BF), ((208, 512), BF)], [], 1, *g_qkv, rows_ffn, deps=[d_token])
    d_h = d_h.reshape(4, 256, 1024)
    d_h = [d_h[0]] + [shift(d_h[k], "y", 4 - k) for k in (1, 2, 3)]
    cross = lax.ppermute(theirs, ("xlo", "xhi"), [(i, i ^ 3) for i in range(4)])
    total, half_ffn = call(
        sum_kernel,
        [((208, 512), BF), ((192, 768), BF)],
        [],
        1,
        mine, shift(theirs, "xlo", 1), shift(mine, "xhi", 1), cross,
        deps=d_h[1:],
    )
    sum_ffn = lax.all_gather(half_ffn, TP, axis=0)
    sum_gate, sum_up, sum_down = call(
        unpack_ffn_kernel, [((128, 3072), F32), ((128, 3072), F32), ((384, 1024), F32)], [], 4, sum_ffn
    )
    own = jnp.stack([total] + [shift(total, "y", k) for k in (1, 2, 3)])
    sum_qkv, sum_out, sum_gains = call(
        unpack_kernel,
        [((128, 4096), F32), ((256, 1024), F32), ((8, 512), F32)],
        [],
        3,
        own, shift(own, "core", 1),
        info=info,
    )
    output, input_grad = call(
        last_kernel, [((RUN, 1024), BF), ((RUN, 1024), F32)], [], 2, *d_h, x_own, x2, d_x2, gain
    )
    return (
        output[None],
        input_grad[None],
        sum_qkv,
        sum_out,
        sum_gate,
        sum_up,
        sum_down,
        sum_gains[0, :128],
        sum_gains[0, 128:256],
        sum_gains[0, 256:272],
        sum_gains[0, 384:400],
    )


def solution(mesh):
    split = Mesh(mesh.devices.reshape(tuple(SIZES.values())), FSDP + CTX)
    rows, both = P(FSDP, None), P(FSDP, CTX, None)
    return jax.shard_map(
        shards,
        mesh=split,
        in_specs=(both,) + (rows,) * 6 + (P(FSDP),) * 4 + (both,),
        out_specs=(both, both) + (rows,) * 5 + (P(FSDP),) * 4,
        check_vma=False,
    )
```

```python
import functools

import jax
import jax.numpy as jnp
from jax import lax
from jax.experimental import pallas as pl
from jax.experimental.pallas import tpu as pltpu
from jax.sharding import Mesh
from jax.sharding import PartitionSpec as P

HEAD = 128
EPS = 1e-06
MASKED = -1e30
THETA = 1000000.0
SCALE = HEAD**-0.5
LOG2E = 1.4426950408889634
RUN = 128
FSDP = ("xlo", "z")
CTX = ("xhi", "y", "core")
TP = ("y", "core")
SIZES = {"xlo": 2, "z": 4, "xhi": 2, "y": 4, "core": 2}
BF = jnp.bfloat16
F32 = jnp.float32
TOKEN = ((8, 128), jnp.float32)
SORTED, FOF, TOF, CORE = 0, 8, 16, 24


def shift(x, axis, step):
    n = SIZES[axis]
    return lax.ppermute(x, axis, [(i, (i + step) % n) for i in range(n)])


def gather_tokens(x):
    own = jnp.concatenate([x] + [shift(x, "y", k) for k in (1, 2, 3)], axis=0)
    return own, shift(own, "core", 1)


def scatter_tokens(own, other):
    blocks = (own.astype(F32) + shift(other, "core", 1).astype(F32)).astype(BF).reshape(4, own.shape[0] // 4, -1)
    return [blocks[0]] + [shift(blocks[k], "y", 4 - k) for k in (1, 2, 3)]


def exchange(own, other):
    both = jnp.stack([own, shift(other, "core", 1)], axis=1)
    return [both[0]] + [shift(both[k], "y", 4 - k) for k in (1, 2, 3)]


def spread_z(pair):
    return [pair] + [shift(pair, "z", k) for k in (1, 2, 3)]


def dot(a, b):
    return jnp.dot(a, b, preferred_element_type=F32)


def dot_nt(a, b):
    return lax.dot_general(a, b, (((1,), (1,)), ((), ())), preferred_element_type=F32)


def dot_tn(a, b):
    return lax.dot_general(a, b, (((0,), (0,)), ((), ())), preferred_element_type=F32)


def inv_rms(x):
    return lax.rsqrt(jnp.mean(x * x, axis=-1, keepdims=True) + EPS)


def norm_pull(x, gain, grad):
    inv = inv_rms(x)
    hat = x * inv
    scaled = grad * gain
    return inv * (scaled - hat * jnp.mean(scaled * hat, axis=-1, keepdims=True)), grad * hat


def ds(at, size):
    return pl.ds(pl.multiple_of(at, size), size)


def rows_of(i, size):
    return slice(i * size, (i + 1) * size)


def pack_kernel(at, q_ref, k_ref, v_ref, attn, ffn, qg, kg, out):
    out[:RUN, :256] = q_ref[...]
    out[:RUN, 256:384] = k_ref[...]
    out[:RUN, 384:] = v_ref[...]
    none = jnp.zeros((16, 112), BF)
    rows = [jnp.broadcast_to(g[...], (16, g.shape[1])) for g in (attn, ffn, qg, kg)]
    out[RUN:, :128] = rows[0]
    out[RUN:, 128:256] = rows[1]
    out[RUN:, 256:384] = jnp.concatenate([rows[2], none], axis=1)
    out[RUN:, 384:] = jnp.concatenate([rows[3], none], axis=1)


def key_value_kernel(info, own, sib, w0, w1, w2, w3, cos, sin, dy, h_ref, w_ref, gain_ref, raw_ref, kv_ref, dy_ref):
    dy_ref[...] = dy[...]
    gain_ref[...] = jnp.zeros_like(gain_ref)
    for k, part in enumerate((w0, w1, w2, w3)):
        for j in range(2):
            f = info[FOF + 4 * j + k]
            w_ref[ds(f * RUN, RUN), :] = part[j, :RUN, :]
            row = part[j, RUN:, :].astype(F32)[:8]
            gain_ref[:, ds(f * RUN, RUN)] = row[:, :128]
            gain_ref[:, ds(1024 + f * RUN, RUN)] = row[:, 128:256]
            gain_ref[:, 2048:2176] += pltpu.roll(row[:, 256:384], f * 16, 1)
            gain_ref[:, 2176:2304] += pltpu.roll(row[:, 384:512], f * 16, 1)
    attn_gain, k_gain = gain_ref[0:1, :1024], gain_ref[0:1, 2176:2304]
    for i in range(4):
        part = (own, sib)[i // 2]
        here = rows_of(i, 256)
        x = part[rows_of(i % 2, 256), :].astype(F32)
        h = (x * inv_rms(x) * attn_gain).astype(BF)
        h_ref[here, :] = h
        raw = dot(h, w_ref[:, 256:])
        raw_ref[here, :] = raw[:, :HEAD]
        key = raw[:, :HEAD]
        key = key * inv_rms(key) * k_gain
        key = key * cos[here, :] + pltpu.roll(key, HEAD // 2, 1) * sin[here, :]
        kv_ref[here, :HEAD] = key.astype(BF)
        kv_ref[here, HEAD:] = raw[:, HEAD:].astype(BF)


def query_kernel(h_ref, w_ref, gain_ref, cos, sin, raw_ref, q_ref):
    gain = gain_ref[0:1, 2048:2176]
    for i in range(4):
        here = rows_of(i, 256)
        raw = dot(h_ref[here, :], w_ref[:, :256])
        raw_ref[here, :] = raw
        for a in range(2):
            u = raw[:, rows_of(a, HEAD)]
            u = u * inv_rms(u) * gain
            u = u * cos[here, :] + pltpu.roll(u, HEAD // 2, 1) * sin[here, :]
            q_ref[here, rows_of(a, HEAD)] = u.astype(BF)


def stacked(rows):
    return jnp.concatenate([rows[:, :HEAD], rows[:, HEAD:]], axis=0)


def own_mask(pos_ref, b):
    row = pos_ref[b]
    keys = jnp.broadcast_to(row, (RUN, RUN)).T
    return jnp.concatenate([keys, keys], axis=1) <= jnp.concatenate([row, row], axis=1)


def expo(keys, q):
    return jnp.exp2(dot_nt(keys, q) * (SCALE * LOG2E))


def forward_own_kernel(info, pos_ref, q_ref, kv, part_ref, ks, vt):
    vt[HEAD:, :] = jnp.ones((HEAD, vt.shape[1]), BF)
    for s in range(8):
        src = ds(info[SORTED + s] * RUN, RUN)
        ks[rows_of(s, RUN), :] = kv[src, :HEAD]
        vt[:HEAD, rows_of(s, RUN)] = kv[src, HEAD:].T
    for s in range(8):
        b = info[SORTED + s]
        q = stacked(q_ref[ds(b * RUN, RUN), :])
        e = jnp.where(own_mask(pos_ref, b), expo(ks[rows_of(s, RUN), :], q), 0.0)
        acc = dot(vt[:, rows_of(s, RUN)], e.astype(BF))
        if s:
            acc += dot(vt[:, : s * RUN], expo(ks[: s * RUN, :], q).astype(BF))
        part_ref[b] = acc[: HEAD + 8]


def forward_other_kernel(bias, q_ref, kv, part_ref, o_ref, lse_ref, low_ref, vt):
    vt[HEAD:, :] = jnp.ones((HEAD, vt.shape[1]), BF)
    vt[:HEAD, :] = kv[:, HEAD:].T
    for i in range(8):
        q = stacked(q_ref[rows_of(i, RUN), :])
        scores = dot_nt(kv[:, :HEAD], q) * (SCALE * LOG2E)
        e = jnp.concatenate([jnp.exp2(scores[rows_of(b, RUN)] + bias[i, b]).astype(BF) for b in range(8)], axis=0)
        acc = dot(vt[...], e)
        total = acc[HEAD : HEAD + 1, :] + part_ref[i, HEAD : HEAD + 1, :]
        out = ((acc[:HEAD, :] + part_ref[i, :HEAD, :]) / total).T
        out = jnp.concatenate([out[:RUN], out[RUN:]], axis=1)
        o_ref[rows_of(i, RUN), :] = out
        low_ref[i // 4, i % 4] = out.astype(BF)
        lse_ref[i] = jnp.log2(total)


def out_kernel(info, x_ref, o0, o1, o2, o3, w_own, w_sib, gain_ref, x2_ref, h2_ref, oall_ref):
    core = info[CORE]
    for k, part in enumerate((o0, o1, o2, o3)):
        for j in range(2):
            at = info[TOF + 4 * j + (4 - k) % 4] * HEAD
            oall_ref[:, ds(at, HEAD)] = part[j, :, ds(core * HEAD, HEAD)]
            oall_ref[:, ds(1024 + at, HEAD)] = part[j, :, ds((1 - core) * HEAD, HEAD)]
    x2 = x_ref[...].astype(F32) + dot(oall_ref[:, :1024], w_own[...]) + dot(oall_ref[:, 1024:], w_sib[...])
    x2_ref[...] = x2
    h2_ref[...] = (x2 * inv_rms(x2) * gain_ref[0:1, 1024:2048]).astype(BF)


def pack_ffn_kernel(rank, gate, up, down, out):
    at = rank[0] * 48
    q = jnp.minimum(at // RUN, 1)
    for a, w in ((0, gate), (384, up)):
        pieces = []
        for f in range(8):
            window = w[:, pl.ds(pl.multiple_of(f * 384 + q * RUN, RUN), 256)].astype(F32)
            pieces.append(pltpu.roll(window, (256 - (at - q * RUN)) % 256, 1)[:, :48])
        out[:RUN, a : a + 384] = jnp.concatenate(pieces, axis=1).astype(BF)
    rows = down[pl.ds(pl.multiple_of(at, 16), 48), :]
    out[128:176, :] = rows[:, :768]
    for n in range(3):
        out[176:192, rows_of(n, 256)] = rows[16 * n : 16 * n + 16, 768:]


def join_kernel(a, b, c, d, out):
    for i, part in enumerate((a, b, c, d)):
        out[rows_of(i, RUN), :] = part[...]


def pair_kernel(rank, a, b, out, rank_out):
    out[0] = a[...]
    out[1] = b[...]
    rank_out[...] = jnp.full(rank_out.shape, rank[0], jnp.int32)


def assemble_out_kernel(info, p0, p1, p2, p3, w_ref):
    for k, part in enumerate((p0, p1, p2, p3)):
        for j in range(2):
            w_ref[ds(info[FOF + 4 * j + k] * HEAD, HEAD), :] = part[j]


def assemble_kernel(info, p0, p1, p2, p3, wgu, wd):
    for k, part in enumerate((p0, p1, p2, p3)):
        for j in range(2):
            f = info[FOF + 4 * j + k]
            wgu[ds(f * RUN, RUN), :] = part[j, :RUN, :]
            wd[pl.ds(pl.multiple_of(f * 48, 16), 48), :768] = part[j, 128:176, :]
            for n in range(3):
                wd[ds(f * 48 + 16 * n, 16), 768:] = part[j, 176:192, rows_of(n, 256)]


def blocks_of(info, dy_ref, first, count):
    return jnp.concatenate([dy_ref[ds(info[TOF + first + n] * RUN, RUN), :] for n in range(count)], axis=0)


def ffn_kernel(base, info, h2_ref, dy_ref, wgu, wd, act_ref, dgu_ref, part_ref):
    for i in range(2):
        here = rows_of(i, 256)
        gu = dot(h2_ref[here, :], wgu[...])
        gate, up = gu[:, :384], gu[:, 384:]
        sg = 1.0 / (1.0 + jnp.exp(-gate))
        silu = gate * sg
        act_ref[here, :] = (silu * up).astype(BF)
        d_act = dot_nt(blocks_of(info, dy_ref, base + 2 * i, 2), wd[...])
        d_gate = (d_act * up * (sg * (1.0 + gate * (1.0 - sg)))).astype(BF)
        d_gu = jnp.concatenate([d_gate, (d_act * silu).astype(BF)], axis=1)
        dgu_ref[here, :] = d_gu
        part_ref[here, :] = dot_nt(d_gu, wgu[...]).astype(BF)


def ffn_grad_kernel(info, h2_own, h2_sib, dy_ref, act_own, act_sib, dgu_own, dgu_sib, wd, g_ref, y_own, y_sib):
    y_own[...] = dot(act_own[...], wd[...]).astype(BF)
    y_sib[...] = dot(act_sib[...], wd[...]).astype(BF)
    for a in range(4):
        cols = rows_of(a, 256)
        g = (dot_tn(h2_own[:, cols], dgu_own[...]) + dot_tn(h2_sib[:, cols], dgu_sib[...])).astype(BF)
        g_ref[2 * a, :RUN, :] = g[:RUN]
        g_ref[2 * a + 1, :RUN, :] = g[RUN:]
    g = dot_tn(act_own[...], blocks_of(info, dy_ref, 0, 4)) + dot_tn(act_sib[...], blocks_of(info, dy_ref, 4, 4))
    g = g.astype(BF)
    for f in range(8):
        rows = g[f * 48 : (f + 1) * 48]
        g_ref[f, 128:176, :] = rows[:, :768]
        for n in range(3):
            g_ref[f, 176:192, rows_of(n, 256)] = rows[16 * n : 16 * n + 16, 768:]


def middle_kernel(
    info, p0, p1, p2, p3, x2_ref, dy_ref, gain_ref, w_own, w_sib, dx2_ref, low_ref, gsum_ref, do_own, do_other, do
):
    grad = sum(p[...].astype(F32) for p in (p0, p1, p2, p3))
    pulled, by_gain = norm_pull(x2_ref[...], gain_ref[0:1, 1024:2048], grad)
    gsum_ref[...] = jnp.sum(by_gain, axis=0, keepdims=True)
    dx2 = dy_ref[...].astype(F32) + pulled
    dx2_ref[...] = dx2
    low = dx2.astype(BF)
    low_ref[...] = low
    do[:, :1024] = dot_nt(low, w_own[...]).astype(BF)
    do[:, 1024:] = dot_nt(low, w_sib[...]).astype(BF)
    core = info[CORE]
    for j, out in enumerate((do_own, do_other)):
        for k in range(4):
            at = info[TOF + 4 * j + k] * HEAD
            out[k, :, ds(core * HEAD, HEAD)] = do[:, ds(at, HEAD)]
            out[k, :, ds((1 - core) * HEAD, HEAD)] = do[:, ds(1024 + at, HEAD)]


def out_grad_kernel(info, o_ref, d_ref, own_ref, other_ref, g_all):
    core = info[CORE]
    for a in range(8):
        g_all[...] = dot_tn(o_ref[:, rows_of(a, 256)], d_ref[...]).astype(BF)
        for n in range(2):
            f, half = (2 * a + n) % 8, core if a < 4 else 1 - core
            rows = ds((2 * f + half) * HEAD, HEAD)
            for k in range(4):
                own_ref[k, rows, :] = g_all[rows_of(n, HEAD), ds(info[TOF + k] * RUN, RUN)]
                other_ref[k, rows, :] = g_all[rows_of(n, HEAD), ds(info[TOF + 4 + k] * RUN, RUN)]


def backward_run(b, ref_b, q_ref, o_ref, lse_ref, do):
    rows = ds(b * RUN, RUN)
    q = stacked(q_ref[rows, :])
    do = stacked(do)
    delta = jnp.sum((do.astype(F32) * stacked(o_ref[rows, :])).T, axis=0, keepdims=True)
    return q, do, delta, lse_ref[ref_b]


def backward_other_kernel(bias, q_ref, kv, o_ref, lse_ref, d0, d1, d2, d3, dq_ref, dkv_ref, dk, dv):
    for i in range(8):
        q, do, delta, lse = backward_run(i, i, q_ref, o_ref, lse_ref, (d0, d3, d2, d1)[i % 4][i // 4])
        scores = dot_nt(kv[:, :HEAD], q) * (SCALE * LOG2E)
        p = jnp.concatenate([jnp.exp2(scores[rows_of(b, RUN)] - (lse - bias[i, b])) for b in range(8)], axis=0)
        d_s = (p * (dot_nt(kv[:, HEAD:], do) - delta)).astype(BF)
        by_v, by_k = dot(p.astype(BF), do), dot(d_s, q)
        dv[...] = by_v if i == 0 else dv[...] + by_v
        dk[...] = by_k if i == 0 else dk[...] + by_k
        dq_ref[i] = dot_tn(d_s, kv[:, :HEAD])
    dkv_ref[:, :HEAD] = (dk[...] * SCALE).astype(BF)
    dkv_ref[:, HEAD:] = dv[...].astype(BF)


def backward_own_kernel(
    info, pos_ref, q_ref, kv, o_ref, lse_ref, d0, d1, d2, d3, before, dq_ref, dkv_ref, ks, vs, dk, dv, dos
):
    for s in range(8):
        src = ds(info[SORTED + s] * RUN, RUN)
        ks[rows_of(s, RUN), :] = kv[src, :HEAD]
        vs[rows_of(s, RUN), :] = kv[src, HEAD:]
        dos[s] = (d0, d3, d2, d1)[s % 4][s // 4]
    dk[...] = jnp.zeros_like(dk)
    dv[...] = jnp.zeros_like(dv)
    for s in range(8):
        b = info[SORTED + s]
        q, do, delta, lse = backward_run(b, b, q_ref, o_ref, lse_ref, dos[b])
        keys = ks[: (s + 1) * RUN, :]
        p = jnp.exp2(dot_nt(keys, q) * (SCALE * LOG2E) - lse)
        diagonal = jnp.where(own_mask(pos_ref, b), p[s * RUN :], 0.0)
        p = jnp.concatenate([p[: s * RUN], diagonal], axis=0) if s else diagonal
        d_s = (p * (dot_nt(vs[: (s + 1) * RUN, :], do) - delta)).astype(BF)
        dv[: (s + 1) * RUN, :] += dot(p.astype(BF), do)
        dk[: (s + 1) * RUN, :] += dot(d_s, q)
        dq = (dot_tn(d_s, keys) + before[b]) * SCALE
        dq_ref[ds(b * RUN, RUN), :HEAD] = dq[:RUN]
        dq_ref[ds(b * RUN, RUN), HEAD:] = dq[RUN:]
    for s in range(8):
        src = ds(info[SORTED + s] * RUN, RUN)
        dkv_ref[src, :HEAD] = dk[rows_of(s, RUN), :] * SCALE
        dkv_ref[src, HEAD:] = dv[rows_of(s, RUN), :]


def head_back(raw, gain, grad, cos, sin):
    grad = grad * cos + pltpu.roll(grad * sin, HEAD // 2, 1)
    pulled, by_gain = norm_pull(raw, gain, grad)
    return pulled.astype(BF), jnp.sum(by_gain, axis=0, keepdims=True)


def query_back_kernel(info, h_ref, gain_ref, cos, sin, raw, dq_ref, low_ref, g_ref, sum_ref):
    sum_ref[...] = jnp.zeros_like(sum_ref)
    for i in range(4):
        here = rows_of(i, 256)
        for a in range(2):
            cols = rows_of(a, HEAD)
            low, by_gain = head_back(raw[here, cols], gain_ref[0:1, 2048:2176], dq_ref[here, cols], cos[here, :], sin[here, :])
            low_ref[here, cols] = low
            sum_ref[...] += by_gain
    for k in range(4):
        for j in range(2):
            f = info[FOF + 4 * j + (4 - k) % 4]
            g_ref[k, j] = dot_tn(h_ref[:, ds(f * RUN, RUN)], low_ref[...])


def key_value_back_kernel(
    info, h_ref, w_ref, gain_ref, cos, sin, raw, dkv_ref, recv, gq_ref, qsum, ffn_ref,
    out0, out1, out2, out3, dq_ref, y_own, y_sib, g0, g1, g2, g3, own_ref, sib_ref, low_ref,
):
    sums = jnp.zeros((1, HEAD), F32)
    for i in range(4):
        here = rows_of(i, 256)
        dkv = dkv_ref[here, :] + recv[here, :].astype(F32)
        low, by_gain = head_back(raw[here, :], gain_ref[0:1, 2176:2304], dkv[:, :HEAD], cos[here, :], sin[here, :])
        low_ref[here, :HEAD] = low
        low_ref[here, HEAD:] = dkv[:, HEAD:].astype(BF)
        sums += by_gain
    lane = lax.broadcasted_iota(jnp.int32, (8, HEAD), 1)
    heads = [jnp.broadcast_to(s, (8, HEAD)) for s in (qsum[...], sums)]
    for k, g_ref in enumerate((g0, g1, g2, g3)):
        for j in range(2):
            f = info[FOF + 4 * j + (4 - k) % 4]
            here = ds(f * RUN, RUN)
            gkv = dot_tn(h_ref[:, here], low_ref[...])
            gq = gq_ref[k, j]
            g_ref[j, :RUN, :256] = gq.astype(BF)
            g_ref[j, :RUN, 256:] = gkv.astype(BF)
            by_attn = jnp.sum(gq * w_ref[here, :256].astype(F32) + gkv * w_ref[here, 256:].astype(F32), axis=1, keepdims=True)
            by_attn = jnp.broadcast_to(by_attn, (RUN, RUN)).T[:8] / gain_ref[:, here]
            rows = [by_attn, jnp.broadcast_to(ffn_ref[0:1, here], (8, RUN))]
            rows += [jnp.where(lane < 16, pltpu.roll(r, HEAD - 16 * f, 1), 0.0) for r in heads]
            rows = jnp.concatenate(rows, axis=1)
            g_ref[j, RUN : RUN + 16, :] = jnp.concatenate([rows, rows], axis=0).astype(BF)
            for n in range(4):
                src = ds(f * 256 + n * 64, 64)
                rows = sum(o[src, :].astype(F32) for o in (out0, out1, out2, out3))
                g_ref[j, RUN + 16 :, rows_of(n, RUN)] = rows.astype(BF)
    for i in range(4):
        here = rows_of(i, 256)
        part = dot_nt(dq_ref[here, :], w_ref[:, :256]) + dot_nt(low_ref[here, :], w_ref[:, 256:])
        part = part.astype(BF)
        out, y_ref = ((own_ref, y_own), (sib_ref, y_sib))[i // 2]
        for n in range(2):
            k = 2 * (i % 2) + n
            out[rows_of(2 * k, RUN), :] = part[rows_of(n, RUN)]
            out[rows_of(2 * k + 1, RUN), :] = y_ref[rows_of(k, RUN), :]


def last_kernel(p0, p1, p2, p3, x_ref, x2_ref, dx2_ref, gain_ref, out_ref, grad_ref):
    sums = sum(p[...].astype(F32) for p in (p0, p1, p2, p3))
    out_ref[...] = (x2_ref[...] + sums[RUN:]).astype(BF)
    grad_ref[...] = dx2_ref[...] + norm_pull(x_ref[...].astype(F32), gain_ref[0:1, :1024], sums[:RUN])[0]


def unpack_kernel(info, own, sib, g_ref, out_ref, gain_ref):
    gain_ref[...] = jnp.zeros_like(gain_ref)
    for j, part in enumerate((own, sib)):
        for k in range(4):
            t = info[TOF + 4 * j + k]
            g_ref[:, ds(t * 256, 256)] = part[k, :RUN, :256].astype(F32)
            g_ref[:, ds(2048 + t * RUN, RUN)] = part[k, :RUN, 256:384].astype(F32)
            g_ref[:, ds(3072 + t * RUN, RUN)] = part[k, :RUN, 384:].astype(F32)
            gain_ref[...] += part[k, RUN : RUN + 16, :].astype(F32)[:8]
            for n in range(4):
                out_ref[rows_of(n, 64), ds(t * RUN, RUN)] = part[k, RUN + 16 :, rows_of(n, RUN)].astype(F32)


def z_sum_kernel(g0, g1, g2, g3, rows, mine, theirs):
    for j, out in enumerate((mine, theirs)):
        out[:208, :] = sum(p[j].astype(F32) for p in (g0, g1, g2, g3)).astype(BF)
    mine[208:400, :] = rows[:, :512]
    mine[400:, :256] = rows[:96, 512:]
    mine[400:, 256:] = rows[96:, 512:]


def add_kernel(a, b, out):
    for i in range(8):
        here = rows_of(i, a.shape[0] // 8)
        out[here, :] = (a[here, :].astype(F32) + b[here, :].astype(F32)).astype(BF)


def sum_kernel(mine, xlo, xhi, cross, out, rows):
    both = mine[...].astype(F32) + xhi[...].astype(F32)
    out[...] = (both[:208] + xlo[...].astype(F32) + cross[...].astype(F32)).astype(BF)
    both = both.astype(BF)
    rows[:, :512] = both[208:400]
    rows[:96, 512:] = both[400:, :256]
    rows[96:, 512:] = both[400:, 256:]


def unpack_ffn_kernel(wide, gate, up, down):
    for a, out in ((0, gate), (384, up)):
        for f in range(8):
            pieces = [wide[t, :RUN, a + f * 48 : a + f * 48 + 48].astype(F32) for t in range(8)]
            out[:, f * 384 : (f + 1) * 384] = jnp.concatenate(pieces, axis=1)
    for t in range(8):
        down[t * 48 : (t + 1) * 48, :768] = wide[t, 128:176, :].astype(F32)
        for n in range(3):
            at = t * 48 + 16 * n
            down[at : at + 16, 768:] = wide[t, 176:192, rows_of(n, 256)].astype(F32)


def call(kernel, outs, scratch, micros, *args, info=None, deps=(), token=False, fetch=False):
    smem = [] if info is None else [info]
    first, late = len(smem) + len(args), len(smem) + len(args) + len(deps)
    outs = outs + [TOKEN] * token
    end = late + len(outs) - token

    def body(*refs):
        inputs, scratches = refs[:first], refs[end + token :]
        if fetch:
            held, sems = scratches[len(scratch) : -1], scratches[-1]
            copies = [
                pltpu.make_async_copy(source, target, sems.at[i])
                for i, (source, target) in enumerate(zip(inputs[len(smem) :], held))
            ]
            for copy in copies:
                copy.start()
            for copy in copies:
                copy.wait()
            inputs, scratches = [*inputs[: len(smem)], *held], scratches[: len(scratch)]
        kernel(*inputs, *refs[late:end], *scratches)
        if token:
            refs[end][...] = jnp.zeros(TOKEN[0], F32)

    vmem = pl.BlockSpec(memory_space=pltpu.VMEM)
    source = pl.BlockSpec(memory_space=pl.ANY) if fetch else vmem
    held = [pltpu.VMEM(a.shape, a.dtype) for a in args] + [pltpu.SemaphoreType.DMA((len(args),))]
    return pl.pallas_call(
        body,
        name=getattr(kernel, "func", kernel).__name__,
        out_shape=[jax.ShapeDtypeStruct(*o) for o in outs],
        in_specs=[pl.BlockSpec(memory_space=pltpu.SMEM)] * len(smem)
        + [source] * (len(args) + len(deps)),
        out_specs=[vmem] * len(outs),
        scratch_shapes=[pltpu.VMEM(*s) for s in scratch] + held * fetch,
        compiler_params=pltpu.CompilerParams(vmem_limit_bytes=(28 if fetch else 16) * 2**20),
        cost_estimate=pl.CostEstimate(flops=int(micros * 3e8), bytes_accessed=2**12, transcendentals=0),
    )(*smem, *args, *deps)


def shards(
    tokens, positions, w_qkv, w_out, w_gate, w_up, w_down, attn_gain, ffn_gain, q_gain, k_gain, cotangent
):
    xhi, y, core = (lax.axis_index(a) for a in CTX)
    xlo, z = (lax.axis_index(a) for a in FSDP)
    t = y * 2 + core
    x_own, dy = tokens[0], cotangent[0]

    wqs = [pl.BlockSpec((RUN, n), lambda i, at, first=first: (0, first + at[0])) for n, first in ((256, 0), (128, 16), (128, 24))]
    small = [g[None] for g in (attn_gain, ffn_gain, q_gain, k_gain)]
    slice_qkv = pl.pallas_call(
        pack_kernel,
        out_shape=jax.ShapeDtypeStruct((RUN + 16, 512), BF),
        grid_spec=pltpu.PrefetchScalarGridSpec(
            num_scalar_prefetch=1,
            grid=(1,),
            in_specs=wqs + [pl.BlockSpec(g.shape, lambda i, at: (0, 0)) for g in small],
            out_specs=pl.BlockSpec((RUN + 16, 512), lambda i, at: (0, 0)),
        ),
    )(t[None].astype(jnp.int32), w_qkv, w_qkv, w_qkv, *small)
    xs = gather_tokens(x_own)
    here = t[None].astype(jnp.int32)
    later = ((8, RUN), jnp.int32)
    pair_qkv, later_t = call(
        pair_kernel, [((2, RUN + 16, 512), BF), later], [], 1, slice_qkv, shift(slice_qkv, "xlo", 1), info=here
    )
    parts_qkv = spread_z(pair_qkv)
    later_t = later_t[0, 0]
    eight = jnp.arange(8, dtype=jnp.int32)
    block = lax.rem(y - eight % 4 + 4, 4) * 2 + (core ^ (eight // 4))
    f_of = (xlo ^ (eight // 4)) * 4 + lax.rem(z - eight % 4 + 4, 4)
    blocks = jnp.concatenate([xhi * 8 + block, (1 - xhi) * 8 + block])
    pos = (positions[0] + later_t // 8).reshape(16, RUN)[blocks]
    rank = pos[:, 0] // RUN
    place = jnp.sum(rank[:8, None] > rank[None, :8], axis=1)
    in_order = jnp.argmax(place[None, :] == eight[:, None], axis=1)
    info = jnp.concatenate([in_order, f_of, block, core[None]]).astype(jnp.int32)
    bias = jnp.where(rank[:8, None] > rank[None, 8:], 0.0, MASKED)
    pos_rows = pos.astype(F32).reshape(16, 1, RUN)
    inverse = THETA ** (-(jnp.arange(HEAD // 2, dtype=F32) * 2.0 / HEAD))
    angles = pos[:8].reshape(1024).astype(F32)[:, None] * inverse[None, :]
    cosine, sine = jnp.cos(angles), jnp.sin(angles)
    cosine = jnp.concatenate([cosine, cosine], axis=1)
    sine = jnp.concatenate([-sine, sine], axis=1)

    (slice_ffn,) = call(
        pack_ffn_kernel, [((192, 768), BF)], [], 3, w_gate, w_up, w_down, info=here, deps=[pair_qkv]
    )
    received = shift(slice_ffn, "xlo", 1)
    half_out = lax.dynamic_slice_in_dim(w_out, core * HEAD, HEAD, 0)
    pair_out, _, out_token = call(
        pair_kernel,
        [((2, RUN, 1024), BF), later],
        [],
        1,
        half_out, shift(half_out, "xlo", 1),
        info=here,
        deps=[received] + parts_qkv[1:],
        token=True,
    )
    parts_out = spread_z(pair_out)

    h, wqkv, gain, kraw, kv, dy_later = call(
        key_value_kernel,
        [((1024, 1024), BF), ((1024, 512), BF), ((8, 2304), F32), ((1024, HEAD), F32), ((1024, 256), BF), ((RUN, 1024), BF)],
        [],
        5,
        *xs, *parts_qkv, cosine, sine, dy,
        info=info,
        deps=[out_token],
    )
    kv_other = shift(kv, "xhi", 1)
    qraw, q = call(query_kernel, [((1024, 256), F32), ((1024, 256), BF)], [], 3, h, wqkv, gain, cosine, sine)
    (partial,) = call(
        forward_own_kernel,
        [((8, HEAD + 8, 256), F32)],
        [((1024, HEAD), BF), ((256, 1024), BF)],
        5,
        pos_rows, q, kv,
        info=info,
    )
    dy_all = lax.all_gather(dy_later, TP, axis=0, tiled=True)
    o32, lse, o_low, o_token = call(
        forward_other_kernel,
        [((1024, 256), F32), ((8, 1, 256), F32), ((2, 4, RUN, 256), BF)],
        [((256, 1024), BF)],
        6,
        q, kv_other, partial,
        info=bias,
        deps=[parts_out[1], parts_out[3]],
        token=True,
    )
    parts_o = exchange(o_low[0], o_low[1])
    (wout_own,) = call(assemble_out_kernel, [((1024, 1024), BF)], [], 1, *parts_out, info=info, deps=[o_token])
    wout_sib = shift(wout_own, "core", 1)
    ffn_pairs = lambda follow: call(
        pair_kernel, [((2, 192, 768), BF), later], [], 1, slice_ffn, received, info=here, deps=[follow]
    )[0]
    pair_ffn = ffn_pairs(o_token)
    parts_ffn = [pair_ffn, shift(pair_ffn, "z", 1), None, shift(pair_ffn, "z", 3)]
    x2, h2_own, o_all, x_token = call(
        out_kernel,
        [((RUN, 1024), F32), ((RUN, 1024), BF), ((RUN, 2048), BF)],
        [],
        4,
        x_own, *parts_o, wout_own, wout_sib, gain,
        info=info,
        deps=[parts_ffn[1], parts_ffn[3]],
        token=True,
    )
    parts_ffn[2] = shift(ffn_pairs(x_token), "z", 2)
    wgu, wd, w_token = call(assemble_kernel, [((1024, 768), BF), ((384, 1024), BF)], [], 2, *parts_ffn, info=info, token=True)

    h2_parts = [h2_own] + [shift(h2_own, "y", k) for k in (1, 2, 3)]
    (h2_join,) = call(join_kernel, [((512, 1024), BF)], [], 1, *h2_parts, deps=[w_token])
    h2 = h2_join, shift(h2_join, "core", 1)
    ffn = [
        call(
            functools.partial(ffn_kernel, 4 * j),
            [((512, 384), BF), ((512, 768), BF), ((512, 1024), BF)],
            [],
            6,
            h2[j], dy_all, wgu, wd,
            info=info,
            fetch=True,
        )
        for j in (1, 0)
    ]
    (act_sib, dgu_sib, part_sib), (act_own, dgu_own, part_own) = ffn
    d_h2 = scatter_tokens(part_own, part_sib)
    g_ffn, y_own, y_sib, g_token = call(
        ffn_grad_kernel,
        [((8, 192, 768), BF), ((512, 1024), BF), ((512, 1024), BF)],
        [],
        8,
        *h2, dy_all, act_own, act_sib, dgu_own, dgu_sib, wd,
        info=info,
        fetch=True,
        token=True,
    )
    d_x2, d_branch, ffn_sum, do_own, do_other = call(
        middle_kernel,
        [((RUN, 1024), F32), ((RUN, 1024), BF), ((1, 1024), F32), ((4, RUN, 256), BF), ((4, RUN, 256), BF)],
        [((RUN, 2048), BF)],
        0,
        *d_h2, x2, dy, gain, wout_own, wout_sib,
        info=info,
        deps=[g_token],
    )
    d_o = exchange(do_own, do_other)
    g_out_own, g_out_other = call(
        out_grad_kernel, [((4, 2048, RUN), BF)] * 2, [((256, 1024), BF)], 0, o_all, d_branch, info=info
    )

    rows_ffn = lax.psum_scatter(g_ffn, FSDP, scatter_dimension=0, tiled=False)
    blocks_out, b_token = call(
        add_kernel,
        [((4 * 2048, RUN), BF)],
        [],
        0,
        g_out_own.reshape(-1, RUN), shift(g_out_other, "core", 1).reshape(-1, RUN),
        token=True,
    )
    blocks_out = blocks_out.reshape(4, 2048, RUN)
    out_parts = [blocks_out[0]] + [shift(blocks_out[k], "y", 4 - k) for k in (1, 2, 3)]

    d_q, d_other = call(
        backward_other_kernel,
        [((8, 256, HEAD), F32), ((1024, 256), BF)],
        [((1024, HEAD), F32), ((1024, HEAD), F32)],
        0,
        q, kv_other, o32, lse, *d_o,
        info=bias,
        deps=[b_token],
    )
    recv = shift(d_other, "xhi", 1)
    d_q, d_kv = call(
        backward_own_kernel,
        [((1024, 256), F32), ((1024, 256), F32)],
        [((1024, HEAD), BF), ((1024, HEAD), BF), ((1024, HEAD), F32), ((1024, HEAD), F32), ((8, RUN, 256), BF)],
        8,
        pos_rows, q, kv, o32, lse, *d_o, d_q,
        info=info,
    )
    dq_low, g_q, q_sum = call(
        query_back_kernel,
        [((1024, 256), BF), ((4, 2, RUN, 256), F32), ((1, HEAD), F32)],
        [],
        5,
        h, gain, cosine, sine, qraw, d_q,
        info=info,
    )
    *g_qkv, part_own, part_sib = call(
        key_value_back_kernel,
        [((2, 208, 512), BF)] * 4 + [((1024, 1024), BF)] * 2,
        [((1024, 256), BF)],
        8,
        h, wqkv, gain, cosine, sine, kraw, d_kv, recv, g_q, q_sum, ffn_sum, *out_parts, dq_low, y_own, y_sib,
        info=info,
        fetch=True,
        deps=[rows_ffn],
    )
    g_qkv = [g_qkv[0]] + [shift(g_qkv[k], "z", k) for k in (1, 2, 3)]
    d_h, d_token = call(
        add_kernel, [((1024, 1024), BF)], [], 1, part_own, shift(part_sib, "core", 1), token=True
    )
    mine, theirs = call(z_sum_kernel, [((496, 512), BF), ((208, 512), BF)], [], 1, *g_qkv, rows_ffn, deps=[d_token])
    d_h = d_h.reshape(4, 256, 1024)
    d_h = [d_h[0]] + [shift(d_h[k], "y", 4 - k) for k in (1, 2, 3)]
    cross = lax.ppermute(theirs, ("xlo", "xhi"), [(i, i ^ 3) for i in range(4)])
    total, half_ffn = call(
        sum_kernel,
        [((208, 512), BF), ((192, 768), BF)],
        [],
        1,
        mine, shift(theirs, "xlo", 1), shift(mine, "xhi", 1), cross,
        deps=d_h[1:],
    )
    sum_ffn = lax.all_gather(half_ffn, TP, axis=0)
    sum_gate, sum_up, sum_down = call(
        unpack_ffn_kernel, [((128, 3072), F32), ((128, 3072), F32), ((384, 1024), F32)], [], 4, sum_ffn
    )
    own = jnp.stack([total] + [shift(total, "y", k) for k in (1, 2, 3)])
    sum_qkv, sum_out, sum_gains = call(
        unpack_kernel,
        [((128, 4096), F32), ((256, 1024), F32), ((8, 512), F32)],
        [],
        3,
        own, shift(own, "core", 1),
        info=info,
    )
    output, input_grad = call(
        last_kernel, [((RUN, 1024), BF), ((RUN, 1024), F32)], [], 2, *d_h, x_own, x2, d_x2, gain
    )
    return (
        output[None],
        input_grad[None],
        sum_qkv,
        sum_out,
        sum_gate,
        sum_up,
        sum_down,
        sum_gains[0, :128],
        sum_gains[0, 128:256],
        sum_gains[0, 256:272],
        sum_gains[0, 384:400],
    )


def solution(mesh):
    split = Mesh(mesh.devices.reshape(tuple(SIZES.values())), FSDP + CTX)
    rows, both = P(FSDP, None), P(FSDP, CTX, None)
    return jax.shard_map(
        shards,
        mesh=split,
        in_specs=(both,) + (rows,) * 6 + (P(FSDP),) * 4 + (both,),
        out_specs=(both, both) + (rows,) * 5 + (P(FSDP),) * 4,
        check_vma=False,
    )
```

```python
import functools

import jax
import jax.numpy as jnp
from jax import lax
from jax.experimental import pallas as pl
from jax.experimental.pallas import tpu as pltpu
from jax.sharding import Mesh
from jax.sharding import PartitionSpec as P

HEAD = 128
EPS = 1e-06
MASKED = -1e30
THETA = 1000000.0
SCALE = HEAD**-0.5
LOG2E = 1.4426950408889634
RUN = 128
FSDP = ("xlo", "z")
CTX = ("xhi", "y", "core")
TP = ("y", "core")
SIZES = {"xlo": 2, "z": 4, "xhi": 2, "y": 4, "core": 2}
BF = jnp.bfloat16
F32 = jnp.float32
TOKEN = ((8, 128), jnp.float32)
SORTED, FOF, TOF, CORE = 0, 8, 16, 24


def shift(x, axis, step):
    n = SIZES[axis]
    return lax.ppermute(x, axis, [(i, (i + step) % n) for i in range(n)])


def gather_tokens(x):
    own = jnp.concatenate([x] + [shift(x, "y", k) for k in (1, 2, 3)], axis=0)
    return own, shift(own, "core", 1)


def scatter_tokens(own, other):
    blocks = (own.astype(F32) + shift(other, "core", 1).astype(F32)).astype(BF).reshape(4, own.shape[0] // 4, -1)
    return [blocks[0]] + [shift(blocks[k], "y", 4 - k) for k in (1, 2, 3)]


def exchange(own, other):
    both = jnp.stack([own, shift(other, "core", 1)], axis=1)
    return [both[0]] + [shift(both[k], "y", 4 - k) for k in (1, 2, 3)]


def spread_z(pair):
    return [pair] + [shift(pair, "z", k) for k in (1, 2, 3)]


def dot(a, b):
    return jnp.dot(a, b, preferred_element_type=F32)


def dot_nt(a, b):
    return lax.dot_general(a, b, (((1,), (1,)), ((), ())), preferred_element_type=F32)


def dot_tn(a, b):
    return lax.dot_general(a, b, (((0,), (0,)), ((), ())), preferred_element_type=F32)


def inv_rms(x):
    return lax.rsqrt(jnp.mean(x * x, axis=-1, keepdims=True) + EPS)


def norm_pull(x, gain, grad):
    inv = inv_rms(x)
    hat = x * inv
    scaled = grad * gain
    return inv * (scaled - hat * jnp.mean(scaled * hat, axis=-1, keepdims=True)), grad * hat


def ds(at, size):
    return pl.ds(pl.multiple_of(at, size), size)


def rows_of(i, size):
    return slice(i * size, (i + 1) * size)


def pack_kernel(at, q_ref, k_ref, v_ref, attn, ffn, qg, kg, out):
    out[:RUN, :256] = q_ref[...]
    out[:RUN, 256:384] = k_ref[...]
    out[:RUN, 384:] = v_ref[...]
    none = jnp.zeros((16, 112), BF)
    rows = [jnp.broadcast_to(g[...], (16, g.shape[1])) for g in (attn, ffn, qg, kg)]
    out[RUN:, :128] = rows[0]
    out[RUN:, 128:256] = rows[1]
    out[RUN:, 256:384] = jnp.concatenate([rows[2], none], axis=1)
    out[RUN:, 384:] = jnp.concatenate([rows[3], none], axis=1)


def key_value_kernel(info, own, sib, w0, w1, w2, w3, cos, sin, dy, h_ref, w_ref, gain_ref, raw_ref, kv_ref, dy_ref):
    dy_ref[...] = dy[...]
    gain_ref[...] = jnp.zeros_like(gain_ref)
    for k, part in enumerate((w0, w1, w2, w3)):
        for j in range(2):
            f = info[FOF + 4 * j + k]
            w_ref[ds(f * RUN, RUN), :] = part[j, :RUN, :]
            row = part[j, RUN:, :].astype(F32)[:8]
            gain_ref[:, ds(f * RUN, RUN)] = row[:, :128]
            gain_ref[:, ds(1024 + f * RUN, RUN)] = row[:, 128:256]
            gain_ref[:, 2048:2176] += pltpu.roll(row[:, 256:384], f * 16, 1)
            gain_ref[:, 2176:2304] += pltpu.roll(row[:, 384:512], f * 16, 1)
    attn_gain, k_gain = gain_ref[0:1, :1024], gain_ref[0:1, 2176:2304]
    for i in range(4):
        part = (own, sib)[i // 2]
        here = rows_of(i, 256)
        x = part[rows_of(i % 2, 256), :].astype(F32)
        h = (x * inv_rms(x) * attn_gain).astype(BF)
        h_ref[here, :] = h
        raw = dot(h, w_ref[:, 256:])
        raw_ref[here, :] = raw[:, :HEAD]
        key = raw[:, :HEAD]
        key = key * inv_rms(key) * k_gain
        key = key * cos[here, :] + pltpu.roll(key, HEAD // 2, 1) * sin[here, :]
        kv_ref[here, :HEAD] = key.astype(BF)
        kv_ref[here, HEAD:] = raw[:, HEAD:].astype(BF)


def query_kernel(h_ref, w_ref, gain_ref, cos, sin, raw_ref, q_ref):
    gain = gain_ref[0:1, 2048:2176]
    for i in range(4):
        here = rows_of(i, 256)
        raw = dot(h_ref[here, :], w_ref[:, :256])
        raw_ref[here, :] = raw
        for a in range(2):
            u = raw[:, rows_of(a, HEAD)]
            u = u * inv_rms(u) * gain
            u = u * cos[here, :] + pltpu.roll(u, HEAD // 2, 1) * sin[here, :]
            q_ref[here, rows_of(a, HEAD)] = u.astype(BF)


def stacked(rows):
    return jnp.concatenate([rows[:, :HEAD], rows[:, HEAD:]], axis=0)


def own_mask(pos_ref, b):
    row = pos_ref[b]
    keys = jnp.broadcast_to(row, (RUN, RUN)).T
    return jnp.concatenate([keys, keys], axis=1) <= jnp.concatenate([row, row], axis=1)


def expo(keys, q):
    return jnp.exp2(dot_nt(keys, q) * (SCALE * LOG2E))


def forward_own_kernel(info, pos_ref, q_ref, kv, part_ref, ks, vt):
    vt[HEAD:, :] = jnp.ones((HEAD, vt.shape[1]), BF)
    for s in range(8):
        src = ds(info[SORTED + s] * RUN, RUN)
        ks[rows_of(s, RUN), :] = kv[src, :HEAD]
        vt[:HEAD, rows_of(s, RUN)] = kv[src, HEAD:].T
    for s in range(8):
        b = info[SORTED + s]
        q = stacked(q_ref[ds(b * RUN, RUN), :])
        e = jnp.where(own_mask(pos_ref, b), expo(ks[rows_of(s, RUN), :], q), 0.0)
        acc = dot(vt[:, rows_of(s, RUN)], e.astype(BF))
        if s:
            acc += dot(vt[:, : s * RUN], expo(ks[: s * RUN, :], q).astype(BF))
        part_ref[b] = acc[: HEAD + 8]


def forward_other_kernel(bias, q_ref, kv, part_ref, o_ref, lse_ref, low_ref, vt):
    vt[HEAD:, :] = jnp.ones((HEAD, vt.shape[1]), BF)
    vt[:HEAD, :] = kv[:, HEAD:].T
    for i in range(8):
        q = stacked(q_ref[rows_of(i, RUN), :])
        scores = dot_nt(kv[:, :HEAD], q) * (SCALE * LOG2E)
        e = jnp.concatenate([jnp.exp2(scores[rows_of(b, RUN)] + bias[i, b]).astype(BF) for b in range(8)], axis=0)
        acc = dot(vt[...], e)
        total = acc[HEAD : HEAD + 1, :] + part_ref[i, HEAD : HEAD + 1, :]
        out = ((acc[:HEAD, :] + part_ref[i, :HEAD, :]) / total).T
        out = jnp.concatenate([out[:RUN], out[RUN:]], axis=1)
        o_ref[rows_of(i, RUN), :] = out
        low_ref[i // 4, i % 4] = out.astype(BF)
        lse_ref[i] = jnp.log2(total)


def out_kernel(info, x_ref, o0, o1, o2, o3, w_own, w_sib, gain_ref, x2_ref, h2_ref, oall_ref):
    core = info[CORE]
    for k, part in enumerate((o0, o1, o2, o3)):
        for j in range(2):
            at = info[TOF + 4 * j + (4 - k) % 4] * HEAD
            oall_ref[:, ds(at, HEAD)] = part[j, :, ds(core * HEAD, HEAD)]
            oall_ref[:, ds(1024 + at, HEAD)] = part[j, :, ds((1 - core) * HEAD, HEAD)]
    x2 = x_ref[...].astype(F32) + dot(oall_ref[:, :1024], w_own[...]) + dot(oall_ref[:, 1024:], w_sib[...])
    x2_ref[...] = x2
    h2_ref[...] = (x2 * inv_rms(x2) * gain_ref[0:1, 1024:2048]).astype(BF)


def pack_ffn_kernel(rank, gate, up, down, out):
    at = rank[0] * 48
    q = jnp.minimum(at // RUN, 1)
    for a, w in ((0, gate), (384, up)):
        pieces = []
        for f in range(8):
            window = w[:, pl.ds(pl.multiple_of(f * 384 + q * RUN, RUN), 256)].astype(F32)
            pieces.append(pltpu.roll(window, (256 - (at - q * RUN)) % 256, 1)[:, :48])
        out[:RUN, a : a + 384] = jnp.concatenate(pieces, axis=1).astype(BF)
    rows = down[pl.ds(pl.multiple_of(at, 16), 48), :]
    out[128:176, :] = rows[:, :768]
    for n in range(3):
        out[176:192, rows_of(n, 256)] = rows[16 * n : 16 * n + 16, 768:]


def join_kernel(a, b, c, d, out):
    for i, part in enumerate((a, b, c, d)):
        out[rows_of(i, RUN), :] = part[...]


def pair_kernel(rank, a, b, out, rank_out):
    out[0] = a[...]
    out[1] = b[...]
    rank_out[...] = jnp.full(rank_out.shape, rank[0], jnp.int32)


def assemble_out_kernel(info, p0, p1, p2, p3, w_ref):
    for k, part in enumerate((p0, p1, p2, p3)):
        for j in range(2):
            w_ref[ds(info[FOF + 4 * j + k] * HEAD, HEAD), :] = part[j]


def assemble_kernel(info, p0, p1, p2, p3, wgu, wd):
    for k, part in enumerate((p0, p1, p2, p3)):
        for j in range(2):
            f = info[FOF + 4 * j + k]
            wgu[ds(f * RUN, RUN), :] = part[j, :RUN, :]
            wd[pl.ds(pl.multiple_of(f * 48, 16), 48), :768] = part[j, 128:176, :]
            for n in range(3):
                wd[ds(f * 48 + 16 * n, 16), 768:] = part[j, 176:192, rows_of(n, 256)]


def blocks_of(info, dy_ref, first, count):
    return jnp.concatenate([dy_ref[ds(info[TOF + first + n] * RUN, RUN), :] for n in range(count)], axis=0)


def ffn_kernel(base, info, h2_ref, dy_ref, wgu, wd, act_ref, dgu_ref, part_ref):
    for i in range(2):
        here = rows_of(i, 256)
        gu = dot(h2_ref[here, :], wgu[...])
        gate, up = gu[:, :384], gu[:, 384:]
        sg = 1.0 / (1.0 + jnp.exp(-gate))
        silu = gate * sg
        act_ref[here, :] = (silu * up).astype(BF)
        d_act = dot_nt(blocks_of(info, dy_ref, base + 2 * i, 2), wd[...])
        d_gate = (d_act * up * (sg * (1.0 + gate * (1.0 - sg)))).astype(BF)
        d_gu = jnp.concatenate([d_gate, (d_act * silu).astype(BF)], axis=1)
        dgu_ref[here, :] = d_gu
        part_ref[here, :] = dot_nt(d_gu, wgu[...]).astype(BF)


def ffn_grad_kernel(info, h2_own, h2_sib, dy_ref, act_own, act_sib, dgu_own, dgu_sib, wd, g_ref, y_own, y_sib):
    y_own[...] = dot(act_own[...], wd[...]).astype(BF)
    y_sib[...] = dot(act_sib[...], wd[...]).astype(BF)
    for a in range(4):
        cols = rows_of(a, 256)
        g = (dot_tn(h2_own[:, cols], dgu_own[...]) + dot_tn(h2_sib[:, cols], dgu_sib[...])).astype(BF)
        g_ref[2 * a, :RUN, :] = g[:RUN]
        g_ref[2 * a + 1, :RUN, :] = g[RUN:]
    g = dot_tn(act_own[...], blocks_of(info, dy_ref, 0, 4)) + dot_tn(act_sib[...], blocks_of(info, dy_ref, 4, 4))
    g = g.astype(BF)
    for f in range(8):
        rows = g[f * 48 : (f + 1) * 48]
        g_ref[f, 128:176, :] = rows[:, :768]
        for n in range(3):
            g_ref[f, 176:192, rows_of(n, 256)] = rows[16 * n : 16 * n + 16, 768:]


def middle_kernel(
    info, p0, p1, p2, p3, x2_ref, dy_ref, gain_ref, w_own, w_sib, dx2_ref, low_ref, gsum_ref, do_own, do_other, do
):
    grad = sum(p[...].astype(F32) for p in (p0, p1, p2, p3))
    pulled, by_gain = norm_pull(x2_ref[...], gain_ref[0:1, 1024:2048], grad)
    gsum_ref[...] = jnp.sum(by_gain, axis=0, keepdims=True)
    dx2 = dy_ref[...].astype(F32) + pulled
    dx2_ref[...] = dx2
    low = dx2.astype(BF)
    low_ref[...] = low
    do[:, :1024] = dot_nt(low, w_own[...]).astype(BF)
    do[:, 1024:] = dot_nt(low, w_sib[...]).astype(BF)
    core = info[CORE]
    for j, out in enumerate((do_own, do_other)):
        for k in range(4):
            at = info[TOF + 4 * j + k] * HEAD
            out[k, :, ds(core * HEAD, HEAD)] = do[:, ds(at, HEAD)]
            out[k, :, ds((1 - core) * HEAD, HEAD)] = do[:, ds(1024 + at, HEAD)]


def out_grad_kernel(info, o_ref, d_ref, own_ref, other_ref, g_all):
    core = info[CORE]
    for a in range(8):
        g_all[...] = dot_tn(o_ref[:, rows_of(a, 256)], d_ref[...]).astype(BF)
        for n in range(2):
            f, half = (2 * a + n) % 8, core if a < 4 else 1 - core
            rows = ds((2 * f + half) * HEAD, HEAD)
            for k in range(4):
                own_ref[k, rows, :] = g_all[rows_of(n, HEAD), ds(info[TOF + k] * RUN, RUN)]
                other_ref[k, rows, :] = g_all[rows_of(n, HEAD), ds(info[TOF + 4 + k] * RUN, RUN)]


def backward_run(b, ref_b, q_ref, o_ref, lse_ref, do):
    rows = ds(b * RUN, RUN)
    q = stacked(q_ref[rows, :])
    do = stacked(do)
    delta = jnp.sum((do.astype(F32) * stacked(o_ref[rows, :])).T, axis=0, keepdims=True)
    return q, do, delta, lse_ref[ref_b]


def backward_other_kernel(bias, q_ref, kv, o_ref, lse_ref, d0, d1, d2, d3, dq_ref, dkv_ref, dk, dv):
    for i in range(8):
        q, do, delta, lse = backward_run(i, i, q_ref, o_ref, lse_ref, (d0, d3, d2, d1)[i % 4][i // 4])
        scores = dot_nt(kv[:, :HEAD], q) * (SCALE * LOG2E)
        p = jnp.concatenate([jnp.exp2(scores[rows_of(b, RUN)] - (lse - bias[i, b])) for b in range(8)], axis=0)
        d_s = (p * (dot_nt(kv[:, HEAD:], do) - delta)).astype(BF)
        by_v, by_k = dot(p.astype(BF), do), dot(d_s, q)
        dv[...] = by_v if i == 0 else dv[...] + by_v
        dk[...] = by_k if i == 0 else dk[...] + by_k
        dq_ref[i] = dot_tn(d_s, kv[:, :HEAD])
    dkv_ref[:, :HEAD] = (dk[...] * SCALE).astype(BF)
    dkv_ref[:, HEAD:] = dv[...].astype(BF)


def backward_own_kernel(
    info, pos_ref, q_ref, kv, o_ref, lse_ref, d0, d1, d2, d3, before, dq_ref, dkv_ref, ks, vs, dk, dv, dos
):
    for s in range(8):
        src = ds(info[SORTED + s] * RUN, RUN)
        ks[rows_of(s, RUN), :] = kv[src, :HEAD]
        vs[rows_of(s, RUN), :] = kv[src, HEAD:]
        dos[s] = (d0, d3, d2, d1)[s % 4][s // 4]
    dk[...] = jnp.zeros_like(dk)
    dv[...] = jnp.zeros_like(dv)
    for s in range(8):
        b = info[SORTED + s]
        q, do, delta, lse = backward_run(b, b, q_ref, o_ref, lse_ref, dos[b])
        keys = ks[: (s + 1) * RUN, :]
        p = jnp.exp2(dot_nt(keys, q) * (SCALE * LOG2E) - lse)
        diagonal = jnp.where(own_mask(pos_ref, b), p[s * RUN :], 0.0)
        p = jnp.concatenate([p[: s * RUN], diagonal], axis=0) if s else diagonal
        d_s = (p * (dot_nt(vs[: (s + 1) * RUN, :], do) - delta)).astype(BF)
        dv[: (s + 1) * RUN, :] += dot(p.astype(BF), do)
        dk[: (s + 1) * RUN, :] += dot(d_s, q)
        dq = (dot_tn(d_s, keys) + before[b]) * SCALE
        dq_ref[ds(b * RUN, RUN), :HEAD] = dq[:RUN]
        dq_ref[ds(b * RUN, RUN), HEAD:] = dq[RUN:]
    for s in range(8):
        src = ds(info[SORTED + s] * RUN, RUN)
        dkv_ref[src, :HEAD] = dk[rows_of(s, RUN), :] * SCALE
        dkv_ref[src, HEAD:] = dv[rows_of(s, RUN), :]


def head_back(raw, gain, grad, cos, sin):
    grad = grad * cos + pltpu.roll(grad * sin, HEAD // 2, 1)
    pulled, by_gain = norm_pull(raw, gain, grad)
    return pulled.astype(BF), jnp.sum(by_gain, axis=0, keepdims=True)


def query_back_kernel(info, h_ref, gain_ref, cos, sin, raw, dq_ref, low_ref, g_ref, sum_ref):
    sum_ref[...] = jnp.zeros_like(sum_ref)
    for i in range(4):
        here = rows_of(i, 256)
        for a in range(2):
            cols = rows_of(a, HEAD)
            low, by_gain = head_back(raw[here, cols], gain_ref[0:1, 2048:2176], dq_ref[here, cols], cos[here, :], sin[here, :])
            low_ref[here, cols] = low
            sum_ref[...] += by_gain
    for k in range(4):
        for j in range(2):
            f = info[FOF + 4 * j + (4 - k) % 4]
            g_ref[k, j] = dot_tn(h_ref[:, ds(f * RUN, RUN)], low_ref[...])


def key_value_back_kernel(
    info, h_ref, w_ref, gain_ref, cos, sin, raw, dkv_ref, recv, gq_ref, qsum, ffn_ref,
    out0, out1, out2, out3, dq_ref, y_own, y_sib, g0, g1, g2, g3, own_ref, sib_ref, low_ref,
):
    sums = jnp.zeros((1, HEAD), F32)
    for i in range(4):
        here = rows_of(i, 256)
        dkv = dkv_ref[here, :] + recv[here, :].astype(F32)
        low, by_gain = head_back(raw[here, :], gain_ref[0:1, 2176:2304], dkv[:, :HEAD], cos[here, :], sin[here, :])
        low_ref[here, :HEAD] = low
        low_ref[here, HEAD:] = dkv[:, HEAD:].astype(BF)
        sums += by_gain
    lane = lax.broadcasted_iota(jnp.int32, (8, HEAD), 1)
    heads = [jnp.broadcast_to(s, (8, HEAD)) for s in (qsum[...], sums)]
    for k, g_ref in enumerate((g0, g1, g2, g3)):
        for j in range(2):
            f = info[FOF + 4 * j + (4 - k) % 4]
            here = ds(f * RUN, RUN)
            gkv = dot_tn(h_ref[:, here], low_ref[...])
            gq = gq_ref[k, j]
            g_ref[j, :RUN, :256] = gq.astype(BF)
            g_ref[j, :RUN, 256:] = gkv.astype(BF)
            by_attn = jnp.sum(gq * w_ref[here, :256].astype(F32) + gkv * w_ref[here, 256:].astype(F32), axis=1, keepdims=True)
            by_attn = jnp.broadcast_to(by_attn, (RUN, RUN)).T[:8] / gain_ref[:, here]
            rows = [by_attn, jnp.broadcast_to(ffn_ref[0:1, here], (8, RUN))]
            rows += [jnp.where(lane < 16, pltpu.roll(r, HEAD - 16 * f, 1), 0.0) for r in heads]
            rows = jnp.concatenate(rows, axis=1)
            g_ref[j, RUN : RUN + 16, :] = jnp.concatenate([rows, rows], axis=0).astype(BF)
            for n in range(4):
                src = ds(f * 256 + n * 64, 64)
                rows = sum(o[src, :].astype(F32) for o in (out0, out1, out2, out3))
                g_ref[j, RUN + 16 :, rows_of(n, RUN)] = rows.astype(BF)
    for i in range(4):
        here = rows_of(i, 256)
        part = dot_nt(dq_ref[here, :], w_ref[:, :256]) + dot_nt(low_ref[here, :], w_ref[:, 256:])
        part = part.astype(BF)
        out, y_ref = ((own_ref, y_own), (sib_ref, y_sib))[i // 2]
        for n in range(2):
            k = 2 * (i % 2) + n
            out[rows_of(2 * k, RUN), :] = part[rows_of(n, RUN)]
            out[rows_of(2 * k + 1, RUN), :] = y_ref[rows_of(k, RUN), :]


def last_kernel(p0, p1, p2, p3, x_ref, x2_ref, dx2_ref, gain_ref, out_ref, grad_ref):
    sums = sum(p[...].astype(F32) for p in (p0, p1, p2, p3))
    out_ref[...] = (x2_ref[...] + sums[RUN:]).astype(BF)
    grad_ref[...] = dx2_ref[...] + norm_pull(x_ref[...].astype(F32), gain_ref[0:1, :1024], sums[:RUN])[0]


def unpack_kernel(info, own, sib, g_ref, out_ref, gain_ref):
    gain_ref[...] = jnp.zeros_like(gain_ref)
    for j, part in enumerate((own, sib)):
        for k in range(4):
            t = info[TOF + 4 * j + k]
            g_ref[:, ds(t * 256, 256)] = part[k, :RUN, :256].astype(F32)
            g_ref[:, ds(2048 + t * RUN, RUN)] = part[k, :RUN, 256:384].astype(F32)
            g_ref[:, ds(3072 + t * RUN, RUN)] = part[k, :RUN, 384:].astype(F32)
            gain_ref[...] += part[k, RUN : RUN + 16, :].astype(F32)[:8]
            for n in range(4):
                out_ref[rows_of(n, 64), ds(t * RUN, RUN)] = part[k, RUN + 16 :, rows_of(n, RUN)].astype(F32)


def z_sum_kernel(g0, g1, g2, g3, rows, mine, theirs):
    for j, out in enumerate((mine, theirs)):
        out[:208, :] = sum(p[j].astype(F32) for p in (g0, g1, g2, g3)).astype(BF)
    mine[208:400, :] = rows[:, :512]
    mine[400:, :256] = rows[:96, 512:]
    mine[400:, 256:] = rows[96:, 512:]


def add_kernel(a, b, out):
    for i in range(8):
        here = rows_of(i, a.shape[0] // 8)
        out[here, :] = (a[here, :].astype(F32) + b[here, :].astype(F32)).astype(BF)


def sum_kernel(mine, xlo, xhi, cross, out, rows):
    both = mine[...].astype(F32) + xhi[...].astype(F32)
    out[...] = (both[:208] + xlo[...].astype(F32) + cross[...].astype(F32)).astype(BF)
    both = both.astype(BF)
    rows[:, :512] = both[208:400]
    rows[:96, 512:] = both[400:, :256]
    rows[96:, 512:] = both[400:, 256:]


def unpack_ffn_kernel(wide, gate, up, down):
    for a, out in ((0, gate), (384, up)):
        for f in range(8):
            pieces = [wide[t, :RUN, a + f * 48 : a + f * 48 + 48].astype(F32) for t in range(8)]
            out[:, f * 384 : (f + 1) * 384] = jnp.concatenate(pieces, axis=1)
    for t in range(8):
        down[t * 48 : (t + 1) * 48, :768] = wide[t, 128:176, :].astype(F32)
        for n in range(3):
            at = t * 48 + 16 * n
            down[at : at + 16, 768:] = wide[t, 176:192, rows_of(n, 256)].astype(F32)


def call(kernel, outs, scratch, micros, *args, info=None, deps=(), token=False):
    smem = [] if info is None else [info]
    first, late = len(smem) + len(args), len(smem) + len(args) + len(deps)
    outs = outs + [TOKEN] * token
    end = late + len(outs) - token

    def body(*refs):
        kernel(*refs[:first], *refs[late:end], *refs[end + token :])
        if token:
            refs[end][...] = jnp.zeros(TOKEN[0], F32)

    vmem = pl.BlockSpec(memory_space=pltpu.VMEM)
    return pl.pallas_call(
        body,
        name=getattr(kernel, "func", kernel).__name__,
        out_shape=[jax.ShapeDtypeStruct(*o) for o in outs],
        in_specs=[pl.BlockSpec(memory_space=pltpu.SMEM)] * len(smem)
        + [vmem] * (len(args) + len(deps)),
        out_specs=[vmem] * len(outs),
        scratch_shapes=[pltpu.VMEM(*s) for s in scratch],
        compiler_params=pltpu.CompilerParams(vmem_limit_bytes=16 * 2**20),
        cost_estimate=pl.CostEstimate(flops=int(micros * 3e8), bytes_accessed=2**12, transcendentals=0),
    )(*smem, *args, *deps)


def shards(
    tokens, positions, w_qkv, w_out, w_gate, w_up, w_down, attn_gain, ffn_gain, q_gain, k_gain, cotangent
):
    xhi, y, core = (lax.axis_index(a) for a in CTX)
    xlo, z = (lax.axis_index(a) for a in FSDP)
    t = y * 2 + core
    x_own, dy = tokens[0], cotangent[0]

    wqs = [pl.BlockSpec((RUN, n), lambda i, at, first=first: (0, first + at[0])) for n, first in ((256, 0), (128, 16), (128, 24))]
    small = [g[None] for g in (attn_gain, ffn_gain, q_gain, k_gain)]
    slice_qkv = pl.pallas_call(
        pack_kernel,
        out_shape=jax.ShapeDtypeStruct((RUN + 16, 512), BF),
        grid_spec=pltpu.PrefetchScalarGridSpec(
            num_scalar_prefetch=1,
            grid=(1,),
            in_specs=wqs + [pl.BlockSpec(g.shape, lambda i, at: (0, 0)) for g in small],
            out_specs=pl.BlockSpec((RUN + 16, 512), lambda i, at: (0, 0)),
        ),
    )(t[None].astype(jnp.int32), w_qkv, w_qkv, w_qkv, *small)
    xs = gather_tokens(x_own)
    here = t[None].astype(jnp.int32)
    later = ((8, RUN), jnp.int32)
    pair_qkv, later_t = call(
        pair_kernel, [((2, RUN + 16, 512), BF), later], [], 1, slice_qkv, shift(slice_qkv, "xlo", 1), info=here
    )
    parts_qkv = spread_z(pair_qkv)
    later_t = later_t[0, 0]
    eight = jnp.arange(8, dtype=jnp.int32)
    block = lax.rem(y - eight % 4 + 4, 4) * 2 + (core ^ (eight // 4))
    f_of = (xlo ^ (eight // 4)) * 4 + lax.rem(z - eight % 4 + 4, 4)
    blocks = jnp.concatenate([xhi * 8 + block, (1 - xhi) * 8 + block])
    pos = (positions[0] + later_t // 8).reshape(16, RUN)[blocks]
    rank = pos[:, 0] // RUN
    place = jnp.sum(rank[:8, None] > rank[None, :8], axis=1)
    in_order = jnp.argmax(place[None, :] == eight[:, None], axis=1)
    info = jnp.concatenate([in_order, f_of, block, core[None]]).astype(jnp.int32)
    bias = jnp.where(rank[:8, None] > rank[None, 8:], 0.0, MASKED)
    pos_rows = pos.astype(F32).reshape(16, 1, RUN)
    inverse = THETA ** (-(jnp.arange(HEAD // 2, dtype=F32) * 2.0 / HEAD))
    angles = pos[:8].reshape(1024).astype(F32)[:, None] * inverse[None, :]
    cosine, sine = jnp.cos(angles), jnp.sin(angles)
    cosine = jnp.concatenate([cosine, cosine], axis=1)
    sine = jnp.concatenate([-sine, sine], axis=1)

    (slice_ffn,) = call(
        pack_ffn_kernel, [((192, 768), BF)], [], 3, w_gate, w_up, w_down, info=here, deps=[pair_qkv]
    )
    received = shift(slice_ffn, "xlo", 1)
    half_out = lax.dynamic_slice_in_dim(w_out, core * HEAD, HEAD, 0)
    pair_out, _, out_token = call(
        pair_kernel,
        [((2, RUN, 1024), BF), later],
        [],
        1,
        half_out, shift(half_out, "xlo", 1),
        info=here,
        deps=parts_qkv[1:],
        token=True,
    )
    parts_out = spread_z(pair_out)

    h, wqkv, gain, kraw, kv, dy_later = call(
        key_value_kernel,
        [((1024, 1024), BF), ((1024, 512), BF), ((8, 2304), F32), ((1024, HEAD), F32), ((1024, 256), BF), ((RUN, 1024), BF)],
        [],
        5,
        *xs, *parts_qkv, cosine, sine, dy,
        info=info,
        deps=[out_token],
    )
    kv_other = shift(kv, "xhi", 1)
    qraw, q = call(query_kernel, [((1024, 256), F32), ((1024, 256), BF)], [], 3, h, wqkv, gain, cosine, sine)
    (partial,) = call(
        forward_own_kernel,
        [((8, HEAD + 8, 256), F32)],
        [((1024, HEAD), BF), ((256, 1024), BF)],
        5,
        pos_rows, q, kv,
        info=info,
    )
    dy_all = lax.all_gather(dy_later, TP, axis=0, tiled=True)
    o32, lse, o_low, o_token = call(
        forward_other_kernel,
        [((1024, 256), F32), ((8, 1, 256), F32), ((2, 4, RUN, 256), BF)],
        [((256, 1024), BF)],
        6,
        q, kv_other, partial,
        info=bias,
        deps=[parts_out[1], parts_out[3], received],
        token=True,
    )
    parts_o = exchange(o_low[0], o_low[1])
    (wout_own,) = call(assemble_out_kernel, [((1024, 1024), BF)], [], 1, *parts_out, info=info, deps=[o_token])
    wout_sib = shift(wout_own, "core", 1)
    ffn_pairs = lambda follow: call(
        pair_kernel, [((2, 192, 768), BF), later], [], 1, slice_ffn, received, info=here, deps=[follow]
    )[0]
    pair_ffn = ffn_pairs(o_token)
    parts_ffn = [pair_ffn, shift(pair_ffn, "z", 1), None, shift(pair_ffn, "z", 3)]
    x2, h2_own, o_all, x_token = call(
        out_kernel,
        [((RUN, 1024), F32), ((RUN, 1024), BF), ((RUN, 2048), BF)],
        [],
        4,
        x_own, *parts_o, wout_own, wout_sib, gain,
        info=info,
        deps=[parts_ffn[1], parts_ffn[3]],
        token=True,
    )
    parts_ffn[2] = shift(ffn_pairs(x_token), "z", 2)
    wgu, wd, w_token = call(assemble_kernel, [((1024, 768), BF), ((384, 1024), BF)], [], 2, *parts_ffn, info=info, token=True)

    h2_parts = [h2_own] + [shift(h2_own, "y", k) for k in (1, 2, 3)]
    (h2_join,) = call(join_kernel, [((512, 1024), BF)], [], 1, *h2_parts, deps=[w_token])
    h2 = h2_join, shift(h2_join, "core", 1)
    ffn = [
        call(
            functools.partial(ffn_kernel, 4 * j),
            [((512, 384), BF), ((512, 768), BF), ((512, 1024), BF)],
            [],
            6,
            h2[j], dy_all, wgu, wd,
            info=info,
        )
        for j in (1, 0)
    ]
    (act_sib, dgu_sib, part_sib), (act_own, dgu_own, part_own) = ffn
    d_h2 = scatter_tokens(part_own, part_sib)
    g_ffn, y_own, y_sib, g_token = call(
        ffn_grad_kernel,
        [((8, 192, 768), BF), ((512, 1024), BF), ((512, 1024), BF)],
        [],
        8,
        *h2, dy_all, act_own, act_sib, dgu_own, dgu_sib, wd,
        info=info,
        token=True,
    )
    d_x2, d_branch, ffn_sum, do_own, do_other = call(
        middle_kernel,
        [((RUN, 1024), F32), ((RUN, 1024), BF), ((1, 1024), F32), ((4, RUN, 256), BF), ((4, RUN, 256), BF)],
        [((RUN, 2048), BF)],
        0,
        *d_h2, x2, dy, gain, wout_own, wout_sib,
        info=info,
        deps=[g_token],
    )
    d_o = exchange(do_own, do_other)
    g_out_own, g_out_other = call(
        out_grad_kernel, [((4, 2048, RUN), BF)] * 2, [((256, 1024), BF)], 0, o_all, d_branch, info=info
    )

    rows_ffn = lax.psum_scatter(g_ffn, FSDP, scatter_dimension=0, tiled=False)
    blocks_out, b_token = call(
        add_kernel,
        [((4 * 2048, RUN), BF)],
        [],
        0,
        g_out_own.reshape(-1, RUN), shift(g_out_other, "core", 1).reshape(-1, RUN),
        token=True,
    )
    blocks_out = blocks_out.reshape(4, 2048, RUN)
    out_parts = [blocks_out[0]] + [shift(blocks_out[k], "y", 4 - k) for k in (1, 2, 3)]

    d_q, d_other = call(
        backward_other_kernel,
        [((8, 256, HEAD), F32), ((1024, 256), BF)],
        [((1024, HEAD), F32), ((1024, HEAD), F32)],
        0,
        q, kv_other, o32, lse, *d_o,
        info=bias,
        deps=[b_token],
    )
    recv = shift(d_other, "xhi", 1)
    d_q, d_kv = call(
        backward_own_kernel,
        [((1024, 256), F32), ((1024, 256), F32)],
        [((1024, HEAD), BF), ((1024, HEAD), BF), ((1024, HEAD), F32), ((1024, HEAD), F32), ((8, RUN, 256), BF)],
        8,
        pos_rows, q, kv, o32, lse, *d_o, d_q,
        info=info,
    )
    dq_low, g_q, q_sum = call(
        query_back_kernel,
        [((1024, 256), BF), ((4, 2, RUN, 256), F32), ((1, HEAD), F32)],
        [],
        5,
        h, gain, cosine, sine, qraw, d_q,
        info=info,
    )
    *g_qkv, part_own, part_sib = call(
        key_value_back_kernel,
        [((2, 208, 512), BF)] * 4 + [((1024, 1024), BF)] * 2,
        [((1024, 256), BF)],
        8,
        h, wqkv, gain, cosine, sine, kraw, d_kv, recv, g_q, q_sum, ffn_sum, *out_parts, dq_low, y_own, y_sib,
        info=info,
        deps=[rows_ffn],
    )
    g_qkv = [g_qkv[0]] + [shift(g_qkv[k], "z", k) for k in (1, 2, 3)]
    d_h, d_token = call(
        add_kernel, [((1024, 1024), BF)], [], 1, part_own, shift(part_sib, "core", 1), token=True
    )
    mine, theirs = call(z_sum_kernel, [((496, 512), BF), ((208, 512), BF)], [], 1, *g_qkv, rows_ffn, deps=[d_token])
    d_h = d_h.reshape(4, 256, 1024)
    d_h = [d_h[0]] + [shift(d_h[k], "y", 4 - k) for k in (1, 2, 3)]
    cross = lax.ppermute(theirs, ("xlo", "xhi"), [(i, i ^ 3) for i in range(4)])
    total, half_ffn = call(
        sum_kernel,
        [((208, 512), BF), ((192, 768), BF)],
        [],
        1,
        mine, shift(theirs, "xlo", 1), shift(mine, "xhi", 1), cross,
        deps=d_h[1:],
    )
    sum_ffn = lax.all_gather(half_ffn, TP, axis=0)
    sum_gate, sum_up, sum_down = call(
        unpack_ffn_kernel, [((128, 3072), F32), ((128, 3072), F32), ((384, 1024), F32)], [], 4, sum_ffn
    )
    own = jnp.stack([total] + [shift(total, "y", k) for k in (1, 2, 3)])
    sum_qkv, sum_out, sum_gains = call(
        unpack_kernel,
        [((128, 4096), F32), ((256, 1024), F32), ((8, 512), F32)],
        [],
        3,
        own, shift(own, "core", 1),
        info=info,
    )
    output, input_grad = call(
        last_kernel, [((RUN, 1024), BF), ((RUN, 1024), F32)], [], 2, *d_h, x_own, x2, d_x2, gain
    )
    return (
        output[None],
        input_grad[None],
        sum_qkv,
        sum_out,
        sum_gate,
        sum_up,
        sum_down,
        sum_gains[0, :128],
        sum_gains[0, 128:256],
        sum_gains[0, 256:272],
        sum_gains[0, 384:400],
    )


def solution(mesh):
    split = Mesh(mesh.devices.reshape(tuple(SIZES.values())), FSDP + CTX)
    rows, both = P(FSDP, None), P(FSDP, CTX, None)
    return jax.shard_map(
        shards,
        mesh=split,
        in_specs=(both,) + (rows,) * 6 + (P(FSDP),) * 4 + (both,),
        out_specs=(both, both) + (rows,) * 5 + (P(FSDP),) * 4,
        check_vma=False,
    )
```
